128 devices in a mesh: wide: 64 (over x, y_lo, z, core), narrow: 2 (over y_hi).
Axes of the slice: x: 4, y: 4 (y_hi: 2, y_lo: 2; y = y_hi * 2 + y_lo), z: 4, core: 2. Of those that a mesh axis runs over, the one named last changes fastest.
Arguments:
- tokens: bfloat16 [32768, 1024], P(('wide', 'narrow')), may hold values from -6 to 6
- seg_ids: int32 [32768], P(('wide', 'narrow')), may hold values from 0 to 681, never falling along the last dimension, each value on 1 to 256 neighbouring positions
- buckets: int32 [256], replicated, may hold values from 0 to 31, as said below
- cotangent: bfloat16 [32768, 1024], P(('wide', 'narrow')), may hold values from -6 to 6
- ln1_gain: bfloat16 [2, 1024], P(None, 'wide'), may hold values from 0.5 to 1.5
- ln1_bias: bfloat16 [2, 1024], P(None, 'wide'), may hold values from -2 to 2
- w_query: bfloat16 [2, 1024, 1024], P(None, 'wide'), may hold values from -0.1875 to 0.1875
- w_key: bfloat16 [2, 1024, 1024], P(None, 'wide'), may hold values from -0.1875 to 0.1875
- w_value: bfloat16 [2, 1024, 1024], P(None, 'wide'), may hold values from -0.1875 to 0.1875
- w_out: bfloat16 [2, 1024, 1024], P(None, 'wide'), may hold values from -0.75 to 0.75
- rel_table: bfloat16 [2, 512], P(None, 'wide'), may hold values from -4 to 4
- ln2_gain: bfloat16 [2, 1024], P(None, 'wide'), may hold values from 0.5 to 1.5
- ln2_bias: bfloat16 [2, 1024], P(None, 'wide'), may hold values from -2 to 2
- w_up: bfloat16 [2, 1024, 4096], P(None, 'wide'), may hold values from -0.1875 to 0.1875
- w_down: bfloat16 [2, 4096, 1024], P(None, 'wide'), may hold values from -0.09375 to 0.09375
Outputs:
- acts: bfloat16 [2, 32768, 1024], P(None, ('wide', 'narrow'))
- grad_input: float32 [32768, 1024], P(('wide', 'narrow'))
- grad_ln1_gain: float32 [2, 1024], P(None, 'wide')
- grad_ln1_bias: float32 [2, 1024], P(None, 'wide')
- grad_query: float32 [2, 1024, 1024], P(None, 'wide')
- grad_key: float32 [2, 1024, 1024], P(None, 'wide')
- grad_value: float32 [2, 1024, 1024], P(None, 'wide')
- grad_out: float32 [2, 1024, 1024], P(None, 'wide')
- grad_table: float32 [2, 512], P(None, 'wide')
- grad_ln2_gain: float32 [2, 1024], P(None, 'wide')
- grad_ln2_bias: float32 [2, 1024], P(None, 'wide')
- grad_up: float32 [2, 1024, 4096], P(None, 'wide')
- grad_down: float32 [2, 4096, 1024], P(None, 'wide')
The draws below stay inside these ranges and needn't reach their ends.
Inputs may be any that keep to these rules, and one draw needn't show every extreme that they name: `seg_ids`: never falling along the tokens. `buckets`: equal to the distance below 16, never falling, reaching 31 at the largest distance.
All inputs are finite; a program needn't handle non-finite values.
Results may differ from the reference program's by a relative error of at most 0.02.
Values may be sent and summed in bfloat16 or wider, within the bound.
A program may use at most 256 MiB of HBM per device.

```python
import math
import jax
import jax.numpy as jnp
import numpy as np
from jax import lax

D = 1024
HEADS = 16
HEAD = 64
FF = 4096
BUCKETS = 32
TOK_DEV = 256
TOKENS = 32768
N_WIDE = 64
N_NARROW = 2


def draw_buckets(key, part):
    key = jax.random.fold_in(key, 7)
    exact = BUCKETS // 2
    shuffled = jax.random.permutation(key, TOK_DEV - exact - 1)
    breakpoints = exact + 1 + shuffled[:BUCKETS - exact - 1]
    positions = jnp.arange(TOK_DEV, dtype=jnp.int32)
    stepped = exact + jnp.sum((breakpoints[None, :] <= positions[:, None]).astype(jnp.int32), axis=1)
    return jnp.where(positions < exact, positions, stepped).astype(jnp.int32)


def level_of(own_key, shape, shards, low, top_value):
    factor_of, own = 1.0, jax.random.fold_in(own_key, 6)
    for dim, shards_of in shards:
        heights = jnp.exp(jax.random.uniform(jax.random.fold_in(own, dim), (shards_of,), jnp.float32, low / len(shards), top_value / len(shards)))
        factor_of = factor_of * jnp.repeat(heights, shape[dim] // shards_of).reshape([-1 if axis == dim else 1 for axis in range(len(shape))])
    return factor_of


def profile(number_of, total, most, skew):
    portions = [(1 << 20) // math.isqrt(grade ** skew) + 1 for grade in range(2, number_of + 1)]
    rest, counts = total - most - (number_of - 1), [1] * (number_of - 1)
    while rest > 0:
        candidates = [i for i in range(number_of - 1) if counts[i] < most]
        whole, remaining = sum([portions[i] for i in candidates]), rest
        for i in candidates:
            addition = min(most - counts[i], max(1, remaining * portions[i] // whole), rest)
            counts[i] = counts[i] + addition
            rest = rest - addition
    return np.array([most] + counts)


def uneven(stream_key, number_of, total, most, skew):
    if number_of == 2:
        one = jax.random.randint(stream_key, (), max(1, total - most), min(most, total - 1) + 1)
        return jnp.stack([one, total - one])
    lengths = jnp.asarray(profile(number_of, total, most, skew), jnp.int32)
    twos = (number_of - 1) // 2
    giver, taker = lengths[1:1 + 2 * twos:2], lengths[2:2 + 2 * twos:2]
    slack = jnp.minimum(giver - 1, most - taker)
    moved = jax.random.randint(jax.random.fold_in(stream_key, 1), (twos,), 0, 1 << 20) % (slack + 1)
    lengths = lengths.at[1:1 + 2 * twos:2].set(giver - moved).at[2:2 + 2 * twos:2].set(taker + moved)
    return lengths[jax.random.permutation(jax.random.fold_in(stream_key, 2), number_of)]


def gaussian(rng, extent, deviation, most, pieces=(), held_as=jnp.bfloat16):
    values = jax.random.normal(rng, extent, jnp.float32) * deviation
    if len(pieces) > 0:
        values = level_of(rng, extent, pieces, -0.22, 0.18) * values
    return jnp.clip(values, min=-most, max=most).astype(held_as)


def setup_inputs(seed: int = 0) -> dict:
    key_list = jax.random.split(jax.random.key(seed), 16)
    tokens = gaussian(key_list[0], (TOKENS, D), 1.0, 6.0, ((0, 128),))
    seg_ids = jnp.searchsorted(jnp.cumsum(uneven(key_list[1], TOKENS // 48, TOKENS, TOK_DEV, 1)), jnp.arange(TOKENS), side="right").astype(jnp.int32)
    buckets = draw_buckets(jax.random.fold_in(key_list[15], 71), 0)
    cotangent = gaussian(key_list[3], (TOKENS, D), 1.0, 6.0, ((0, 128),))
    ln1_gain = jnp.clip(1.0 + 0.1 * jax.random.normal(key_list[4], (2, D), jnp.float32), 0.5, 1.5).astype(jnp.bfloat16)
    ln1_bias = gaussian(key_list[5], (2, D), 0.3, 2.0, ((1, 64),))
    w_query = gaussian(key_list[6], (2, D, D), D ** -0.5, 0.1875, ((1, 64),))
    w_key = gaussian(key_list[7], (2, D, D), D ** -0.5, 0.1875, ((1, 64),))
    w_value = gaussian(key_list[8], (2, D, D), D ** -0.5, 0.1875, ((1, 64),))
    w_out = gaussian(key_list[9], (2, D, D), (D // 16) ** -0.5, 0.75, ((1, 64),))
    rel_table = gaussian(key_list[10], (2, BUCKETS * HEADS), 1.0, 4.0, ((1, 64),))
    ln2_gain = jnp.clip(1.0 + 0.1 * jax.random.normal(key_list[11], (2, D), jnp.float32), 0.5, 1.5).astype(jnp.bfloat16)
    ln2_bias = gaussian(key_list[12], (2, D), 0.3, 2.0, ((1, 64),))
    w_up = gaussian(key_list[13], (2, D, FF), D ** -0.5, 0.1875, ((1, 64),))
    w_down = gaussian(key_list[14], (2, FF, D), FF ** -0.5, 0.09375, ((1, 64),))
    return {"tokens": tokens, "seg_ids": seg_ids, "buckets": buckets, "cotangent": cotangent, "ln1_gain": ln1_gain, "ln1_bias": ln1_bias, "w_query": w_query, "w_key": w_key, "w_value": w_value, "w_out": w_out, "rel_table": rel_table, "ln2_gain": ln2_gain, "ln2_bias": ln2_bias, "w_up": w_up, "w_down": w_down}


highest = lax.Precision.HIGHEST
epsilon = 1e-05
gelu_coef = 0.7978845608028654

@jax.custom_vjp
def low(v):
    return lax.optimization_barrier(v.astype(jnp.bfloat16)).astype(jnp.float32)

@jax.custom_vjp
def low_back(v):
    return v

def low_keep(v):
    return (low(v), None)

def low_pass(kept, grad):
    return (grad,)

def back_keep(v):
    return (v, None)

def back_low(kept, grad):
    return (low(grad),)
low.defvjp(low_keep, low_pass)
low_back.defvjp(back_keep, back_low)

def rounded(value):
    return low(low_back(value))

def layer_norm(inputs, gain, shift):
    center = lax.optimization_barrier(jnp.mean(inputs, -1, keepdims=True))
    centered = inputs - center
    spread = lax.optimization_barrier(jnp.mean(centered * centered, -1, keepdims=True))
    return centered * lax.rsqrt(spread + epsilon) * gain + shift

def smooth_gelu(inputs):
    return 0.5 * inputs * (1.0 + jnp.tanh(gelu_coef * (inputs + 0.044715 * inputs * inputs * inputs)))

def residual_layer(stream, mask_block, onehot, layer_weights):
    gain_one, shift_one, query_w, key_w, value_w, out_w, table, gain_two, shift_two, up_w, down_w = layer_weights
    groups, length, model_width = stream.shape
    input_one = low(layer_norm(stream, gain_one, shift_one))

    def project(matrix):
        product = jnp.einsum('gld,de->gle', input_one, matrix, precision=highest)
        return rounded(product).reshape(groups, length, HEADS, HEAD)
    queries = project(query_w)
    key_rows = project(key_w)
    values = project(value_w)
    rel_bias = jnp.einsum('ijb,bh->hij', onehot, table.reshape(BUCKETS, HEADS), precision=highest)
    raw_scores = jnp.einsum('gihe,gjhe->ghij', queries, key_rows, precision=highest) * HEAD ** (-0.5) + rel_bias
    scores = jnp.where(mask_block, low_back(raw_scores), -1e+30)
    row_peak = lax.optimization_barrier(jnp.max(scores, -1, keepdims=True))
    exp_terms = jnp.exp(scores - row_peak)
    prob_rows = exp_terms / lax.optimization_barrier(jnp.sum(exp_terms, -1, keepdims=True))
    mixed = jnp.einsum('ghij,gjhe->gihe', low(prob_rows), values, precision=highest).reshape(groups, length, model_width)
    branch = low_back(jnp.einsum('gld,de->gle', rounded(mixed), out_w, precision=highest))
    middle = stream + branch
    input_two = low(layer_norm(middle, gain_two, shift_two))
    upward = low_back(jnp.einsum('gld,df->glf', input_two, up_w, precision=highest))
    activated = low(smooth_gelu(upward))
    return middle + low_back(jnp.einsum('glf,fd->gld', activated, down_w, precision=highest))

def reference(tokens, seg_ids, buckets, cotangent, ln1_gain, ln1_bias, w_query, w_key, w_value, w_out, rel_table, ln2_gain, ln2_bias, w_up, w_down):
    rows_all = N_WIDE * N_NARROW
    grouped = math.gcd(max(4096 // TOK_DEV, 1), rows_all)
    blocks = rows_all // grouped
    positions = jnp.arange(TOK_DEV, dtype=jnp.int32)
    distance = jnp.maximum(positions[:, None] - positions[None, :], 0).astype(jnp.int32)
    onehot = (buckets[distance][:, :, None] == jnp.arange(BUCKETS, dtype=jnp.int32)[None, None, :]).astype(jnp.float32)
    causal = positions[:, None] >= positions[None, :]
    segments = seg_ids.reshape(blocks, grouped, TOK_DEV)
    masks = ((segments[:, :, :, None] == segments[:, :, None, :]) & causal[None, None])[:, :, None]
    weights = (ln1_gain.astype(jnp.float32), ln1_bias.astype(jnp.float32), w_query.astype(jnp.float32), w_key.astype(jnp.float32), w_value.astype(jnp.float32), w_out.astype(jnp.float32), rel_table.astype(jnp.float32), ln2_gain.astype(jnp.float32), ln2_bias.astype(jnp.float32), w_up.astype(jnp.float32), w_down.astype(jnp.float32))
    inputs = tokens.astype(jnp.float32).reshape(blocks, grouped, TOK_DEV, D)

    def forward(inputs, weights):

        def group_pass(block):
            stream, mask_block = block
            layer_outs = []
            for layer_at in range(2):
                stream = residual_layer(stream, mask_block, onehot, tuple((w[layer_at] for w in weights)))
                layer_outs.append(stream)
            return jnp.stack(layer_outs)
        return lax.map(jax.checkpoint(group_pass), (inputs, masks))
    outputs, pullback = jax.vjp(forward, inputs, weights)
    final_grad = cotangent.astype(jnp.float32).reshape(blocks, grouped, TOK_DEV, D)
    seed_grad = jnp.stack([jnp.zeros_like(final_grad), final_grad], axis=1)
    grad_inputs, grad_weights = pullback(seed_grad)
    acts = jnp.moveaxis(outputs, 1, 0).reshape(2, rows_all * TOK_DEV, D).astype(jnp.bfloat16)
    grad_tokens = grad_inputs.reshape(rows_all * TOK_DEV, D)
    return (acts, grad_tokens, grad_weights[0], grad_weights[1], grad_weights[2], grad_weights[3], grad_weights[4], grad_weights[5], grad_weights[6], grad_weights[7], grad_weights[8], grad_weights[9], grad_weights[10])
```

```python
import functools

import jax
import jax.numpy as jnp
from jax import lax
from jax.experimental import pallas as pl
from jax.experimental.pallas import tpu as pltpu
from jax.sharding import PartitionSpec as P

HEADS = 16
HEAD = 64
BUCKETS = 32

epsilon = 1e-05
gelu_coef = 0.7978845608028654


def normalize(stream, gain, shift):
    center = jnp.mean(stream, -1, keepdims=True)
    centered = stream - center
    spread = jnp.mean(centered * centered, -1, keepdims=True)
    inverse = lax.rsqrt(spread + epsilon)
    normed = centered * inverse
    return (normed, inverse, normed * gain.astype(jnp.float32) + shift.astype(jnp.float32))


def norm_back(grad_hidden, normed, inverse, gain):
    scaled = grad_hidden * gain.astype(jnp.float32)
    return inverse * (
        scaled
        - jnp.mean(scaled, -1, keepdims=True)
        - normed * jnp.mean(scaled * normed, -1, keepdims=True)
    )


def smooth_gelu(inputs):
    return (
        0.5 * inputs * (1.0 + jnp.tanh(gelu_coef * (inputs + 0.044715 * inputs * inputs * inputs)))
    )


def gelu_slope(inputs):
    tangent = jnp.tanh(gelu_coef * (inputs + 0.044715 * inputs * inputs * inputs))
    return 0.5 * (1.0 + tangent) + 0.5 * inputs * (1.0 - tangent * tangent) * gelu_coef * (
        1.0 + 3.0 * 0.044715 * inputs * inputs
    )


MESH = pl.DeviceIdType.MESH
TILE = 128
BF = jnp.bfloat16
F32 = jnp.float32
ORDERS = (("y", "x", "z"), ("z", "y", "x"), ("x", "z", "y"))
CHAINS = (
    ((0, 0, 10, 0), (0, 10, 10, 1), (0, 20, 12, 2), (3, 0, 2, 0)),
    ((1, 0, 10, 0), (1, 10, 10, 1), (1, 20, 12, 2)),
    ((2, 0, 3, 0), (2, 3, 3, 1), (2, 6, 2, 2)),
)


def place():
    wide, narrow = lax.axis_index("wide"), lax.axis_index("narrow")
    return {
        "x": wide // 16,
        "y": narrow * 2 + (wide // 8) % 2,
        "z": (wide // 2) % 4,
        "c": wide % 2,
    }


def device(at):
    return (((at["x"] * 2 + at["y"] % 2) * 4 + at["z"]) * 2 + at["c"], at["y"] // 2)


def moved(at, axis, by):
    new = dict(at)
    new[axis] = (at[axis] + by) % (2 if axis == "c" else 4)
    return new


def pick(ref, chain, sel, lead=()):
    array, tile, tiles, _ = chain
    y = sel["y"]
    columns = pl.ds(tile * TILE, tiles * TILE)
    rows = pl.ds(0, 64 if array == 2 else 16)
    if y is None:
        low = pl.ds(0, 2)
    elif isinstance(y, tuple):
        low = pl.ds(y[0], 1)
    else:
        low = y % 2
        if array == 2:
            rows = pl.ds(pl.multiple_of((y // 2) * 32, 32), 32)
        else:
            half = tiles // 2 * TILE
            columns = pl.ds(pl.multiple_of(tile * TILE + (y // 2) * half, TILE), half)

    def one(v):
        return pl.ds(0, 4) if v is None else v

    index = lead + (one(sel["x"]), low, one(sel["z"]))
    if "c" in sel:
        index = index + (sel["c"],)
    return ref.at[index + (rows, columns)]


def half_of(axis, part):
    return (part,) if axis == "y" else pl.ds(2 * part, 2)


def greet(at, peers):
    barrier = pltpu.get_barrier_semaphore()
    for axis, by in peers:
        pl.semaphore_signal(barrier, inc=1, device_id=device(moved(at, axis, by)), device_id_type=MESH)
    pl.semaphore_wait(barrier, len(peers))


PEERS = tuple((a, b) for a in "xyz" for b in (1, 3, 2)) + (("c", 1),)


class Gather:
    def __init__(self, at, ref, chain, send, recv):
        self.at, self.ref, self.chain, self.send, self.recv = at, ref, chain, send, recv
        self.axes = ORDERS[chain[3]]
        self.count = 0
        self.sent = []

    def place_own(self, mine, sem):
        array, tile, tiles, _ = self.chain
        side = self.at["y"] // 2
        if array == 2:
            where = (pl.ds(pl.multiple_of(side * 32, 32), 32), pl.ds(tile * TILE, tiles * TILE))
        else:
            wide = tiles // 2 * TILE
            where = (slice(None), pl.ds(pl.multiple_of(tile * TILE + side * wide, TILE), wide))
        self.own = pltpu.make_async_copy(mine.at[where], pick(self.ref, self.chain, self.sel(())), sem)
        self.own.start()

    def copy(self, sel, axis, by):
        slot = self.count
        self.count += 1
        block = pick(self.ref, self.chain, sel)
        made = pltpu.make_async_remote_copy(
            src_ref=block,
            dst_ref=block,
            send_sem=self.send.at[slot],
            recv_sem=self.recv.at[slot],
            device_id=device(moved(self.at, axis, by)),
            device_id_type=MESH,
        )
        made.start()
        self.sent.append(made)
        return made

    def sel(self, done, axis=None, by=0, half=None):
        at = {k: self.at[k] for k in "xyzc"}
        for d in done:
            at[d] = None
        if half is not None:
            at[done[0]] = half_of(done[0], half)
        if axis is not None:
            at[axis] = (self.at[axis] + by) % 4
        return at

    def step(self, k):
        a1, a2, a3 = self.axes
        if k == 0:
            self.own.wait()
            own = self.sel(())
            self.first = [self.copy(own, a1, by) for by in (1, 3, 2)]
        elif k in (1, 3):
            done, axis = ((a1,), a2) if k == 1 else ((a1, a2), a3)
            for c in self.first:
                c.wait_recv()
            own = self.sel(done)
            self.pair = [self.copy(own, axis, 1), self.copy(own, axis, 3)]
            if k == 3:
                self.across = [self.copy(own, "c", 1)]
        elif k in (2, 4):
            done, axis = ((a1,), a2) if k == 2 else ((a1, a2), a3)
            self.pair[0].wait_recv()
            forward = self.copy(self.sel(done, axis, 3, 0), axis, 1)
            self.pair[1].wait_recv()
            self.first = [forward, self.copy(self.sel(done, axis, 1, 1), axis, 3)]
            if k == 4:
                for by in (3, 1):
                    self.across.append(self.copy(self.sel(done, axis, by), "c", 1))
        elif k == 5:
            for c in self.first:
                c.wait_recv()
            self.across.append(self.copy(self.sel((a1, a2), a3, 2), "c", 1))
        elif k == 6:
            for c in self.across:
                c.wait_recv()
            for c in self.sent:
                c.wait_send()


N_GATHER = 15


def gather_kernel(n_layers, att, up, down, small, *rest):
    outs, (send, recv, local) = rest[:-3], rest[-3:]
    at = place()
    greet(at, PEERS)
    mine = (att, up, down, small)
    groups = []
    index = 0
    for layer in range(n_layers):
        for group in CHAINS:
            chains = []
            for chain in group:
                if chain[0] == 3:
                    if layer > 0:
                        continue
                    ref = outs[3 * n_layers]
                else:
                    ref = outs[3 * layer + chain[0]]
                made = Gather(at, ref, chain, send.at[index], recv.at[index])
                made.place_own(mine[chain[0]] if chain[0] == 3 else mine[chain[0]].at[layer], local.at[index])
                chains.append(made)
                index += 1
            groups.append(chains)
    for slot in range(7 + len(groups) - 1):
        for g, chains in reversed(list(enumerate(groups))):
            k = slot - g
            if 0 <= k < 7:
                for chain in chains:
                    chain.step(k)


def gather(att, up, down, small):
    n_layers = att.shape[0]
    n_chains = n_layers * 9 + 1
    shapes = []
    for _ in range(n_layers):
        shapes += [(4, 2, 4, 2, 16, 4096), (4, 2, 4, 2, 16, 4096), (4, 2, 4, 2, 64, 1024)]
    shapes.append((4, 2, 4, 2, 16, 256))
    return pl.pallas_call(
        functools.partial(gather_kernel, n_layers),
        out_shape=[jax.ShapeDtypeStruct(s, BF) for s in shapes],
        in_specs=[pl.BlockSpec(memory_space=pltpu.VMEM)] * 4,
        out_specs=[pl.BlockSpec(memory_space=pl.ANY)] * len(shapes),
        scratch_shapes=[
            pltpu.SemaphoreType.DMA((n_chains, N_GATHER)),
            pltpu.SemaphoreType.DMA((n_chains, N_GATHER)),
            pltpu.SemaphoreType.DMA((n_chains,)),
        ],
        compiler_params=pltpu.CompilerParams(collective_id=0, has_side_effects=True),
        name="gather_weights",
    )(att, up, down, small)


N_SCATTER = 12
PART_SHAPES = ((4, 2, 4, 16, 4096), (4, 2, 4, 16, 4096), (4, 2, 4, 64, 1024), (4, 2, 4, 16, 256))
OUT_SHAPES = ((16, 4096), (16, 4096), (64, 1024), (16, 256))
SCATTER_ORDER = (CHAINS[2], CHAINS[1], CHAINS[0])


def landing_shapes(chain):
    array, _, tiles, order = chain
    a1, a2, a3 = ORDERS[order]
    rows, cols = (64, tiles * TILE) if array == 2 else (16, tiles * TILE)
    unit = (rows // 2, cols) if array == 2 else (rows, cols // 2)

    def block(full, half=None):
        dims = []
        for axis in "xyz":
            if axis in full:
                size = 2 if axis == "y" else 4
                dims.append(size // 2 if axis == half else size)
        return tuple(dims) + ((rows, cols) if "y" in full else unit)

    return (
        (2,) + block((a1, a2), a1),
        (2,) + block((a1, a2)),
        (2,) + block((a1,), a1),
        (2,) + block((a1,)),
        (3,) + unit,
        unit,
    )


class Scatter:
    def __init__(self, at, part, out, landing, chain, send, recv):
        self.at, self.part, self.out, self.chain = at, part, out, chain
        self.landing, self.send, self.recv = landing, send, recv
        self.axes = ORDERS[chain[3]]
        self.count = 0
        self.sent = []

    def copy(self, src, dst, axis, by):
        slot = self.count
        self.count += 1
        made = pltpu.make_async_remote_copy(
            src_ref=src,
            dst_ref=dst,
            send_sem=self.send.at[slot],
            recv_sem=self.recv.at[slot],
            device_id=device(moved(self.at, axis, by)),
            device_id_type=MESH,
        )
        made.start()
        self.sent.append(made)
        return made

    def sel(self, done, axis=None, by=0, half=None):
        at = {k: self.at[k] for k in "xyz"}
        for d in done:
            at[d] = None
        if half is not None:
            at[done[0]] = half_of(done[0], half)
        if axis is not None:
            at[axis] = (self.at[axis] + by) % 4
        return pick(self.part, self.chain, at)

    def step(self, k):
        a1, a2, a3 = self.axes
        if k in (1, 3):
            done, axis = ((a1, a2), a3) if k == 1 else ((a1,), a2)
            land, blocks = self.landing[k - 1], self.landing[k]
            self.blocks = []
            for i, by in ((0, 1), (1, 3)):
                self.halves[i].wait_recv()
                add_to(self.sel(done, axis, by, i), (land.at[i],))
                self.blocks.append(self.copy(self.sel(done, axis, by), blocks.at[i], axis, by))
        if k in (2, 4):
            done = (a1, a2) if k == 2 else (a1,)
            blocks = self.landing[k - 1]
            for c in self.blocks:
                c.wait_recv()
            add_to(self.sel(done), (blocks.at[0], blocks.at[1]))
        if k in (0, 2):
            done, axis = ((a1, a2), a3) if k == 0 else ((a1,), a2)
            land = self.landing[0 if k == 0 else 2]
            self.halves = [
                self.copy(self.sel(done, axis, 2, 0), land.at[0], axis, 1),
                self.copy(self.sel(done, axis, 2, 1), land.at[1], axis, 3),
            ]
        if k == 4:
            land = self.landing[4]
            self.units = [self.copy(self.sel((), a1, by), land.at[i], a1, by) for i, by in enumerate((1, 3, 2))]
        if k == 5:
            land = self.landing[4]
            for c in self.units:
                c.wait_recv()
            add_to(self.sel(()), (land.at[0], land.at[1], land.at[2]))
            self.last = self.copy(self.sel(()), self.landing[5], "y", 2)
        if k == 6:
            self.last.wait_recv()
            array, tile, tiles, _ = self.chain
            high = self.at["y"] // 2
            for side, ref in ((high, self.sel(())), (1 - high, self.landing[5])):
                if array == 2:
                    where = (pl.ds(pl.multiple_of(side * 32, 32), 32), pl.ds(tile * TILE, tiles * TILE))
                else:
                    wide = tiles // 2 * TILE
                    where = (slice(None), pl.ds(pl.multiple_of(tile * TILE + side * wide, TILE), wide))
                self.out[where] = ref[...].astype(F32)
            for c in self.sent:
                c.wait_send()


def add_to(ref, terms):
    lead = ref.shape[:-2]
    if not lead:
        total = ref[...]
        for t in terms:
            total = total + t[...]
        ref[...] = total
        return
    n = 1
    for d in lead:
        n *= d

    def body(i, _):
        index = []
        rest = i
        for d in reversed(lead):
            index.append(rest % d)
            rest = rest // d
        index = tuple(reversed(index))
        total = ref[index]
        for t in terms:
            total = total + t[index]
        ref[index] = total
        return 0

    lax.fori_loop(0, n, body, 0)


def scatter_kernel(gqkv, go, gup, gdown, gsmall, *rest):
    outs, rest = rest[:4], rest[4:]
    parts, lands, rest = rest[:4], rest[4:8], rest[8:]
    landings, (send, recv, local, across_s, across_r) = rest[:-5], rest[-5:]
    at = place()
    c = at["c"]
    greet(at, PEERS)
    partner = device(moved(at, "c", 1))

    def half(ref, core):
        return ref.at[:, :, :, core]

    loads = {}
    for array, src, cols in (
        (2, gdown, None),
        (1, gup, None),
        (0, gqkv, (0, 3072)),
        (0, go, (3072, 1024)),
        (3, gsmall, None),
    ):
        i = len(loads)
        window = (lambda r: r) if cols is None else (lambda r, w=cols: r.at[:, :, :, :, pl.ds(w[0], w[1])])
        own = pltpu.make_async_copy(half(src, c), window(parts[array]), local.at[i])
        other = pltpu.make_async_remote_copy(
            src_ref=half(src, 1 - c),
            dst_ref=window(lands[array]),
            send_sem=across_s.at[i],
            recv_sem=across_r.at[i],
            device_id=partner,
            device_id_type=MESH,
        )
        own.start()
        other.start()
        loads[i] = (own, other)
    needs = {2: (0,), 1: (1,), 0: (2, 3), 3: (4,)}
    groups = []
    index = 0
    for group in SCATTER_ORDER:
        chains = []
        for chain in group:
            land = landings[6 * index : 6 * index + 6]
            chains.append(Scatter(at, parts[chain[0]], outs[chain[0]], land, chain, send.at[index], recv.at[index]))
            index += 1
        groups.append(chains)

    def enter(chains):
        for array in sorted({chain.chain[0] for chain in chains}):
            for i in needs[array]:
                loads[i][0].wait()
                loads[i][1].wait_recv()
            add_to(parts[array], (lands[array],))

    for slot in range(8 + len(groups) - 1):
        for g, chains in enumerate(groups):
            k = slot - g
            if k == 0:
                enter(chains)
            elif 0 < k < 8:
                for chain in chains:
                    chain.step(k - 1)
    for i in loads:
        loads[i][1].wait_send()


def scatter(gqkv, go, gup, gdown, gsmall):
    lead = (4, 2, 4, 2)
    args = (
        gqkv.reshape(lead + (16, 3072)),
        go.reshape(lead + (16, 1024)),
        gup.reshape(lead + (16, 4096)),
        gdown.reshape(lead + (64, 1024)),
        gsmall.reshape(lead + (16, 256)),
    )
    chains = [c for g in SCATTER_ORDER for c in g]
    scratch = [pltpu.VMEM(s, BF) for s in PART_SHAPES] * 2
    for chain in chains:
        scratch += [pltpu.VMEM(s, BF) for s in landing_shapes(chain)]
    scratch += [pltpu.SemaphoreType.DMA((len(chains), N_SCATTER))] * 2
    scratch += [pltpu.SemaphoreType.DMA((5,))] * 3
    return pl.pallas_call(
        scatter_kernel,
        out_shape=[jax.ShapeDtypeStruct(s, F32) for s in OUT_SHAPES],
        in_specs=[pl.BlockSpec(memory_space=pl.ANY)] * 5,
        out_specs=[pl.BlockSpec(memory_space=pltpu.VMEM)] * 4,
        scratch_shapes=scratch,
        compiler_params=pltpu.CompilerParams(collective_id=1, has_side_effects=True, vmem_limit_bytes=56 << 20),
        name="scatter_grads",
    )(*args)


def on_device(
    tokens,
    seg_ids,
    buckets,
    cotangent,
    ln1_gain,
    ln1_bias,
    w_query,
    w_key,
    w_value,
    w_out,
    rel_table,
    ln2_gain,
    ln2_bias,
    w_up,
    w_down,
):
    length = tokens.shape[0]
    model_width = tokens.shape[1]
    score_scale = HEAD ** (-0.5)
    positions = jnp.arange(length, dtype=jnp.int32)
    distance = jnp.maximum(positions[:, None] - positions[None, :], 0)
    at_distance = (distance[:, :, None] == positions[None, None, :]).astype(jnp.bfloat16)
    bucket_of = (buckets[:, None] == jnp.arange(BUCKETS, dtype=jnp.int32)[None, :]).astype(jnp.bfloat16)
    onehot = jnp.dot(at_distance, bucket_of, preferred_element_type=jnp.float32).astype(jnp.bfloat16)
    allowed = (positions[:, None] >= positions[None, :]) & (seg_ids[:, None] == seg_ids[None, :])

    def masked_scores(queries, key_rows, rel_bias):
        raw_scores = (
            jnp.einsum("ihe,jhe->hij", queries, key_rows, preferred_element_type=jnp.float32)
            * score_scale
            + rel_bias
        )
        return jnp.where(allowed[None], raw_scores, -1e30)

    def layer_backward(grad_result, saved_layer, layer_weights):
        (
            gain_one,
            shift_one,
            query_w,
            key_w,
            value_w,
            out_w,
            table,
            gain_two,
            shift_two,
            up_w,
            down_w,
        ) = layer_weights
        (
            normed_one,
            inverse_one,
            input_one,
            queries,
            key_rows,
            values,
            rel_bias,
            log_total,
            mixed,
            normed_two,
            inverse_two,
            input_two,
            upward,
            activated,
        ) = saved_layer
        down_in = grad_result.astype(jnp.bfloat16)
        grad_down = jnp.einsum("lf,ld->fd", activated, down_in, preferred_element_type=jnp.float32)
        grad_active = jnp.einsum("ld,fd->lf", down_in, down_w, preferred_element_type=jnp.float32)
        grad_upward = (grad_active * gelu_slope(upward)).astype(jnp.bfloat16)
        grad_up = jnp.einsum(
            "ld,lf->df", input_two, grad_upward, preferred_element_type=jnp.float32
        )
        grad_hidden_two = jnp.einsum(
            "lf,df->ld", grad_upward, up_w, preferred_element_type=jnp.float32
        )
        grad_gain_two = jnp.sum(grad_hidden_two * normed_two, 0)
        grad_shift_two = jnp.sum(grad_hidden_two, 0)
        grad_middle = grad_result + norm_back(grad_hidden_two, normed_two, inverse_two, gain_two)
        branch_in = grad_middle.astype(jnp.bfloat16)
        grad_out_w = jnp.einsum("ld,le->de", mixed, branch_in, preferred_element_type=jnp.float32)
        grad_mixed = jnp.einsum("le,de->ld", branch_in, out_w, preferred_element_type=jnp.float32)
        grad_mixed = grad_mixed.astype(jnp.bfloat16).reshape(length, HEADS, HEAD)
        scores = masked_scores(queries, key_rows, rel_bias)
        prob_rows = jnp.exp(scores - log_total)
        grad_probs = jnp.einsum(
            "ihe,jhe->hij", grad_mixed, values, preferred_element_type=jnp.float32
        )
        grad_values = jnp.einsum(
            "hij,ihe->jhe",
            prob_rows.astype(jnp.bfloat16),
            grad_mixed,
            preferred_element_type=jnp.float32,
        )
        grad_values = grad_values.astype(jnp.bfloat16).reshape(length, model_width)
        grad_scores = (
            prob_rows * (grad_probs - jnp.sum(prob_rows * grad_probs, -1, keepdims=True))
        ).astype(jnp.bfloat16)
        grad_queries = (
            (
                jnp.einsum(
                    "hij,jhe->ihe", grad_scores, key_rows, preferred_element_type=jnp.float32
                )
                * score_scale
            )
            .astype(jnp.bfloat16)
            .reshape(length, model_width)
        )
        grad_keys = (
            (
                jnp.einsum("hij,ihe->jhe", grad_scores, queries, preferred_element_type=jnp.float32)
                * score_scale
            )
            .astype(jnp.bfloat16)
            .reshape(length, model_width)
        )
        grad_bias_table = jnp.einsum(
            "hij,ijb->bh", grad_scores, onehot, preferred_element_type=jnp.float32
        ).reshape(BUCKETS * HEADS)
        grad_all = jnp.concatenate([grad_queries, grad_keys, grad_values], 1)
        grad_qkv = jnp.einsum("ld,le->de", input_one, grad_all, preferred_element_type=jnp.float32)
        grad_hidden_one = jnp.einsum(
            "le,de->ld", grad_queries, query_w, preferred_element_type=jnp.float32
        )
        grad_hidden_one = grad_hidden_one + jnp.einsum(
            "le,de->ld", grad_keys, key_w, preferred_element_type=jnp.float32
        )
        grad_hidden_one = grad_hidden_one + jnp.einsum(
            "le,de->ld", grad_values, value_w, preferred_element_type=jnp.float32
        )
        grad_gain_one = jnp.sum(grad_hidden_one * normed_one, 0)
        grad_shift_one = jnp.sum(grad_hidden_one, 0)
        grad_stream = grad_middle + norm_back(grad_hidden_one, normed_one, inverse_one, gain_one)
        small = jnp.concatenate(
            [
                grad_gain_one.reshape(64, 16),
                grad_shift_one.reshape(64, 16),
                grad_gain_two.reshape(64, 16),
                grad_shift_two.reshape(64, 16),
                grad_bias_table.reshape(64, 8),
            ],
            1,
        )
        small = jnp.pad(small[:, None], ((0, 0), (0, 15), (0, 56)))
        small = jnp.concatenate([small, small], 2)
        grads = tuple(g.astype(BF) for g in (grad_qkv, grad_out_w, grad_up, grad_down, small))
        return (grad_stream, grads)

    def shares(layer_at):
        return jnp.concatenate(
            [ln1_gain[layer_at], ln1_bias[layer_at], ln2_gain[layer_at], ln2_bias[layer_at], rel_table[layer_at]]
        )

    small = jnp.stack([shares(0), shares(1)])
    small = jnp.pad(small, ((0, 14), (0, 56)))
    fetched = gather(jnp.concatenate([w_query, w_key, w_value, w_out], 2), w_up, w_down, jnp.concatenate([small, small], 1))
    small_all = fetched[6].reshape(64, 16, 256)[:, :2, :128]

    def weights_of(layer_at):
        att = fetched[3 * layer_at].reshape(1024, 4096)
        up = fetched[3 * layer_at + 1].reshape(1024, 4096)
        down = fetched[3 * layer_at + 2].reshape(4096, 1024)
        mine = small_all[:, layer_at]
        return (
            mine[:, 0:16].reshape(1024),
            mine[:, 16:32].reshape(1024),
            att[:, :1024],
            att[:, 1024:2048],
            att[:, 2048:3072],
            att[:, 3072:],
            mine[:, 64:72].reshape(512),
            mine[:, 32:48].reshape(1024),
            mine[:, 48:64].reshape(1024),
            up,
            down,
        )

    stream = tokens.astype(jnp.float32)
    saved_all = []
    layer_acts = []
    for layer_at in range(2):
        layer_weights = weights_of(layer_at)
        (
            layer_gain_one,
            layer_shift_one,
            layer_query_w,
            layer_key_w,
            layer_value_w,
            layer_out_w,
            layer_table,
            layer_gain_two,
            layer_shift_two,
            layer_up_w,
            layer_down_w,
        ) = layer_weights
        layer_normed_one, layer_inverse_one, hidden_one = normalize(
            stream, layer_gain_one, layer_shift_one
        )
        layer_input_one = hidden_one.astype(jnp.bfloat16)
        layer_queries = (
            jnp.dot(layer_input_one, layer_query_w, preferred_element_type=jnp.float32)
            .astype(jnp.bfloat16)
            .reshape(length, HEADS, HEAD)
        )
        layer_key_rows = (
            jnp.dot(layer_input_one, layer_key_w, preferred_element_type=jnp.float32)
            .astype(jnp.bfloat16)
            .reshape(length, HEADS, HEAD)
        )
        layer_values = (
            jnp.dot(layer_input_one, layer_value_w, preferred_element_type=jnp.float32)
            .astype(jnp.bfloat16)
            .reshape(length, HEADS, HEAD)
        )
        layer_rel_bias = jnp.einsum(
            "ijb,bh->hij",
            onehot,
            layer_table.reshape(BUCKETS, HEADS),
            preferred_element_type=jnp.float32,
        )
        layer_scores = masked_scores(layer_queries, layer_key_rows, layer_rel_bias)
        row_peak = jnp.max(layer_scores, -1, keepdims=True)
        exp_terms = jnp.exp(layer_scores - row_peak)
        totals = jnp.sum(exp_terms, -1, keepdims=True)
        layer_prob_rows = exp_terms / totals
        layer_log_total = row_peak + jnp.log(totals)
        layer_mixed = jnp.einsum(
            "hij,jhe->ihe",
            layer_prob_rows.astype(jnp.bfloat16),
            layer_values,
            preferred_element_type=jnp.float32,
        )
        layer_mixed = layer_mixed.reshape(length, model_width).astype(jnp.bfloat16)
        middle = stream + jnp.dot(layer_mixed, layer_out_w, preferred_element_type=jnp.float32)
        layer_normed_two, layer_inverse_two, hidden_two = normalize(
            middle, layer_gain_two, layer_shift_two
        )
        layer_input_two = hidden_two.astype(jnp.bfloat16)
        layer_upward = jnp.dot(layer_input_two, layer_up_w, preferred_element_type=jnp.float32)
        layer_activated = smooth_gelu(layer_upward).astype(jnp.bfloat16)
        result = middle + jnp.dot(layer_activated, layer_down_w, preferred_element_type=jnp.float32)
        layer_saved_layer = (
            layer_normed_one,
            layer_inverse_one,
            layer_input_one,
            layer_queries,
            layer_key_rows,
            layer_values,
            layer_rel_bias,
            layer_log_total,
            layer_mixed,
            layer_normed_two,
            layer_inverse_two,
            layer_input_two,
            layer_upward,
            layer_activated,
        )
        stream = result
        saved_layer = layer_saved_layer
        saved_all.append(saved_layer)
        layer_acts.append(stream.astype(jnp.bfloat16))
    grad_stream = cotangent.astype(jnp.float32)
    reduced = [None, None]
    for layer_at in (1, 0):
        grad_stream, grads = layer_backward(grad_stream, saved_all[layer_at], weights_of(layer_at))
        reduced[layer_at] = scatter(*grads)
    stacked = [jnp.stack([reduced[0][i], reduced[1][i]]) for i in range(4)]
    att, up, down, small = stacked
    return (
        jnp.stack(layer_acts),
        grad_stream,
        small[:, 0, 0:16],
        small[:, 0, 16:32],
        att[:, :, :1024],
        att[:, :, 1024:2048],
        att[:, :, 2048:3072],
        att[:, :, 3072:],
        small[:, 0, 64:72],
        small[:, 0, 32:48],
        small[:, 0, 48:64],
        up,
        down,
    )


def solution(mesh):
    placed = (
        P(("wide", "narrow"), None),
        P(("wide", "narrow")),
        P(),
        P(("wide", "narrow"), None),
        P(None, "wide"),
        P(None, "wide"),
        P(None, "wide", None),
        P(None, "wide", None),
        P(None, "wide", None),
        P(None, "wide", None),
        P(None, "wide"),
        P(None, "wide"),
        P(None, "wide"),
        P(None, "wide", None),
        P(None, "wide", None),
    )
    return jax.shard_map(
        on_device,
        mesh=mesh,
        in_specs=placed,
        out_specs=(
            P(None, ("wide", "narrow"), None),
            P(("wide", "narrow"), None),
            P(None, "wide"),
            P(None, "wide"),
            P(None, "wide", None),
            P(None, "wide", None),
            P(None, "wide", None),
            P(None, "wide", None),
            P(None, "wide"),
            P(None, "wide"),
            P(None, "wide"),
            P(None, "wide", None),
            P(None, "wide", None),
        ),
        check_vma=False,
    )
```

```python
import functools

import jax
import jax.numpy as jnp
from jax import lax
from jax.experimental import pallas as pl
from jax.experimental.pallas import tpu as pltpu
from jax.sharding import PartitionSpec as P

epsilon = 1e-05
gelu_coef = 0.7978845608028654


def normalize(stream, gain, shift):
    center = jnp.mean(stream, -1, keepdims=True)
    centered = stream - center
    spread = jnp.mean(centered * centered, -1, keepdims=True)
    inverse = lax.rsqrt(spread + epsilon)
    normed = centered * inverse
    return (normed, inverse, normed * gain.astype(jnp.float32) + shift.astype(jnp.float32))


def norm_back(grad_hidden, normed, inverse, gain):
    scaled = grad_hidden * gain.astype(jnp.float32)
    return inverse * (
        scaled
        - jnp.mean(scaled, -1, keepdims=True)
        - normed * jnp.mean(scaled * normed, -1, keepdims=True)
    )


MESH = pl.DeviceIdType.MESH
TILE = 128
BF = jnp.bfloat16
F32 = jnp.float32
ORDERS = (("y", "x", "z"), ("z", "y", "x"), ("x", "z", "y"))
CHAINS = (
    ((0, 0, 10, 0), (0, 10, 10, 1), (0, 20, 12, 2), (3, 0, 2, 0)),
    ((1, 0, 10, 0), (1, 10, 10, 1), (1, 20, 12, 2)),
    ((2, 0, 3, 0), (2, 3, 3, 1), (2, 6, 2, 2)),
)


def place():
    wide, narrow = lax.axis_index("wide"), lax.axis_index("narrow")
    return {
        "x": wide // 16,
        "y": narrow * 2 + (wide // 8) % 2,
        "z": (wide // 2) % 4,
        "c": wide % 2,
    }


def device(at):
    return (((at["x"] * 2 + at["y"] % 2) * 4 + at["z"]) * 2 + at["c"], at["y"] // 2)


def moved(at, axis, by):
    new = dict(at)
    new[axis] = (at[axis] + by) % (2 if axis == "c" else 4)
    return new


def pick(ref, chain, sel, lead=()):
    array, tile, tiles, _ = chain
    y = sel["y"]
    columns = pl.ds(tile * TILE, tiles * TILE)
    rows = pl.ds(0, 64 if array == 2 else 16)
    if y is None:
        low = pl.ds(0, 2)
    elif isinstance(y, tuple):
        low = pl.ds(y[0], 1)
    else:
        low = y % 2
        if array == 2:
            rows = pl.ds(pl.multiple_of((y // 2) * 32, 32), 32)
        else:
            half = tiles // 2 * TILE
            columns = pl.ds(pl.multiple_of(tile * TILE + (y // 2) * half, TILE), half)

    def one(v):
        return pl.ds(0, 4) if v is None else v

    index = lead + (one(sel["x"]), low, one(sel["z"]))
    if "c" in sel:
        index = index + (sel["c"],)
    return ref.at[index + (rows, columns)]


def half_of(axis, part):
    return (part,) if axis == "y" else pl.ds(2 * part, 2)


def greet(at, peers):
    barrier = pltpu.get_barrier_semaphore()
    for axis, by in peers:
        pl.semaphore_signal(barrier, inc=1, device_id=device(moved(at, axis, by)), device_id_type=MESH)
    pl.semaphore_wait(barrier, len(peers))


PEERS = tuple((a, b) for a in "xyz" for b in (1, 3, 2)) + (("c", 1),)


class Gather:
    def __init__(self, at, ref, chain, send, recv):
        self.at, self.ref, self.chain, self.send, self.recv = at, ref, chain, send, recv
        self.axes = ORDERS[chain[3]]
        self.count = 0
        self.sent = []

    def place_own(self, mine, sem):
        array, tile, tiles, _ = self.chain
        side = self.at["y"] // 2
        if array == 2:
            where = (pl.ds(pl.multiple_of(side * 32, 32), 32), pl.ds(tile * TILE, tiles * TILE))
        else:
            wide = tiles // 2 * TILE
            where = (slice(None), pl.ds(pl.multiple_of(tile * TILE + side * wide, TILE), wide))
        self.own = pltpu.make_async_copy(mine.at[where], pick(self.ref, self.chain, self.sel(())), sem)
        self.own.start()

    def copy(self, sel, axis, by):
        slot = self.count
        self.count += 1
        block = pick(self.ref, self.chain, sel)
        made = pltpu.make_async_remote_copy(
            src_ref=block,
            dst_ref=block,
            send_sem=self.send.at[slot],
            recv_sem=self.recv.at[slot],
            device_id=device(moved(self.at, axis, by)),
            device_id_type=MESH,
        )
        made.start()
        self.sent.append(made)
        return made

    def sel(self, done, axis=None, by=0, half=None):
        at = {k: self.at[k] for k in "xyzc"}
        for d in done:
            at[d] = None
        if half is not None:
            at[done[0]] = half_of(done[0], half)
        if axis is not None:
            at[axis] = (self.at[axis] + by) % 4
        return at

    def step(self, k):
        a1, a2, a3 = self.axes
        if k == 0:
            self.own.wait()
            own = self.sel(())
            self.first = [self.copy(own, a1, by) for by in (1, 3, 2)]
        elif k in (1, 3):
            done, axis = ((a1,), a2) if k == 1 else ((a1, a2), a3)
            for c in self.first:
                c.wait_recv()
            own = self.sel(done)
            self.pair = [self.copy(own, axis, 1), self.copy(own, axis, 3)]
            if k == 3:
                self.across = [self.copy(own, "c", 1)]
        elif k in (2, 4):
            done, axis = ((a1,), a2) if k == 2 else ((a1, a2), a3)
            self.pair[0].wait_recv()
            forward = self.copy(self.sel(done, axis, 3, 0), axis, 1)
            self.pair[1].wait_recv()
            self.first = [forward, self.copy(self.sel(done, axis, 1, 1), axis, 3)]
            if k == 4:
                for by in (3, 1):
                    self.across.append(self.copy(self.sel(done, axis, by), "c", 1))
        elif k == 5:
            for c in self.first:
                c.wait_recv()
            self.across.append(self.copy(self.sel((a1, a2), a3, 2), "c", 1))
        elif k == 6:
            for c in self.across:
                c.wait_recv()
            for c in self.sent:
                c.wait_send()


N_GATHER = 15


def gather_groups(at, n_layers, mine, fetched, send, recv, local):
    groups = []
    index = 0
    for layer in range(n_layers):
        for group in CHAINS:
            chains = []
            for chain in group:
                array = chain[0]
                if array == 3 and layer > 0:
                    continue
                ref = fetched[3 * n_layers] if array == 3 else fetched[3 * layer + array]
                made = Gather(at, ref, chain, send.at[index], recv.at[index])
                made.place_own(mine[array] if array == 3 else mine[array].at[layer], local.at[index])
                chains.append(made)
                index += 1
            groups.append(chains)
    return groups


N_SCATTER = 12
PART_SHAPES = ((4, 2, 4, 16, 4096), (4, 2, 4, 16, 4096), (4, 2, 4, 64, 1024), (4, 2, 4, 16, 256))
OUT_SHAPES = ((16, 4096), (16, 4096), (64, 1024), (16, 256))
SCATTER_ORDER = (CHAINS[2], CHAINS[1], CHAINS[0])


def landing_shapes(chain):
    array, _, tiles, order = chain
    a1, a2, a3 = ORDERS[order]
    rows, cols = (64, tiles * TILE) if array == 2 else (16, tiles * TILE)
    unit = (rows // 2, cols) if array == 2 else (rows, cols // 2)

    def block(full, half=None):
        dims = []
        for axis in "xyz":
            if axis in full:
                size = 2 if axis == "y" else 4
                dims.append(size // 2 if axis == half else size)
        return tuple(dims) + ((rows, cols) if "y" in full else unit)

    return (
        (2,) + block((a1, a2), a1),
        (2,) + block((a1, a2)),
        (2,) + block((a1,), a1),
        (2,) + block((a1,)),
        (3,) + unit,
        unit,
    )


class Scatter:
    def __init__(self, at, part, out, landing, chain, send, recv):
        self.at, self.part, self.out, self.chain = at, part, out, chain
        self.landing, self.send, self.recv = landing, send, recv
        self.axes = ORDERS[chain[3]]
        self.count = 0
        self.sent = []

    def copy(self, src, dst, axis, by):
        slot = self.count
        self.count += 1
        made = pltpu.make_async_remote_copy(
            src_ref=src,
            dst_ref=dst,
            send_sem=self.send.at[slot],
            recv_sem=self.recv.at[slot],
            device_id=device(moved(self.at, axis, by)),
            device_id_type=MESH,
        )
        made.start()
        self.sent.append(made)
        return made

    def sel(self, done, axis=None, by=0, half=None):
        at = {k: self.at[k] for k in "xyz"}
        for d in done:
            at[d] = None
        if half is not None:
            at[done[0]] = half_of(done[0], half)
        if axis is not None:
            at[axis] = (self.at[axis] + by) % 4
        return pick(self.part, self.chain, at)

    def step(self, k):
        a1, a2, a3 = self.axes
        if k in (1, 3):
            done, axis = ((a1, a2), a3) if k == 1 else ((a1,), a2)
            land, blocks = self.landing[k - 1], self.landing[k]
            self.blocks = []
            for i, by in ((0, 1), (1, 3)):
                self.halves[i].wait_recv()
                add_to(self.sel(done, axis, by, i), (land.at[i],))
                self.blocks.append(self.copy(self.sel(done, axis, by), blocks.at[i], axis, by))
        if k in (2, 4):
            done = (a1, a2) if k == 2 else (a1,)
            blocks = self.landing[k - 1]
            for c in self.blocks:
                c.wait_recv()
            add_to(self.sel(done), (blocks.at[0], blocks.at[1]))
        if k in (0, 2):
            done, axis = ((a1, a2), a3) if k == 0 else ((a1,), a2)
            land = self.landing[0 if k == 0 else 2]
            self.halves = [
                self.copy(self.sel(done, axis, 2, 0), land.at[0], axis, 1),
                self.copy(self.sel(done, axis, 2, 1), land.at[1], axis, 3),
            ]
        if k == 4:
            land = self.landing[4]
            self.units = [self.copy(self.sel((), a1, by), land.at[i], a1, by) for i, by in enumerate((1, 3, 2))]
        if k == 5:
            land = self.landing[4]
            for c in self.units:
                c.wait_recv()
            add_to(self.sel(()), (land.at[0], land.at[1], land.at[2]))
            self.last = self.copy(self.sel(()), self.landing[5], "y", 2)
        if k == 6:
            self.last.wait_recv()
            array, tile, tiles, _ = self.chain
            high = self.at["y"] // 2
            for side, ref in ((high, self.sel(())), (1 - high, self.landing[5])):
                if array == 2:
                    where = (pl.ds(pl.multiple_of(side * 32, 32), 32), pl.ds(tile * TILE, tiles * TILE))
                else:
                    wide = tiles // 2 * TILE
                    where = (slice(None), pl.ds(pl.multiple_of(tile * TILE + side * wide, TILE), wide))
                self.out[where] = ref[...].astype(F32)
            for c in self.sent:
                c.wait_send()


def add_to(ref, terms):
    lead = ref.shape[:-2]
    if not lead:
        total = ref[...]
        for t in terms:
            total = total + t[...]
        ref[...] = total
        return
    n = 1
    for d in lead:
        n *= d

    def body(i, _):
        index = []
        rest = i
        for d in reversed(lead):
            index.append(rest % d)
            rest = rest // d
        index = tuple(reversed(index))
        total = ref[index]
        for t in terms:
            total = total + t[index]
        ref[index] = total
        return 0

    lax.fori_loop(0, n, body, 0)


def scatter_kernel(gqkv, go, gup, gdown, gsmall, *rest):
    outs, rest = rest[:4], rest[4:]
    parts, lands, rest = rest[:4], rest[4:8], rest[8:]
    landings, (send, recv, local, across_s, across_r) = rest[:-5], rest[-5:]
    at = place()
    c = at["c"]
    greet(at, PEERS)
    partner = device(moved(at, "c", 1))

    def half(ref, core):
        return ref.at[:, :, :, core]

    loads = {}
    for array, src, cols in (
        (2, gdown, None),
        (1, gup, None),
        (0, gqkv, (0, 3072)),
        (0, go, (3072, 1024)),
        (3, gsmall, None),
    ):
        i = len(loads)
        window = (lambda r: r) if cols is None else (lambda r, w=cols: r.at[:, :, :, :, pl.ds(w[0], w[1])])
        own = pltpu.make_async_copy(half(src, c), window(parts[array]), local.at[i])
        other = pltpu.make_async_remote_copy(
            src_ref=half(src, 1 - c),
            dst_ref=window(lands[array]),
            send_sem=across_s.at[i],
            recv_sem=across_r.at[i],
            device_id=partner,
            device_id_type=MESH,
        )
        own.start()
        other.start()
        loads[i] = (own, other)
    needs = {2: (0,), 1: (1,), 0: (2, 3), 3: (4,)}
    groups = []
    index = 0
    for group in SCATTER_ORDER:
        chains = []
        for chain in group:
            land = landings[6 * index : 6 * index + 6]
            chains.append(Scatter(at, parts[chain[0]], outs[chain[0]], land, chain, send.at[index], recv.at[index]))
            index += 1
        groups.append(chains)

    def enter(chains):
        for array in sorted({chain.chain[0] for chain in chains}):
            for i in needs[array]:
                loads[i][0].wait()
                loads[i][1].wait_recv()
            add_to(parts[array], (lands[array],))

    for slot in range(8 + len(groups) - 1):
        for g, chains in enumerate(groups):
            k = slot - g
            if k == 0:
                enter(chains)
            elif 0 < k < 8:
                for chain in chains:
                    chain.step(k - 1)
    for i in loads:
        loads[i][1].wait_send()


def scatter(gqkv, go, gup, gdown, gsmall):
    lead = (4, 2, 4, 2)
    args = (
        gqkv.reshape(lead + (16, 3072)),
        go.reshape(lead + (16, 1024)),
        gup.reshape(lead + (16, 4096)),
        gdown.reshape(lead + (64, 1024)),
        gsmall.reshape(lead + (16, 256)),
    )
    chains = [c for g in SCATTER_ORDER for c in g]
    scratch = [pltpu.VMEM(s, BF) for s in PART_SHAPES] * 2
    for chain in chains:
        scratch += [pltpu.VMEM(s, BF) for s in landing_shapes(chain)]
    scratch += [pltpu.SemaphoreType.DMA((len(chains), N_SCATTER))] * 2
    scratch += [pltpu.SemaphoreType.DMA((5,))] * 3
    return pl.pallas_call(
        scatter_kernel,
        out_shape=[jax.ShapeDtypeStruct(s, F32) for s in OUT_SHAPES],
        in_specs=[pl.BlockSpec(memory_space=pl.ANY)] * 5,
        out_specs=[pl.BlockSpec(memory_space=pltpu.VMEM)] * 4,
        scratch_shapes=scratch,
        compiler_params=pltpu.CompilerParams(collective_id=1, has_side_effects=True, vmem_limit_bytes=56 << 20),
        name="scatter_grads",
    )(*args)


LANES = 128
GELU = 0.7978845608028654
EPSILON = 1e-05
ROWS = 256
WIDTH = 1024
HIDDEN = 4096
HEADS = 16
HEAD = 64
BUCKETS = 32
MASKED = -1e30


def dot(a, b, ca=1, cb=0):
    return lax.dot_general(a, b, (((ca,), (cb,)), ((), ())), preferred_element_type=F32)


def iota(shape, dim):
    return lax.broadcasted_iota(jnp.int32, shape, dim)


def param_rows(small, layer):
    flat = small[...].reshape(1024, 256)[:, :128]
    chosen = (iota((64, 1024), 1) == iota((64, 1024), 0) * 16 + layer).astype(BF)
    shares = dot(chosen, flat).astype(BF)
    owner = iota((64, 1024), 0) == iota((64, 1024), 1) // 16
    rows = []
    for k in range(4):
        spread = (iota((128, 1024), 0) == 16 * k + iota((128, 1024), 1) % 16).astype(BF)
        rows.append(jnp.sum(jnp.where(owner, dot(shares, spread), 0.0), 0, keepdims=True))
    return rows, shares


def bias_rows(shares, bucket_rows):
    picked = (iota((16, 128), 1) == 64 + iota((16, 128), 0) % 8).astype(BF)
    entries = dot(picked, shares, 1, 1)
    entries = jnp.where(iota((16, 64), 1) % 2 == iota((16, 64), 0) // 8, entries, 0.0).astype(BF)
    return dot(entries, bucket_rows)


def norm_parts(rows):
    center = jnp.mean(rows, -1, keepdims=True)
    centered = rows - center
    inverse = lax.rsqrt(jnp.mean(centered * centered, -1, keepdims=True) + EPSILON)
    return centered * inverse, inverse


def norm_into(dst, src, gain, shift):
    def body(i, _):
        at = pl.ds(pl.multiple_of(i * 64, 64), 64)
        normed, _unused = norm_parts(src[at, :])
        dst[at, :] = (normed * gain[...] + shift[...]).astype(BF)
        return 0

    lax.fori_loop(0, ROWS // 64, body, 0)


def attention_forward(qkv, probs, mixed, bias, allowed):
    scale = HEAD ** (-0.5)
    low = iota((ROWS, LANES), 1) < HEAD

    def pair(i, _):
        def columns(k):
            return pl.ds(pl.multiple_of(k * WIDTH + i * LANES, LANES), LANES)

        q, k, v = (qkv[:, columns(j)] for j in range(3))
        halves = []
        for side in range(2):
            head = 2 * i + side
            mine = jnp.where(low == (side == 0), q, jnp.zeros_like(q))
            scores = dot(mine, k, 1, 1) * scale
            first = bias[head]
            shifted = jnp.concatenate([first] + [pltpu.roll(first, 16 * b, 1) for b in range(1, 16)], 0)
            scores = jnp.where(allowed[...] > 0, scores + shifted, MASKED)
            peak = jnp.max(scores, -1, keepdims=True)
            terms = jnp.exp(scores - peak)
            rounded = (terms / jnp.sum(terms, -1, keepdims=True)).astype(BF)
            probs[head] = rounded
            halves.append(dot(rounded, v))
        mixed[:, pl.ds(pl.multiple_of(i * LANES, LANES), LANES)] = jnp.where(low, halves[0], halves[1]).astype(BF)
        return 0

    lax.fori_loop(0, HEADS // 2, pair, 0)


def forward_kernel(att, up, down, small, tokens, seg_col, seg_row, bucket_rows, *rest):
    outs, rest = rest[:16], rest[16:]
    fetched = outs[:7]
    o_acts, o_mid0, o_mid1, o_next, o_qkv, o_probs, o_mixed, o_active, o_slope = outs[7:]
    (w_att, w_up, w_down, w_small, stream, middle, hidden, qkv, probs, mixed, active, slope, rounded,
     bias, allowed, params, send, recv, local, loads, stores) = rest
    at = place()
    greet(at, PEERS)
    groups = gather_groups(at, 2, (att, up, down, small), fetched, send, recv, local)
    stored = []

    def store(src, dst):
        made = pltpu.make_async_copy(src, dst, stores.at[len(stored)])
        made.start()
        stored.append(made)

    def load(i, src, dst):
        made = pltpu.make_async_copy(src, dst, loads.at[i])
        made.start()
        return made

    def slot(n):
        for g, chains in reversed(list(enumerate(groups))):
            k = n - g
            if 0 <= k < 7:
                for chain in chains:
                    chain.step(k)

    same = (seg_col[...] == seg_row[...]) & (iota((ROWS, ROWS), 0) >= iota((ROWS, ROWS), 1))
    allowed[...] = same.astype(F32)
    stream[0] = tokens[...].astype(F32)
    for n in range(7):
        slot(n)
    load(0, fetched[6], w_small).wait()
    for layer in range(2):
        load(1, fetched[3 * layer], w_att).wait()
        rows, shares = param_rows(w_small, layer)
        for k in range(4):
            params[layer, pl.ds(k, 1), :] = rows[k]
        by_offset = bias_rows(shares, bucket_rows[...])
        for head in range(HEADS):
            wide = jnp.broadcast_to(by_offset[head : head + 1], (16, ROWS))
            bias[head] = pltpu.roll(wide, 0, 1, stride=1, stride_axis=0)
        here, mid = stream.at[layer], middle.at[layer]
        row = lambda k: params.at[layer, pl.ds(k, 1), :]
        norm_into(hidden, here, row(0), row(1))
        wide_qkv, wide_probs, wide_mixed = qkv.at[layer], probs.at[layer], mixed.at[layer]
        wide_active, wide_slope = active.at[layer], slope.at[layer]

        def project(i, _):
            cols = pl.ds(pl.multiple_of(i * 512, 512), 512)
            weights = w_att[:, :, :, :, :, cols].reshape(WIDTH, 512)
            wide_qkv[:, cols] = dot(hidden[...], weights).astype(BF)
            return 0

        lax.fori_loop(0, 6, project, 0)
        attention_forward(wide_qkv, wide_probs, wide_mixed, bias, allowed)

        def out_project(i, _):
            cols = pl.ds(pl.multiple_of(i * 512, 512), 512)
            from_cols = pl.ds(pl.multiple_of(3072 + i * 512, 512), 512)
            weights = w_att[:, :, :, :, :, from_cols].reshape(WIDTH, 512)
            mid[:, cols] = here[:, cols] + dot(wide_mixed[...], weights)
            return 0

        lax.fori_loop(0, 2, out_project, 0)
        norm_into(hidden, mid, row(2), row(3))
        store(wide_qkv, o_qkv.at[layer])
        store(wide_probs, o_probs.at[layer])
        store(wide_mixed, o_mixed.at[layer])
        store(mid, (o_mid0, o_mid1)[layer])
        slot(7 + 3 * layer)
        load(2, fetched[3 * layer + 1], w_up).wait()

        def expand(i, _):
            cols = pl.ds(pl.multiple_of(i * 512, 512), 512)
            weights = w_up[:, :, :, :, :, cols].reshape(WIDTH, 512)
            u = dot(hidden[...], weights)
            square = u * u
            tangent = jnp.tanh(GELU * (u + 0.044715 * square * u))
            wide_active[:, cols] = (0.5 * u * (1.0 + tangent)).astype(BF)
            wide_slope[:, cols] = (
                0.5 * (1.0 + tangent)
                + 0.5 * u * (1.0 - tangent * tangent) * GELU * (1.0 + 3.0 * 0.044715 * square)
            ).astype(BF)
            return 0

        lax.fori_loop(0, 8, expand, 0)
        store(wide_active, o_active.at[layer])
        store(wide_slope, o_slope.at[layer])
        slot(8 + 3 * layer)
        load(3, fetched[3 * layer + 2], w_down).wait()
        acts = rounded.at[layer]

        def contract(i, _):
            cols = pl.ds(pl.multiple_of(i * 256, 256), 256)
            weights = w_down[:, :, :, :, :, cols].reshape(HIDDEN, 256)
            result = mid[:, cols] + dot(wide_active[...], weights)
            if layer == 0:
                stream[1, :, cols] = result
            acts[:, cols] = result.astype(BF)
            return 0

        lax.fori_loop(0, 4, contract, 0)
        store(acts, o_acts.at[layer])
        if layer == 0:
            store(stream.at[1], o_next)
            slot(9)
    for made in stored:
        made.wait()


def forward(att, up, down, small, tokens, seg_ids, bucket_rows):
    lead = (4, 2, 4, 2)
    gathered = [lead + (16, 4096), lead + (16, 4096), lead + (64, 1024)] * 2 + [lead + (16, 256)]
    saved = [
        ((2, ROWS, WIDTH), BF),
        ((ROWS, WIDTH), F32),
        ((ROWS, WIDTH), F32),
        ((ROWS, WIDTH), F32),
        ((2, ROWS, 3 * WIDTH), BF),
        ((2, HEADS, ROWS, ROWS), BF),
        ((2, ROWS, WIDTH), BF),
        ((2, ROWS, HIDDEN), BF),
        ((2, ROWS, HIDDEN), BF),
    ]
    vmem = pl.BlockSpec(memory_space=pltpu.VMEM)
    hbm = pl.BlockSpec(memory_space=pl.ANY)
    return pl.pallas_call(
        forward_kernel,
        out_shape=[jax.ShapeDtypeStruct(s, BF) for s in gathered] + [jax.ShapeDtypeStruct(s, t) for s, t in saved],
        in_specs=[vmem] * 8,
        out_specs=[hbm] * 16,
        scratch_shapes=[
            pltpu.VMEM(gathered[0], BF),
            pltpu.VMEM(gathered[1], BF),
            pltpu.VMEM(gathered[2], BF),
            pltpu.VMEM(gathered[6], BF),
            pltpu.VMEM((2, ROWS, WIDTH), F32),
            pltpu.VMEM((2, ROWS, WIDTH), F32),
            pltpu.VMEM((ROWS, WIDTH), BF),
            pltpu.VMEM((2, ROWS, 3 * WIDTH), BF),
            pltpu.VMEM((2, HEADS, ROWS, ROWS), BF),
            pltpu.VMEM((2, ROWS, WIDTH), BF),
            pltpu.VMEM((2, ROWS, HIDDEN), BF),
            pltpu.VMEM((2, ROWS, HIDDEN), BF),
            pltpu.VMEM((2, ROWS, WIDTH), BF),
            pltpu.VMEM((HEADS, 16, ROWS), F32),
            pltpu.VMEM((ROWS, ROWS), F32),
            pltpu.VMEM((2, 8, WIDTH), F32),
            pltpu.SemaphoreType.DMA((19, N_GATHER)),
            pltpu.SemaphoreType.DMA((19, N_GATHER)),
            pltpu.SemaphoreType.DMA((19,)),
            pltpu.SemaphoreType.DMA((4,)),
            pltpu.SemaphoreType.DMA((16,)),
        ],
        compiler_params=pltpu.CompilerParams(
            collective_id=0, has_side_effects=True, vmem_limit_bytes=58 << 20
        ),
        name="gather_forward",
    )(att, up, down, small, tokens, seg_ids[:, None], seg_ids[None, :], bucket_rows)


def on_device(
    tokens,
    seg_ids,
    buckets,
    cotangent,
    ln1_gain,
    ln1_bias,
    w_query,
    w_key,
    w_value,
    w_out,
    rel_table,
    ln2_gain,
    ln2_bias,
    w_up,
    w_down,
):
    length, width = ROWS, WIDTH
    score_scale = HEAD ** (-0.5)
    positions = jnp.arange(length, dtype=jnp.int32)
    distance = jnp.maximum(positions[:, None] - positions[None, :], 0)
    at_distance = (distance[:, :, None] == positions[None, None, :]).astype(jnp.bfloat16)
    bucket_of = (buckets[:, None] == jnp.arange(BUCKETS, dtype=jnp.int32)[None, :]).astype(jnp.bfloat16)
    onehot = jnp.dot(at_distance, bucket_of, preferred_element_type=jnp.float32).astype(jnp.bfloat16)

    small = jnp.stack(
        [
            jnp.concatenate([ln1_gain[i], ln1_bias[i], ln2_gain[i], ln2_bias[i], rel_table[i]])
            for i in range(2)
        ]
    )
    small = jnp.pad(small, ((0, 14), (0, 56)))
    by_offset = jnp.concatenate([buckets[:1], buckets[:0:-1]])
    bucket_rows = (by_offset[None, :] == (jnp.arange(64, dtype=jnp.int32) // 2)[:, None]).astype(BF)
    done = forward(
        jnp.concatenate([w_query, w_key, w_value, w_out], 2),
        w_up,
        w_down,
        jnp.concatenate([small, small], 1),
        tokens,
        seg_ids,
        bucket_rows,
    )
    fetched = done[:7]
    acts, mid0, mid1, stream1, qkv_all, probs_all, mixed_all, active_all, slope_all = done[7:]
    middles = (mid0, mid1)
    streams = (tokens.astype(F32), stream1)
    small_all = fetched[6].reshape(64, 16, 256)[:, :2, :128]

    def heads_of(value):
        return value.reshape(length, HEADS, HEAD)

    def layer_backward(grad_result, layer_at):
        att = fetched[3 * layer_at].reshape(1024, 4096)
        up_w = fetched[3 * layer_at + 1].reshape(1024, 4096)
        down_w = fetched[3 * layer_at + 2].reshape(4096, 1024)
        mine = small_all[:, layer_at]
        gain_one, shift_one, gain_two, shift_two = (mine[:, 16 * i : 16 * i + 16].reshape(1024) for i in range(4))
        out_w = att[:, 3072:]
        normed_one, inverse_one, hidden_one = normalize(streams[layer_at], gain_one, shift_one)
        normed_two, inverse_two, hidden_two = normalize(middles[layer_at], gain_two, shift_two)
        input_one, input_two = hidden_one.astype(BF), hidden_two.astype(BF)
        queries, key_rows, values = (heads_of(qkv_all[layer_at][:, i * width : (i + 1) * width]) for i in range(3))
        prob_rows = probs_all[layer_at]
        mixed, activated, slope = mixed_all[layer_at], active_all[layer_at], slope_all[layer_at]
        down_in = grad_result.astype(jnp.bfloat16)
        grad_down = jnp.einsum("lf,ld->fd", activated, down_in, preferred_element_type=jnp.float32)
        grad_active = jnp.einsum("ld,fd->lf", down_in, down_w, preferred_element_type=jnp.float32)
        grad_upward = (grad_active * slope.astype(F32)).astype(jnp.bfloat16)
        grad_up = jnp.einsum(
            "ld,lf->df", input_two, grad_upward, preferred_element_type=jnp.float32
        )
        grad_hidden_two = jnp.einsum(
            "lf,df->ld", grad_upward, up_w, preferred_element_type=jnp.float32
        )
        grad_gain_two = jnp.sum(grad_hidden_two * normed_two, 0)
        grad_shift_two = jnp.sum(grad_hidden_two, 0)
        grad_middle = grad_result + norm_back(grad_hidden_two, normed_two, inverse_two, gain_two)
        branch_in = grad_middle.astype(jnp.bfloat16)
        grad_out_w = jnp.einsum("ld,le->de", mixed, branch_in, preferred_element_type=jnp.float32)
        grad_mixed = jnp.einsum("le,de->ld", branch_in, out_w, preferred_element_type=jnp.float32)
        grad_mixed = grad_mixed.astype(jnp.bfloat16).reshape(length, HEADS, HEAD)
        grad_probs = jnp.einsum(
            "ihe,jhe->hij", grad_mixed, values, preferred_element_type=jnp.float32
        )
        grad_values = jnp.einsum(
            "hij,ihe->jhe",
            prob_rows.astype(jnp.bfloat16),
            grad_mixed,
            preferred_element_type=jnp.float32,
        )
        grad_values = grad_values.astype(jnp.bfloat16).reshape(length, width)
        grad_scores = (
            prob_rows.astype(F32) * (grad_probs - jnp.sum(prob_rows.astype(F32) * grad_probs, -1, keepdims=True))
        ).astype(jnp.bfloat16)
        grad_queries = (
            (
                jnp.einsum(
                    "hij,jhe->ihe", grad_scores, key_rows, preferred_element_type=jnp.float32
                )
                * score_scale
            )
            .astype(jnp.bfloat16)
            .reshape(length, width)
        )
        grad_keys = (
            (
                jnp.einsum("hij,ihe->jhe", grad_scores, queries, preferred_element_type=jnp.float32)
                * score_scale
            )
            .astype(jnp.bfloat16)
            .reshape(length, width)
        )
        grad_bias_table = jnp.einsum(
            "hij,ijb->bh", grad_scores, onehot, preferred_element_type=jnp.float32
        ).reshape(BUCKETS * HEADS)
        grad_all = jnp.concatenate([grad_queries, grad_keys, grad_values], 1)
        grad_qkv = jnp.einsum("ld,le->de", input_one, grad_all, preferred_element_type=jnp.float32)
        grad_hidden_one = jnp.einsum("le,de->ld", grad_all, att[:, :3072], preferred_element_type=jnp.float32)
        grad_gain_one = jnp.sum(grad_hidden_one * normed_one, 0)
        grad_shift_one = jnp.sum(grad_hidden_one, 0)
        grad_stream = grad_middle + norm_back(grad_hidden_one, normed_one, inverse_one, gain_one)
        small = jnp.concatenate(
            [
                grad_gain_one.reshape(64, 16),
                grad_shift_one.reshape(64, 16),
                grad_gain_two.reshape(64, 16),
                grad_shift_two.reshape(64, 16),
                grad_bias_table.reshape(64, 8),
            ],
            1,
        )
        small = jnp.pad(small[:, None], ((0, 0), (0, 15), (0, 56)))
        small = jnp.concatenate([small, small], 2)
        grads = tuple(g.astype(BF) for g in (grad_qkv, grad_out_w, grad_up, grad_down, small))
        return (grad_stream, grads)

    grad_stream = cotangent.astype(jnp.float32)
    reduced = [None, None]
    for layer_at in (1, 0):
        grad_stream, grads = layer_backward(grad_stream, layer_at)
        reduced[layer_at] = scatter(*grads)
    stacked = [jnp.stack([reduced[0][i], reduced[1][i]]) for i in range(4)]
    att, up, down, small = stacked
    return (
        acts,
        grad_stream,
        small[:, 0, 0:16],
        small[:, 0, 16:32],
        att[:, :, :1024],
        att[:, :, 1024:2048],
        att[:, :, 2048:3072],
        att[:, :, 3072:],
        small[:, 0, 64:72],
        small[:, 0, 32:48],
        small[:, 0, 48:64],
        up,
        down,
    )


def solution(mesh):
    placed = (
        P(("wide", "narrow"), None),
        P(("wide", "narrow")),
        P(),
        P(("wide", "narrow"), None),
        P(None, "wide"),
        P(None, "wide"),
        P(None, "wide", None),
        P(None, "wide", None),
        P(None, "wide", None),
        P(None, "wide", None),
        P(None, "wide"),
        P(None, "wide"),
        P(None, "wide"),
        P(None, "wide", None),
        P(None, "wide", None),
    )
    return jax.shard_map(
        on_device,
        mesh=mesh,
        in_specs=placed,
        out_specs=(
            P(None, ("wide", "narrow"), None),
            P(("wide", "narrow"), None),
            P(None, "wide"),
            P(None, "wide"),
            P(None, "wide", None),
            P(None, "wide", None),
            P(None, "wide", None),
            P(None, "wide", None),
            P(None, "wide"),
            P(None, "wide"),
            P(None, "wide"),
            P(None, "wide", None),
            P(None, "wide", None),
        ),
        check_vma=False,
    )
```

```python
import jax
import jax.numpy as jnp
from jax import lax
from jax.experimental import pallas as pl
from jax.experimental.pallas import tpu as pltpu
from jax.sharding import PartitionSpec as P

MESH = pl.DeviceIdType.MESH
TILE = 128
BF = jnp.bfloat16
F32 = jnp.float32
ORDERS = (("y", "x", "z"), ("z", "y", "x"), ("x", "z", "y"))
CHAINS = (
    ((0, 0, 10, 0), (0, 10, 10, 1), (0, 20, 12, 2), (3, 0, 2, 0)),
    ((1, 0, 10, 0), (1, 10, 10, 1), (1, 20, 12, 2)),
    ((2, 0, 3, 0), (2, 3, 3, 1), (2, 6, 2, 2)),
)


def place():
    wide, narrow = lax.axis_index("wide"), lax.axis_index("narrow")
    return {
        "x": wide // 16,
        "y": narrow * 2 + (wide // 8) % 2,
        "z": (wide // 2) % 4,
        "c": wide % 2,
    }


def device(at):
    return (((at["x"] * 2 + at["y"] % 2) * 4 + at["z"]) * 2 + at["c"], at["y"] // 2)


def moved(at, axis, by):
    new = dict(at)
    new[axis] = (at[axis] + by) % (2 if axis == "c" else 4)
    return new


def pick(ref, chain, sel, lead=()):
    array, tile, tiles, _ = chain
    y = sel["y"]
    columns = pl.ds(tile * TILE, tiles * TILE)
    rows = pl.ds(0, 64 if array == 2 else 16)
    if y is None:
        low = pl.ds(0, 2)
    elif isinstance(y, tuple):
        low = pl.ds(y[0], 1)
    else:
        low = y % 2
        if array == 2:
            rows = pl.ds(pl.multiple_of((y // 2) * 32, 32), 32)
        else:
            half = tiles // 2 * TILE
            columns = pl.ds(pl.multiple_of(tile * TILE + (y // 2) * half, TILE), half)

    def one(v):
        return pl.ds(0, 4) if v is None else v

    index = lead + (one(sel["x"]), low, one(sel["z"]))
    if "c" in sel:
        index = index + (sel["c"],)
    return ref.at[index + (rows, columns)]


def half_of(axis, part):
    return (part,) if axis == "y" else pl.ds(2 * part, 2)


def greet(at, peers):
    barrier = pltpu.get_barrier_semaphore()
    for axis, by in peers:
        pl.semaphore_signal(barrier, inc=1, device_id=device(moved(at, axis, by)), device_id_type=MESH)
    pl.semaphore_wait(barrier, len(peers))


PEERS = tuple((a, b) for a in "xyz" for b in (1, 3, 2)) + (("c", 1),)


class Gather:
    def __init__(self, at, ref, chain, send, recv):
        self.at, self.ref, self.chain, self.send, self.recv = at, ref, chain, send, recv
        self.axes = ORDERS[chain[3]]
        self.count = 0
        self.sent = []

    def place_own(self, mine, sem):
        array, tile, tiles, _ = self.chain
        side = self.at["y"] // 2
        if array == 2:
            where = (pl.ds(pl.multiple_of(side * 32, 32), 32), pl.ds(tile * TILE, tiles * TILE))
        else:
            wide = tiles // 2 * TILE
            where = (slice(None), pl.ds(pl.multiple_of(tile * TILE + side * wide, TILE), wide))
        self.own = pltpu.make_async_copy(mine.at[where], pick(self.ref, self.chain, self.sel(())), sem)
        self.own.start()

    def copy(self, sel, axis, by):
        slot = self.count
        self.count += 1
        block = pick(self.ref, self.chain, sel)
        made = pltpu.make_async_remote_copy(
            src_ref=block,
            dst_ref=block,
            send_sem=self.send.at[slot],
            recv_sem=self.recv.at[slot],
            device_id=device(moved(self.at, axis, by)),
            device_id_type=MESH,
        )
        made.start()
        self.sent.append(made)
        return made

    def sel(self, done, axis=None, by=0, half=None):
        at = {k: self.at[k] for k in "xyzc"}
        for d in done:
            at[d] = None
        if half is not None:
            at[done[0]] = half_of(done[0], half)
        if axis is not None:
            at[axis] = (self.at[axis] + by) % 4
        return at

    def step(self, k):
        a1, a2, a3 = self.axes
        if k == 0:
            self.own.wait()
            own = self.sel(())
            self.first = [self.copy(own, a1, by) for by in (1, 3, 2)]
        elif k in (1, 3):
            done, axis = ((a1,), a2) if k == 1 else ((a1, a2), a3)
            for c in self.first:
                c.wait_recv()
            own = self.sel(done)
            self.pair = [self.copy(own, axis, 1), self.copy(own, axis, 3)]
            if k == 3:
                self.across = [self.copy(own, "c", 1)]
        elif k in (2, 4):
            done, axis = ((a1,), a2) if k == 2 else ((a1, a2), a3)
            self.pair[0].wait_recv()
            forward = self.copy(self.sel(done, axis, 3, 0), axis, 1)
            self.pair[1].wait_recv()
            self.first = [forward, self.copy(self.sel(done, axis, 1, 1), axis, 3)]
            if k == 4:
                for by in (3, 1):
                    self.across.append(self.copy(self.sel(done, axis, by), "c", 1))
        elif k == 5:
            for c in self.first:
                c.wait_recv()
            self.across.append(self.copy(self.sel((a1, a2), a3, 2), "c", 1))
        elif k == 6:
            for c in self.across:
                c.wait_recv()
            for c in self.sent:
                c.wait_send()


N_GATHER = 15


def gather_groups(at, n_layers, mine, fetched, send, recv, local):
    groups = []
    index = 0
    for layer in range(n_layers):
        for group in CHAINS:
            chains = []
            for chain in group:
                array = chain[0]
                if array == 3 and layer > 0:
                    continue
                ref = fetched[3 * n_layers] if array == 3 else fetched[3 * layer + array]
                made = Gather(at, ref, chain, send.at[index], recv.at[index])
                made.place_own(mine[array] if array == 3 else mine[array].at[layer], local.at[index])
                chains.append(made)
                index += 1
            groups.append(chains)
    return groups


N_SCATTER = 12
PART_SHAPES = ((4, 2, 4, 16, 4096), (4, 2, 4, 16, 4096), (4, 2, 4, 64, 1024), (4, 2, 4, 16, 256))


def landing_shapes(chain):
    array, _, tiles, order = chain
    a1, a2, a3 = ORDERS[order]
    rows, cols = (64, tiles * TILE) if array == 2 else (16, tiles * TILE)
    unit = (rows // 2, cols) if array == 2 else (rows, cols // 2)

    def block(full, half=None):
        dims = []
        for axis in "xyz":
            if axis in full:
                size = 2 if axis == "y" else 4
                dims.append(size // 2 if axis == half else size)
        return tuple(dims) + ((rows, cols) if "y" in full else unit)

    return (
        (2,) + block((a1, a2), a1),
        (2,) + block((a1, a2)),
        (2,) + block((a1,), a1),
        (2,) + block((a1,)),
        (3,) + unit,
        unit,
    )


class Scatter:
    def __init__(self, at, part, out, landing, chain, send, recv):
        self.at, self.part, self.out, self.chain = at, part, out, chain
        self.landing, self.send, self.recv = landing, send, recv
        self.axes = ORDERS[chain[3]]
        self.count = 0
        self.sent = []

    def copy(self, src, dst, axis, by):
        slot = self.count
        self.count += 1
        made = pltpu.make_async_remote_copy(
            src_ref=src,
            dst_ref=dst,
            send_sem=self.send.at[slot],
            recv_sem=self.recv.at[slot],
            device_id=device(moved(self.at, axis, by)),
            device_id_type=MESH,
        )
        made.start()
        self.sent.append(made)
        return made

    def sel(self, done, axis=None, by=0, half=None):
        at = {k: self.at[k] for k in "xyz"}
        for d in done:
            at[d] = None
        if half is not None:
            at[done[0]] = half_of(done[0], half)
        if axis is not None:
            at[axis] = (self.at[axis] + by) % 4
        return pick(self.part, self.chain, at)

    def step(self, k):
        a1, a2, a3 = self.axes
        if k in (1, 3):
            done, axis = ((a1, a2), a3) if k == 1 else ((a1,), a2)
            land, blocks = self.landing[k - 1], self.landing[k]
            self.blocks = []
            for i, by in ((0, 1), (1, 3)):
                self.halves[i].wait_recv()
                add_to(self.sel(done, axis, by, i), (land.at[i],))
                self.blocks.append(self.copy(self.sel(done, axis, by), blocks.at[i], axis, by))
        if k in (2, 4):
            done = (a1, a2) if k == 2 else (a1,)
            blocks = self.landing[k - 1]
            for c in self.blocks:
                c.wait_recv()
            add_to(self.sel(done), (blocks.at[0], blocks.at[1]))
        if k in (0, 2):
            done, axis = ((a1, a2), a3) if k == 0 else ((a1,), a2)
            land = self.landing[0 if k == 0 else 2]
            self.halves = [
                self.copy(self.sel(done, axis, 2, 0), land.at[0], axis, 1),
                self.copy(self.sel(done, axis, 2, 1), land.at[1], axis, 3),
            ]
        if k == 4:
            land = self.landing[4]
            self.units = [self.copy(self.sel((), a1, by), land.at[i], a1, by) for i, by in enumerate((1, 3, 2))]
        if k == 5:
            land = self.landing[4]
            for c in self.units:
                c.wait_recv()
            add_to(self.sel(()), (land.at[0], land.at[1], land.at[2]))
            self.last = self.copy(self.sel(()), self.landing[5], "y", 2)
        if k == 6:
            self.last.wait_recv()
            array, tile, tiles, _ = self.chain
            high = self.at["y"] // 2
            for side, ref in ((high, self.sel(())), (1 - high, self.landing[5])):
                if array == 2:
                    where = (pl.ds(pl.multiple_of(side * 32, 32), 32), pl.ds(tile * TILE, tiles * TILE))
                else:
                    wide = tiles // 2 * TILE
                    where = (slice(None), pl.ds(pl.multiple_of(tile * TILE + side * wide, TILE), wide))
                self.out[where] = ref[...].astype(F32)
            for c in self.sent:
                c.wait_send()


def add_to(ref, terms):
    lead = ref.shape[:-2]
    if not lead:
        total = ref[...]
        for t in terms:
            total = total + t[...]
        ref[...] = total
        return
    n = 1
    for d in lead:
        n *= d

    def body(i, _):
        index = []
        rest = i
        for d in reversed(lead):
            index.append(rest % d)
            rest = rest // d
        index = tuple(reversed(index))
        total = ref[index]
        for t in terms:
            total = total + t[index]
        ref[index] = total
        return 0

    lax.fori_loop(0, n, body, 0)


LANES = 128
GELU = 0.7978845608028654
EPSILON = 1e-05
ROWS = 256
WIDTH = 1024
HIDDEN = 4096
HEADS = 16
HEAD = 64
BUCKETS = 32
MASKED = -1e30


def dot(a, b, ca=1, cb=0):
    return lax.dot_general(a, b, (((ca,), (cb,)), ((), ())), preferred_element_type=F32)


def iota(shape, dim):
    return lax.broadcasted_iota(jnp.int32, shape, dim)


def param_rows(small, layer):
    flat = small[...].reshape(1024, 256)[:, :128]
    chosen = (iota((64, 1024), 1) == iota((64, 1024), 0) * 16 + layer).astype(BF)
    shares = dot(chosen, flat).astype(BF)
    owner = iota((64, 1024), 0) == iota((64, 1024), 1) // 16
    rows = []
    for k in range(4):
        spread = (iota((128, 1024), 0) == 16 * k + iota((128, 1024), 1) % 16).astype(BF)
        rows.append(jnp.sum(jnp.where(owner, dot(shares, spread), 0.0), 0, keepdims=True))
    return rows, shares


def bias_rows(shares, bucket_rows):
    picked = (iota((16, 128), 1) == 64 + iota((16, 128), 0) % 8).astype(BF)
    entries = dot(picked, shares, 1, 1)
    entries = jnp.where(iota((16, 64), 1) % 2 == iota((16, 64), 0) // 8, entries, 0.0).astype(BF)
    return dot(entries, bucket_rows)


def norm_parts(rows):
    center = jnp.mean(rows, -1, keepdims=True)
    centered = rows - center
    inverse = lax.rsqrt(jnp.mean(centered * centered, -1, keepdims=True) + EPSILON)
    return centered * inverse, inverse


def norm_into(dst, src, gain, shift):
    def body(i, _):
        at = pl.ds(pl.multiple_of(i * 64, 64), 64)
        normed, _unused = norm_parts(src[at, :])
        dst[at, :] = (normed * gain[...] + shift[...]).astype(BF)
        return 0

    lax.fori_loop(0, ROWS // 64, body, 0)


def attention_forward(qkv, probs, mixed, bias, allowed):
    scale = HEAD ** (-0.5)
    low = iota((ROWS, LANES), 1) < HEAD

    def pair(i, _):
        def columns(k):
            return pl.ds(pl.multiple_of(k * WIDTH + i * LANES, LANES), LANES)

        q, k, v = (qkv[:, columns(j)] for j in range(3))
        halves = []
        for side in range(2):
            head = 2 * i + side
            mine = jnp.where(low == (side == 0), q, jnp.zeros_like(q))
            scores = dot(mine, k, 1, 1) * scale
            first = bias[head]
            shifted = jnp.concatenate([first] + [pltpu.roll(first, 16 * b, 1) for b in range(1, 16)], 0)
            scores = jnp.where(allowed[...] > 0, scores + shifted, MASKED)
            peak = jnp.max(scores, -1, keepdims=True)
            terms = jnp.exp(scores - peak)
            rounded = (terms / jnp.sum(terms, -1, keepdims=True)).astype(BF)
            probs[head] = rounded
            halves.append(dot(rounded, v))
        mixed[:, pl.ds(pl.multiple_of(i * LANES, LANES), LANES)] = jnp.where(low, halves[0], halves[1]).astype(BF)
        return 0

    lax.fori_loop(0, HEADS // 2, pair, 0)


def forward_kernel(att, up, down, small, tokens, seg_col, seg_row, bucket_rows, *rest):
    outs, rest = rest[:17], rest[17:]
    fetched = outs[:7]
    o_acts, o_mid0, o_mid1, o_stream, o_params, o_qkv, o_probs, o_mixed, o_active, o_slope = outs[7:]
    (w_att, w_up, w_down, w_small, stream, middle, hidden, qkv, probs, mixed, active, slope, rounded,
     bias, allowed, params, send, recv, local, loads, stores) = rest
    at = place()
    greet(at, PEERS)
    groups = gather_groups(at, 2, (att, up, down, small), fetched, send, recv, local)
    stored = []

    def store(src, dst):
        made = pltpu.make_async_copy(src, dst, stores.at[len(stored)])
        made.start()
        stored.append(made)

    def load(i, src, dst):
        made = pltpu.make_async_copy(src, dst, loads.at[i])
        made.start()
        return made

    def slot(n):
        for g, chains in reversed(list(enumerate(groups))):
            k = n - g
            if 0 <= k < 7:
                for chain in chains:
                    chain.step(k)

    same = (seg_col[...] == seg_row[...]) & (iota((ROWS, ROWS), 0) >= iota((ROWS, ROWS), 1))
    allowed[...] = same.astype(F32)
    stream[0] = tokens[...].astype(F32)
    for n in range(7):
        slot(n)
    load(0, fetched[6], w_small).wait()
    for layer in range(2):
        load(1, fetched[3 * layer], w_att).wait()
        rows, shares = param_rows(w_small, layer)
        for k in range(4):
            params[layer, pl.ds(k, 1), :] = rows[k]
        by_offset = bias_rows(shares, bucket_rows[...])
        for head in range(HEADS):
            wide = jnp.broadcast_to(by_offset[head : head + 1], (16, ROWS))
            bias[head] = pltpu.roll(wide, 0, 1, stride=1, stride_axis=0)
        here, mid = stream.at[layer], middle.at[layer]
        row = lambda k: params.at[layer, pl.ds(k, 1), :]
        norm_into(hidden, here, row(0), row(1))
        wide_qkv, wide_probs, wide_mixed = qkv.at[layer], probs.at[layer], mixed.at[layer]
        wide_active, wide_slope = active.at[layer], slope.at[layer]

        def project(i, _):
            cols = pl.ds(pl.multiple_of(i * 512, 512), 512)
            weights = w_att[:, :, :, :, :, cols].reshape(WIDTH, 512)
            wide_qkv[:, cols] = dot(hidden[...], weights).astype(BF)
            return 0

        lax.fori_loop(0, 6, project, 0)
        attention_forward(wide_qkv, wide_probs, wide_mixed, bias, allowed)

        def out_project(i, _):
            cols = pl.ds(pl.multiple_of(i * 512, 512), 512)
            from_cols = pl.ds(pl.multiple_of(3072 + i * 512, 512), 512)
            weights = w_att[:, :, :, :, :, from_cols].reshape(WIDTH, 512)
            mid[:, cols] = here[:, cols] + dot(wide_mixed[...], weights)
            return 0

        lax.fori_loop(0, 2, out_project, 0)
        norm_into(hidden, mid, row(2), row(3))
        store(wide_qkv, o_qkv.at[layer])
        store(wide_probs, o_probs.at[layer])
        store(wide_mixed, o_mixed.at[layer])
        store(mid, (o_mid0, o_mid1)[layer])
        slot(7 + 3 * layer)
        load(2, fetched[3 * layer + 1], w_up).wait()

        def expand(i, _):
            cols = pl.ds(pl.multiple_of(i * 512, 512), 512)
            weights = w_up[:, :, :, :, :, cols].reshape(WIDTH, 512)
            u = dot(hidden[...], weights)
            square = u * u
            tangent = jnp.tanh(GELU * (u + 0.044715 * square * u))
            wide_active[:, cols] = (0.5 * u * (1.0 + tangent)).astype(BF)
            wide_slope[:, cols] = (
                0.5 * (1.0 + tangent)
                + 0.5 * u * (1.0 - tangent * tangent) * GELU * (1.0 + 3.0 * 0.044715 * square)
            ).astype(BF)
            return 0

        lax.fori_loop(0, 8, expand, 0)
        store(wide_active, o_active.at[layer])
        store(wide_slope, o_slope.at[layer])
        slot(8 + 3 * layer)
        load(3, fetched[3 * layer + 2], w_down).wait()
        acts = rounded.at[layer]

        def contract(i, _):
            cols = pl.ds(pl.multiple_of(i * 256, 256), 256)
            weights = w_down[:, :, :, :, :, cols].reshape(HIDDEN, 256)
            result = mid[:, cols] + dot(wide_active[...], weights)
            if layer == 0:
                stream[1, :, cols] = result
            acts[:, cols] = result.astype(BF)
            return 0

        lax.fori_loop(0, 4, contract, 0)
        store(acts, o_acts.at[layer])
        if layer == 0:
            slot(9)
    store(stream, o_stream)
    store(params, o_params)
    for made in stored:
        made.wait()


def forward(att, up, down, small, tokens, seg_ids, bucket_rows):
    lead = (4, 2, 4, 2)
    gathered = [lead + (16, 4096), lead + (16, 4096), lead + (64, 1024)] * 2 + [lead + (16, 256)]
    saved = [
        ((2, ROWS, WIDTH), BF),
        ((ROWS, WIDTH), F32),
        ((ROWS, WIDTH), F32),
        ((2, ROWS, WIDTH), F32),
        ((2, 8, WIDTH), F32),
        ((2, ROWS, 3 * WIDTH), BF),
        ((2, HEADS, ROWS, ROWS), BF),
        ((2, ROWS, WIDTH), BF),
        ((2, ROWS, HIDDEN), BF),
        ((2, ROWS, HIDDEN), BF),
    ]
    vmem = pl.BlockSpec(memory_space=pltpu.VMEM)
    hbm = pl.BlockSpec(memory_space=pl.ANY)
    return pl.pallas_call(
        forward_kernel,
        out_shape=[jax.ShapeDtypeStruct(s, BF) for s in gathered] + [jax.ShapeDtypeStruct(s, t) for s, t in saved],
        in_specs=[vmem] * 8,
        out_specs=[hbm] * 17,
        scratch_shapes=[
            pltpu.VMEM(gathered[0], BF),
            pltpu.VMEM(gathered[1], BF),
            pltpu.VMEM(gathered[2], BF),
            pltpu.VMEM(gathered[6], BF),
            pltpu.VMEM((2, ROWS, WIDTH), F32),
            pltpu.VMEM((2, ROWS, WIDTH), F32),
            pltpu.VMEM((ROWS, WIDTH), BF),
            pltpu.VMEM((2, ROWS, 3 * WIDTH), BF),
            pltpu.VMEM((2, HEADS, ROWS, ROWS), BF),
            pltpu.VMEM((2, ROWS, WIDTH), BF),
            pltpu.VMEM((2, ROWS, HIDDEN), BF),
            pltpu.VMEM((2, ROWS, HIDDEN), BF),
            pltpu.VMEM((2, ROWS, WIDTH), BF),
            pltpu.VMEM((HEADS, 16, ROWS), F32),
            pltpu.VMEM((ROWS, ROWS), F32),
            pltpu.VMEM((2, 8, WIDTH), F32),
            pltpu.SemaphoreType.DMA((19, N_GATHER)),
            pltpu.SemaphoreType.DMA((19, N_GATHER)),
            pltpu.SemaphoreType.DMA((19,)),
            pltpu.SemaphoreType.DMA((4,)),
            pltpu.SemaphoreType.DMA((16,)),
        ],
        compiler_params=pltpu.CompilerParams(
            collective_id=0, has_side_effects=True, vmem_limit_bytes=58 << 20
        ),
        name="gather_forward",
    )(att, up, down, small, tokens, seg_ids[:, None], seg_ids[None, :], bucket_rows)


def split_cores(value, core, shape):
    both = value.reshape(shape)
    axis = len(shape) - 3
    even, odd = (lax.index_in_dim(both, i, axis, keepdims=False) for i in range(2))
    mine = core == 0
    return jnp.where(mine, even, odd), jnp.where(mine, odd, even)


def norm_back_into(grad, dst, src, gain, sums, base):
    def body(i, carry):
        by_gain, by_shift = carry
        at = pl.ds(pl.multiple_of(i * 32, 32), 32)
        normed, inverse = norm_parts(src[at, :])
        value = grad[at, :]
        scaled = value * gain[...]
        dst[at, :] = dst[at, :] + inverse * (
            scaled
            - jnp.mean(scaled, -1, keepdims=True)
            - normed * jnp.mean(scaled * normed, -1, keepdims=True)
        )
        by_gain = by_gain + jnp.sum(value * normed, 0, keepdims=True)
        return by_gain, by_shift + jnp.sum(value, 0, keepdims=True)

    zero = jnp.zeros((1, WIDTH), F32)
    by_gain, by_shift = lax.fori_loop(0, ROWS // 32, body, (zero, zero))
    sums[pl.ds(base, 1), :] = by_gain
    sums[pl.ds(base + 1, 1), :] = by_shift


def attention_backward(qkv, probs, grad_mixed, first, last):
    scale = HEAD ** (-0.5)
    low = iota((ROWS, LANES), 1) < HEAD

    def pair(i, _):
        def columns(k):
            return pl.ds(pl.multiple_of(k * WIDTH + i * LANES, LANES), LANES)

        q, k, v = (qkv[:, columns(j)] for j in range(3))
        grad = grad_mixed[:, pl.ds(pl.multiple_of(i * LANES, LANES), LANES)]
        grads = []
        for side in range(2):
            head = 2 * i + side
            rounded = probs[head]
            prob = rounded.astype(F32)
            mine = jnp.where(low == (side == 0), grad, jnp.zeros_like(grad))
            grad_probs = dot(mine, v, 1, 1)
            inner = jnp.sum(prob * grad_probs, -1, keepdims=True)
            grad_scores = (prob * (grad_probs - inner)).astype(BF)
            probs[head] = grad_scores
            grads.append(
                (dot(grad_scores, k) * scale, dot(grad_scores, q, 0, 0) * scale, dot(rounded, grad, 0, 0))
            )
        for j in range(3):
            qkv[:, columns(j)] = jnp.where(low, grads[0][j], grads[1][j]).astype(BF)
        return 0

    lax.fori_loop(first, last, pair, 0)


def table_grads(grad_scores, bucket_rows):
    total = jnp.zeros((HEADS, 16, ROWS), F32)
    for b in range(15, -1, -1):
        if b < 15:
            total = pltpu.roll(total, ROWS - 16, 2)
        total = total + grad_scores[:, pl.ds(16 * b, 16), :].astype(F32)
    line = iota((HEADS, 16, ROWS), 1)
    for bit in (1, 2, 4, 8):
        total = jnp.where((line // bit) % 2 == 1, pltpu.roll(total, ROWS - bit, 2), total)
    by_offset = jnp.sum(total, 1)
    high = by_offset.astype(BF)
    rest = (by_offset - high.astype(F32)).astype(BF)
    return dot(high, bucket_rows, 1, 1) + dot(rest, bucket_rows, 1, 1)


def share_grads(sums, table):
    owner = iota((64, 1024), 0) == iota((64, 1024), 1) // 16
    shares = jnp.zeros((64, 128), F32)
    for k in range(4):
        spread = (iota((128, 1024), 0) == 16 * k + iota((128, 1024), 1) % 16).astype(BF)
        mine = jnp.where(owner, sums[pl.ds(k, 1), :], 0.0).astype(BF)
        shares = shares + dot(mine, spread, 1, 1)
    picked = (iota((16, 128), 1) == 64 + iota((16, 128), 0) % 8).astype(BF)
    entries = jnp.where(iota((16, 64), 1) % 2 == iota((16, 64), 0) // 8, table, 0.0).astype(BF)
    return shares + dot(entries, picked, 0, 0)


def backward_kernel(*refs):
    (cotangent, params, bucket_rows, att1, up1, down1, att0, up0, down0,
     h_stream, h_mid0, h_mid1, h_qkv, h_probs, h_mixed, h_active, h_slope) = refs[:17]
    o_input, o_att, o_up, o_down, o_small = refs[17:22]
    rest = refs[22:]
    parts, lands, rest = rest[:4], rest[4:7], rest[7:]
    landings, rest = rest[:60], rest[60:]
    (stage_down, stage_wide, stage_small, tiles_down, tiles_wide, active, slope, probs, qkv, mixed, grad_mixed,
     state, stream, hidden, grad_hidden, rounded, sums, small_total,
     send, recv, across_s, across_r, free, free_land, loads, tile_sems, out_sem) = rest
    weights = ((att0, up0, down0), (att1, up1, down1))
    middles = (h_mid0, h_mid1)
    at = place()
    core = at["c"]
    partner = device(moved(at, "c", 1))
    greet(at, PEERS)

    pending = {}

    def fetch(name, i, src, dst):
        made = pltpu.make_async_copy(src, dst, loads.at[i])
        made.start()
        pending[name] = made

    def ready(name):
        pending.pop(name).wait()

    def fetch_active(layer):
        fetch("active", 0, h_active.at[layer], active)

    def fetch_slope(layer):
        fetch("slope", 1, h_slope.at[layer], slope)

    def fetch_mid(layer):
        fetch("mid", 2, middles[layer], stream)

    def fetch_stream(layer):
        fetch("stream", 3, h_stream.at[layer], stream)

    def fetch_probs(layer):
        fetch("probs", 4, h_probs.at[layer], probs)

    def fetch_qkv(layer):
        fetch("qkv", 5, h_qkv.at[layer], qkv)

    def fetch_mixed(layer):
        fetch("mixed", 6, h_mixed.at[layer], mixed)

    def streamed(n, source, buffer, body):
        def tile(i, slot):
            return pltpu.make_async_copy(source(i), buffer(slot), tile_sems.at[slot])

        tile(0, 0).start()

        def step(i, _):
            slot = i % 2

            @pl.when(i + 1 < n)
            def _():
                tile(i + 1, 1 - slot).start()

            tile(i, slot).wait()
            body(i, buffer(slot))
            return 0

        lax.fori_loop(0, n, step, 0)

    chains_of = {array: [c for c in CHAINS[array] if c[0] == array] for array in range(3)}
    small_chain = CHAINS[0][3]
    numbers = {}
    for array in (2, 1, 0):
        for chain in chains_of[array]:
            numbers[chain] = len(numbers)
    numbers[small_chain] = 9
    land_of = (lands[1], lands[1], lands[0], lands[2])
    outs = (o_att, o_up, o_down, o_small)

    class Group:
        def __init__(self, layer, array):
            self.layer, self.array = layer, array
            self.turn = 3 * (1 - layer) + (2 - array) if array < 3 else 6
            self.pieces = []
            todo = [small_chain] if array == 3 else chains_of[array]
            self.chains = []
            for chain in todo:
                n = numbers[chain]
                out = outs[array] if array == 3 else outs[array].at[layer]
                sems = n if array == 3 else n + 10 * (1 - layer)
                self.chains.append(
                    Scatter(at, parts[array], out, landings[6 * n : 6 * n + 6], chain, send.at[sems], recv.at[sems])
                )

        def admit(self):
            if self.array < 3 and self.layer == 0:
                pl.semaphore_wait(free.at[self.array], len(PEERS))
            if self.array in (0, 1) and (self.layer, self.array) != (1, 1):
                pl.semaphore_wait(free_land, 1)

        def piece(self, src, dst):
            n = 4 * self.turn + len(self.pieces)
            made = pltpu.make_async_remote_copy(
                src_ref=src,
                dst_ref=dst,
                send_sem=across_s.at[n],
                recv_sem=across_r.at[n],
                device_id=partner,
                device_id_type=MESH,
            )
            made.start()
            self.pieces.append(made)

        def enter(self):
            part, land = parts[self.array], land_of[self.array]
            for x, made in enumerate(self.pieces):
                made.wait_recv()
                if self.array == 3:
                    add_to(part, (land,))
                else:
                    add_to(part.at[x], (land.at[x],))
            if self.array in (0, 1) and (self.layer, self.array) != (0, 0):
                pl.semaphore_signal(free_land, inc=1, device_id=partner, device_id_type=MESH)
            for made in self.pieces[-2:]:
                made.wait_send()

        def step(self, k):
            for chain in self.chains:
                chain.step(k)
            if k == 6 and self.layer == 1 and self.array < 3:
                for axis, by in PEERS:
                    pl.semaphore_signal(
                        free.at[self.array], inc=1, device_id=device(moved(at, axis, by)), device_id_type=MESH
                    )

    groups = {(layer, array): Group(layer, array) for layer in (1, 0) for array in (2, 1, 0)}
    last_small = Group(0, 3)

    def serve(*steps):
        for layer, array, k in steps:
            groups[(layer, array)].step(k)

    def down_grads(layer):
        group = groups[(layer, 2)]
        group.admit()
        for x in range(4):
            slot = x % 2
            if x >= 2:
                group.pieces[x - 2].wait_send()

            def body(j, _):
                low, pairs = j // 2, j % 2
                columns = pl.ds(pl.multiple_of((4 * x + j) * 256, 256), 256)
                value = dot(active[:, columns], rounded[...], 0, 0).astype(BF)
                mine, other = split_cores(value, core, (2, 2, 64, WIDTH))
                parts[2][x, low, pl.ds(2 * pairs, 2)] = mine
                stage_down[slot, low, pl.ds(2 * pairs, 2)] = other
                return 0

            lax.fori_loop(0, 4, body, 0)
            group.piece(stage_down.at[slot], lands[0].at[x])

    def wide_grads(layer, array, terms):
        group = groups[(layer, array)]
        group.admit()
        part = parts[array]
        for x in range(4):
            slot = x % 2
            if x >= 2:
                group.pieces[x - 2].wait_send()
            for start, count, left, right, skip in terms:

                def body(j, _):
                    to = pl.ds(pl.multiple_of(start + j * 1024, 1024), 1024)
                    frm = pl.ds(pl.multiple_of(skip + j * 1024, 1024), 1024)
                    value = dot(left[:, pl.ds(256 * x, 256)], right[:, frm], 0, 0).astype(BF)
                    mine, other = split_cores(value, core, (2, 4, 2, 16, 1024))
                    part[x, :, :, :, to] = mine
                    stage_wide[slot, :, :, :, to] = other
                    return 0

                lax.fori_loop(0, count, body, 0)
            group.piece(stage_wide.at[slot], lands[1].at[x])

    def through_rows(layer, array, columns, left, put):
        start, size = columns
        source = weights[layer][array]

        def body(x, tile):
            put(x, dot(left[...], tile[:, pl.ds(0, size)], 1, 1))

        streamed(
            4,
            lambda x: source.at[pl.ds(pl.multiple_of(x * 256, 256), 256), pl.ds(start, size)],
            lambda slot: tiles_wide.at[slot, :, pl.ds(0, size)],
            body,
        )

    def put_hidden(x, value):
        grad_hidden[:, pl.ds(pl.multiple_of(x * 256, 256), 256)] = value

    def put_mixed(x, value):
        grad_mixed[:, pl.ds(pl.multiple_of(x * 256, 256), 256)] = value.astype(BF)

    fetch_active(1)
    fetch_slope(1)
    fetch_mid(1)
    fetch_probs(1)
    fetch_qkv(1)
    fetch_mixed(1)
    state[...] = cotangent[...].astype(F32)
    rounded[...] = cotangent[...]
    for layer in (1, 0):
        row = lambda k: params.at[layer, pl.ds(k, 1), :]
        ready("active")
        down_grads(layer)
        if layer == 1:
            fetch_active(0)
        groups[(layer, 2)].enter()
        serve((layer, 2, 0))
        if layer == 0:
            serve((1, 1, 6), (1, 0, 2))
        ready("slope")
        down = weights[layer][2]

        def through_down(i, tile):
            columns = pl.ds(pl.multiple_of(i * 256, 256), 256)
            value = dot(rounded[...], tile[...], 1, 1)
            slope[:, columns] = (value * slope[:, columns].astype(F32)).astype(BF)

        streamed(
            16,
            lambda i: down.at[pl.ds(pl.multiple_of(i * 256, 256), 256)],
            lambda slot: tiles_down.at[slot],
            through_down,
        )
        serve((layer, 2, 1))
        if layer == 0:
            serve((1, 0, 3))
        ready("mid")
        norm_into(hidden, stream, row(2), row(3))
        wide_grads(layer, 1, ((0, 4, hidden, slope, 0),))
        groups[(layer, 1)].enter()
        serve((layer, 1, 0), (layer, 2, 2))
        if layer == 0:
            serve((1, 0, 4))
        through_rows(layer, 1, (0, HIDDEN), slope, put_hidden)
        if layer == 1:
            fetch_slope(0)
        norm_back_into(grad_hidden, state, stream, row(2), sums, 2)
        fetch_stream(layer)
        rounded[...] = state[...].astype(BF)
        serve((layer, 2, 3), (layer, 1, 1))
        if layer == 0:
            serve((1, 0, 5))
        through_rows(layer, 0, (3 * WIDTH, WIDTH), rounded, put_mixed)
        ready("qkv")
        ready("probs")
        attention_backward(qkv, probs, grad_mixed, 0, 4)
        serve((layer, 2, 4), (layer, 1, 2))
        if layer == 0:
            serve((1, 0, 6))
        attention_backward(qkv, probs, grad_mixed, 4, 8)
        serve((layer, 2, 5), (layer, 1, 3))
        ready("stream")
        ready("mixed")
        norm_into(hidden, stream, row(0), row(1))
        wide_grads(layer, 0, ((0, 3, hidden, qkv, 0), (3 * WIDTH, 1, mixed, rounded, 0)))
        groups[(layer, 0)].enter()
        serve((layer, 0, 0), (layer, 2, 6), (layer, 1, 4))
        table = table_grads(probs, bucket_rows[...])
        if layer == 1:
            fetch_probs(0)
            fetch_mixed(0)
        through_rows(layer, 0, (0, 3 * WIDTH), qkv, put_hidden)
        norm_back_into(grad_hidden, state, stream, row(0), sums, 0)
        if layer == 1:
            fetch_qkv(0)
            fetch_mid(0)
        rounded[...] = state[...].astype(BF)
        shares = share_grads(sums, table).astype(BF)
        chosen = (iota((64, 1024), 1) == iota((64, 1024), 0) * 16 + layer).astype(BF)
        placed = dot(chosen, shares, 0, 0)
        if layer == 1:
            small_total[...] = placed
        else:
            small_total[...] = small_total[...] + placed
        serve((layer, 0, 1), (layer, 1, 5))
    finish = pltpu.make_async_copy(state, o_input, out_sem)
    finish.start()
    mine, other = split_cores(small_total[...].astype(BF), core, (4, 2, 4, 2, 16, LANES))
    for i in range(2):
        columns = pl.ds(i * LANES, LANES)
        parts[3][:, :, :, :, columns] = mine
        stage_small[:, :, :, :, columns] = other
    last_small.piece(stage_small, lands[2])
    last_small.enter()
    last_small.step(0)
    serve((0, 0, 2), (0, 1, 6))
    for k in range(1, 3):
        last_small.step(k)
    serve((0, 0, 3))
    last_small.step(3)
    serve((0, 0, 4))
    last_small.step(4)
    serve((0, 0, 5))
    last_small.step(5)
    serve((0, 0, 6))
    last_small.step(6)
    finish.wait()


def backward(cotangent, params, bucket_rows, fetched, saved):
    wide, tall = (1024, 4096), (4096, 1024)
    arrays = [fetched[i].reshape(s) for i, s in ((3, wide), (4, wide), (5, tall), (0, wide), (1, wide), (2, tall))]
    vmem = pl.BlockSpec(memory_space=pltpu.VMEM)
    hbm = pl.BlockSpec(memory_space=pl.ANY)
    chains = [c for array in (2, 1, 0) for c in CHAINS[array] if c[0] == array] + [CHAINS[0][3]]
    scratch = [pltpu.VMEM(s, BF) for s in PART_SHAPES]
    scratch += [pltpu.VMEM(PART_SHAPES[i], BF) for i in (2, 1, 3)]
    for chain in chains:
        scratch += [pltpu.VMEM(s, BF) for s in landing_shapes(chain)]
    scratch += [
        pltpu.VMEM((2,) + PART_SHAPES[2][1:], BF),
        pltpu.VMEM((2,) + PART_SHAPES[1][1:], BF),
        pltpu.VMEM(PART_SHAPES[3], BF),
        pltpu.VMEM((2, 256, WIDTH), BF),
        pltpu.VMEM((2, 256, HIDDEN), BF),
        pltpu.VMEM((ROWS, HIDDEN), BF),
        pltpu.VMEM((ROWS, HIDDEN), BF),
        pltpu.VMEM((HEADS, ROWS, ROWS), BF),
        pltpu.VMEM((ROWS, 3 * WIDTH), BF),
        pltpu.VMEM((ROWS, WIDTH), BF),
        pltpu.VMEM((ROWS, WIDTH), BF),
        pltpu.VMEM((ROWS, WIDTH), F32),
        pltpu.VMEM((ROWS, WIDTH), F32),
        pltpu.VMEM((ROWS, WIDTH), BF),
        pltpu.VMEM((ROWS, WIDTH), F32),
        pltpu.VMEM((ROWS, WIDTH), BF),
        pltpu.VMEM((8, WIDTH), F32),
        pltpu.VMEM((1024, LANES), F32),
        pltpu.SemaphoreType.DMA((20, N_SCATTER)),
        pltpu.SemaphoreType.DMA((20, N_SCATTER)),
        pltpu.SemaphoreType.DMA((28,)),
        pltpu.SemaphoreType.DMA((28,)),
        pltpu.SemaphoreType.REGULAR((3,)),
        pltpu.SemaphoreType.REGULAR,
        pltpu.SemaphoreType.DMA((7,)),
        pltpu.SemaphoreType.DMA((2,)),
        pltpu.SemaphoreType.DMA,
    ]
    return pl.pallas_call(
        backward_kernel,
        out_shape=[
            jax.ShapeDtypeStruct((ROWS, WIDTH), F32),
            jax.ShapeDtypeStruct((2, 16, 4096), F32),
            jax.ShapeDtypeStruct((2, 16, 4096), F32),
            jax.ShapeDtypeStruct((2, 64, 1024), F32),
            jax.ShapeDtypeStruct((16, 256), F32),
        ],
        in_specs=[vmem] * 3 + [hbm] * 14,
        out_specs=[hbm] + [vmem] * 4,
        scratch_shapes=scratch,
        compiler_params=pltpu.CompilerParams(
            collective_id=1, has_side_effects=True, vmem_limit_bytes=63 << 20
        ),
        name="backward_scatter",
    )(cotangent, params, bucket_rows, *arrays, *saved)


def on_device(
    tokens,
    seg_ids,
    buckets,
    cotangent,
    ln1_gain,
    ln1_bias,
    w_query,
    w_key,
    w_value,
    w_out,
    rel_table,
    ln2_gain,
    ln2_bias,
    w_up,
    w_down,
):
    small = jnp.concatenate([ln1_gain, ln1_bias, ln2_gain, ln2_bias, rel_table], 1)
    small = jnp.pad(small, ((0, 14), (0, 56)))
    by_offset = jnp.concatenate([buckets[:1], buckets[:0:-1]])
    bucket_rows = (by_offset[None, :] == (jnp.arange(64, dtype=jnp.int32) // 2)[:, None]).astype(BF)
    done = forward(
        jnp.concatenate([w_query, w_key, w_value, w_out], 2),
        w_up,
        w_down,
        jnp.concatenate([small, small], 1),
        tokens,
        seg_ids,
        bucket_rows,
    )
    acts, mid0, mid1, stream, params = done[7:12]
    saved = (stream, mid0, mid1) + tuple(done[12:])
    grad_input, att, up, down, small = backward(cotangent, params, bucket_rows, done[:6], saved)
    return (
        acts,
        grad_input,
        small[:2, 0:16],
        small[:2, 16:32],
        att[:, :, :1024],
        att[:, :, 1024:2048],
        att[:, :, 2048:3072],
        att[:, :, 3072:],
        small[:2, 64:72],
        small[:2, 32:48],
        small[:2, 48:64],
        up,
        down,
    )


def solution(mesh):
    placed = (
        P(("wide", "narrow"), None),
        P(("wide", "narrow")),
        P(),
        P(("wide", "narrow"), None),
        P(None, "wide"),
        P(None, "wide"),
        P(None, "wide", None),
        P(None, "wide", None),
        P(None, "wide", None),
        P(None, "wide", None),
        P(None, "wide"),
        P(None, "wide"),
        P(None, "wide"),
        P(None, "wide", None),
        P(None, "wide", None),
    )
    return jax.shard_map(
        on_device,
        mesh=mesh,
        in_specs=placed,
        out_specs=(
            P(None, ("wide", "narrow"), None),
            P(("wide", "narrow"), None),
            P(None, "wide"),
            P(None, "wide"),
            P(None, "wide", None),
            P(None, "wide", None),
            P(None, "wide", None),
            P(None, "wide", None),
            P(None, "wide"),
            P(None, "wide"),
            P(None, "wide"),
            P(None, "wide", None),
            P(None, "wide", None),
        ),
        check_vma=False,
    )
```

```python
import jax
import jax.numpy as jnp
from jax import lax
from jax.experimental import pallas as pl
from jax.experimental.pallas import tpu as pltpu
from jax.sharding import PartitionSpec as P

MESH = pl.DeviceIdType.MESH
TILE = 128
BF = jnp.bfloat16
F32 = jnp.float32
ORDERS = (("y", "x", "z"), ("z", "y", "x"), ("x", "z", "y"))
CHAINS = (
    ((0, 0, 10, 0), (0, 10, 10, 1), (0, 20, 12, 2), (3, 0, 2, 0)),
    ((1, 0, 10, 0), (1, 10, 10, 1), (1, 20, 12, 2)),
    ((2, 0, 3, 0), (2, 3, 3, 1), (2, 6, 2, 2)),
)


def place():
    wide, narrow = lax.axis_index("wide"), lax.axis_index("narrow")
    return {
        "x": wide // 16,
        "y": narrow * 2 + (wide // 8) % 2,
        "z": (wide // 2) % 4,
        "c": wide % 2,
    }


def device(at):
    return (((at["x"] * 2 + at["y"] % 2) * 4 + at["z"]) * 2 + at["c"], at["y"] // 2)


def moved(at, axis, by):
    new = dict(at)
    new[axis] = (at[axis] + by) % (2 if axis == "c" else 4)
    return new


def pick(ref, chain, sel, lead=()):
    array, tile, tiles, _ = chain
    y = sel["y"]
    columns = pl.ds(tile * TILE, tiles * TILE)
    rows = pl.ds(0, 64 if array == 2 else 16)
    if y is None:
        low = pl.ds(0, 2)
    elif isinstance(y, tuple):
        low = pl.ds(y[0], 1)
    else:
        low = y % 2
        if array == 2:
            rows = pl.ds(pl.multiple_of((y // 2) * 32, 32), 32)
        else:
            half = tiles // 2 * TILE
            columns = pl.ds(pl.multiple_of(tile * TILE + (y // 2) * half, TILE), half)

    def one(v):
        return pl.ds(0, 4) if v is None else v

    index = lead + (one(sel["x"]), low, one(sel["z"]))
    if "c" in sel:
        index = index + (sel["c"],)
    return ref.at[index + (rows, columns)]


def half_of(axis, part):
    return (part,) if axis == "y" else pl.ds(2 * part, 2)


def greet(at, peers):
    barrier = pltpu.get_barrier_semaphore()
    for axis, by in peers:
        pl.semaphore_signal(barrier, inc=1, device_id=device(moved(at, axis, by)), device_id_type=MESH)
    pl.semaphore_wait(barrier, len(peers))


PEERS = tuple((a, b) for a in "xyz" for b in (1, 3, 2)) + (("c", 1),)


class Gather:
    def __init__(self, at, ref, chain, send, recv):
        self.at, self.ref, self.chain, self.send, self.recv = at, ref, chain, send, recv
        self.axes = ORDERS[chain[3]]
        self.count = 0
        self.sent = []

    def place_own(self, mine, sem):
        array, tile, tiles, _ = self.chain
        side = self.at["y"] // 2
        if array == 2:
            where = (pl.ds(pl.multiple_of(side * 32, 32), 32), pl.ds(tile * TILE, tiles * TILE))
        else:
            wide = tiles // 2 * TILE
            where = (slice(None), pl.ds(pl.multiple_of(tile * TILE + side * wide, TILE), wide))
        self.own = pltpu.make_async_copy(mine.at[where], pick(self.ref, self.chain, self.sel(())), sem)
        self.own.start()

    def copy(self, sel, axis, by):
        slot = self.count
        self.count += 1
        block = pick(self.ref, self.chain, sel)
        made = pltpu.make_async_remote_copy(
            src_ref=block,
            dst_ref=block,
            send_sem=self.send.at[slot],
            recv_sem=self.recv.at[slot],
            device_id=device(moved(self.at, axis, by)),
            device_id_type=MESH,
        )
        made.start()
        self.sent.append(made)
        return made

    def sel(self, done, axis=None, by=0, half=None):
        at = {k: self.at[k] for k in "xyzc"}
        for d in done:
            at[d] = None
        if half is not None:
            at[done[0]] = half_of(done[0], half)
        if axis is not None:
            at[axis] = (self.at[axis] + by) % 4
        return at

    def step(self, k):
        a1, a2, a3 = self.axes
        if k == 0:
            self.own.wait()
            own = self.sel(())
            self.first = [self.copy(own, a1, by) for by in (1, 3, 2)]
        elif k in (1, 3):
            done, axis = ((a1,), a2) if k == 1 else ((a1, a2), a3)
            for c in self.first:
                c.wait_recv()
            own = self.sel(done)
            self.pair = [self.copy(own, axis, 1), self.copy(own, axis, 3)]
            if k == 3:
                self.across = [self.copy(own, "c", 1)]
        elif k in (2, 4):
            done, axis = ((a1,), a2) if k == 2 else ((a1, a2), a3)
            self.pair[0].wait_recv()
            forward = self.copy(self.sel(done, axis, 3, 0), axis, 1)
            self.pair[1].wait_recv()
            self.first = [forward, self.copy(self.sel(done, axis, 1, 1), axis, 3)]
            if k == 4:
                for by in (3, 1):
                    self.across.append(self.copy(self.sel(done, axis, by), "c", 1))
        elif k == 5:
            for c in self.first:
                c.wait_recv()
            self.across.append(self.copy(self.sel((a1, a2), a3, 2), "c", 1))
        elif k == 6:
            for c in self.across:
                c.wait_recv()
            for c in self.sent:
                c.wait_send()


N_GATHER = 15


def gather_groups(at, n_layers, mine, fetched, send, recv, local):
    groups = []
    index = 0
    for layer in range(n_layers):
        for group in CHAINS:
            chains = []
            for chain in group:
                array = chain[0]
                if array == 3 and layer > 0:
                    continue
                ref = fetched[3 * n_layers] if array == 3 else fetched[3 * layer + array]
                made = Gather(at, ref, chain, send.at[index], recv.at[index])
                made.place_own(mine[array] if array == 3 else mine[array].at[layer], local.at[index])
                chains.append(made)
                index += 1
            groups.append(chains)
    return groups


N_SCATTER = 12
PART_SHAPES = ((4, 2, 4, 16, 4096), (4, 2, 4, 16, 4096), (4, 2, 4, 64, 1024), (4, 2, 4, 16, 256))


def landing_shapes(chain):
    array, _, tiles, order = chain
    a1, a2, a3 = ORDERS[order]
    rows, cols = (64, tiles * TILE) if array == 2 else (16, tiles * TILE)
    unit = (rows // 2, cols) if array == 2 else (rows, cols // 2)

    def block(full, half=None):
        dims = []
        for axis in "xyz":
            if axis in full:
                size = 2 if axis == "y" else 4
                dims.append(size // 2 if axis == half else size)
        return tuple(dims) + ((rows, cols) if "y" in full else unit)

    return (
        (2,) + block((a1, a2), a1),
        (2,) + block((a1, a2)),
        (2,) + block((a1,), a1),
        (2,) + block((a1,)),
        (3,) + unit,
        unit,
    )


class Scatter:
    def __init__(self, at, part, out, landing, chain, send, recv):
        self.at, self.part, self.out, self.chain = at, part, out, chain
        self.landing, self.send, self.recv = landing, send, recv
        self.axes = ORDERS[chain[3]]
        self.count = 0
        self.sent = []

    def copy(self, src, dst, axis, by):
        slot = self.count
        self.count += 1
        made = pltpu.make_async_remote_copy(
            src_ref=src,
            dst_ref=dst,
            send_sem=self.send.at[slot],
            recv_sem=self.recv.at[slot],
            device_id=device(moved(self.at, axis, by)),
            device_id_type=MESH,
        )
        made.start()
        self.sent.append(made)
        return made

    def sel(self, done, axis=None, by=0, half=None):
        at = {k: self.at[k] for k in "xyz"}
        for d in done:
            at[d] = None
        if half is not None:
            at[done[0]] = half_of(done[0], half)
        if axis is not None:
            at[axis] = (self.at[axis] + by) % 4
        return pick(self.part, self.chain, at)

    def step(self, k):
        a1, a2, a3 = self.axes
        if k in (1, 3):
            done, axis = ((a1, a2), a3) if k == 1 else ((a1,), a2)
            land, blocks = self.landing[k - 1], self.landing[k]
            self.blocks = []
            for i, by in ((0, 1), (1, 3)):
                self.halves[i].wait_recv()
                add_to(self.sel(done, axis, by, i), (land.at[i],))
                self.blocks.append(self.copy(self.sel(done, axis, by), blocks.at[i], axis, by))
        if k in (2, 4):
            done = (a1, a2) if k == 2 else (a1,)
            blocks = self.landing[k - 1]
            for c in self.blocks:
                c.wait_recv()
            add_to(self.sel(done), (blocks.at[0], blocks.at[1]))
        if k in (0, 2):
            done, axis = ((a1, a2), a3) if k == 0 else ((a1,), a2)
            land = self.landing[0 if k == 0 else 2]
            self.halves = [
                self.copy(self.sel(done, axis, 2, 0), land.at[0], axis, 1),
                self.copy(self.sel(done, axis, 2, 1), land.at[1], axis, 3),
            ]
        if k == 4:
            land = self.landing[4]
            self.units = [self.copy(self.sel((), a1, by), land.at[i], a1, by) for i, by in enumerate((1, 3, 2))]
        if k == 5:
            land = self.landing[4]
            for c in self.units:
                c.wait_recv()
            add_to(self.sel(()), (land.at[0], land.at[1], land.at[2]))
            self.last = self.copy(self.sel(()), self.landing[5], "y", 2)
        if k == 6:
            self.last.wait_recv()
            array, tile, tiles, _ = self.chain
            high = self.at["y"] // 2
            for side, ref in ((high, self.sel(())), (1 - high, self.landing[5])):
                if array == 2:
                    where = (pl.ds(pl.multiple_of(side * 32, 32), 32), pl.ds(tile * TILE, tiles * TILE))
                else:
                    wide = tiles // 2 * TILE
                    where = (slice(None), pl.ds(pl.multiple_of(tile * TILE + side * wide, TILE), wide))
                self.out[where] = ref[...].astype(F32)
            for c in self.sent:
                c.wait_send()


def add_to(ref, terms):
    lead = ref.shape[:-2]
    if not lead:
        total = ref[...]
        for t in terms:
            total = total + t[...]
        ref[...] = total
        return
    n = 1
    for d in lead:
        n *= d

    def body(i, _):
        index = []
        rest = i
        for d in reversed(lead):
            index.append(rest % d)
            rest = rest // d
        index = tuple(reversed(index))
        total = ref[index]
        for t in terms:
            total = total + t[index]
        ref[index] = total
        return 0

    lax.fori_loop(0, n, body, 0)


FORWARD_SERVED = (
    (0, 1, 2, 3, 0, 1, 2, 3, 0, 1, 2, 3, 0, 4, 1, 5, 2, 3, 0, 4, 1, 5, 2, 3, 0, 4, 0, 1,),
    (1, 5,),
    (2,),
    (3, 4,),
    (2, 5, 3,),
    (),
    (),
    (),
    (4,),
    (),
    (),
    (),
    (),
    (5,),
    (4,),
    (5, 4,),
    (),
    (5,),
    (),
    (),
    (),
    (),
    (),
    (),
    (),
    (),
)


LANES = 128
GELU = 0.7978845608028654
EPSILON = 1e-05
ROWS = 256
WIDTH = 1024
HIDDEN = 4096
HEADS = 16
HEAD = 64
BUCKETS = 32
MASKED = -1e30


def dot(a, b, ca=1, cb=0):
    return lax.dot_general(a, b, (((ca,), (cb,)), ((), ())), preferred_element_type=F32)


def iota(shape, dim):
    return lax.broadcasted_iota(jnp.int32, shape, dim)


def param_rows(small, layer):
    flat = small[...].reshape(1024, 256)[:, :128]
    chosen = (iota((64, 1024), 1) == iota((64, 1024), 0) * 16 + layer).astype(BF)
    shares = dot(chosen, flat).astype(BF)
    owner = iota((64, 1024), 0) == iota((64, 1024), 1) // 16
    rows = []
    for k in range(4):
        spread = (iota((128, 1024), 0) == 16 * k + iota((128, 1024), 1) % 16).astype(BF)
        rows.append(jnp.sum(jnp.where(owner, dot(shares, spread), 0.0), 0, keepdims=True))
    return rows, shares


def bias_rows(shares, bucket_rows):
    picked = (iota((16, 128), 1) == 64 + iota((16, 128), 0) % 8).astype(BF)
    entries = dot(picked, shares, 1, 1)
    entries = jnp.where(iota((16, 64), 1) % 2 == iota((16, 64), 0) // 8, entries, 0.0).astype(BF)
    return dot(entries, bucket_rows)


def norm_parts(rows):
    center = jnp.mean(rows, -1, keepdims=True)
    centered = rows - center
    inverse = lax.rsqrt(jnp.mean(centered * centered, -1, keepdims=True) + EPSILON)
    return centered * inverse, inverse


def norm_into(dst, src, gain, shift):
    def body(i, _):
        at = pl.ds(pl.multiple_of(i * 64, 64), 64)
        normed, _unused = norm_parts(src[at, :])
        dst[at, :] = (normed * gain[...] + shift[...]).astype(BF)
        return 0

    lax.fori_loop(0, ROWS // 64, body, 0)


def attention_forward(qkv, probs, mixed, bias, allowed, start, stop):
    scale = HEAD ** (-0.5)
    low = iota((ROWS, LANES), 1) < HEAD

    def pair(i, _):
        def columns(k):
            return pl.ds(pl.multiple_of(k * WIDTH + i * LANES, LANES), LANES)

        q, k, v = (qkv[:, columns(j)] for j in range(3))
        halves = []
        for side in range(2):
            head = 2 * i + side
            mine = jnp.where(low == (side == 0), q, jnp.zeros_like(q))
            scores = dot(mine, k, 1, 1) * scale
            first = bias[head]
            shifted = jnp.concatenate([first] + [pltpu.roll(first, 16 * b, 1) for b in range(1, 16)], 0)
            scores = jnp.where(allowed[...] > 0, scores + shifted, MASKED)
            peak = jnp.max(scores, -1, keepdims=True)
            terms = jnp.exp(scores - peak)
            rounded = (terms / jnp.sum(terms, -1, keepdims=True)).astype(BF)
            probs[head] = rounded
            halves.append(dot(rounded, v))
        mixed[:, pl.ds(pl.multiple_of(i * LANES, LANES), LANES)] = jnp.where(low, halves[0], halves[1]).astype(BF)
        return 0

    lax.fori_loop(start, stop, pair, 0)


def forward_kernel(att, up, down, small, tokens, seg_col, seg_row, bucket_rows, *rest):
    outs, rest = rest[:17], rest[17:]
    fetched = outs[:7]
    o_acts, o_mid0, o_mid1, o_stream, o_params, o_qkv, o_probs, o_mixed, o_active, o_slope = outs[7:]
    (w_att, w_up, w_down, w_small, stream, middle, hidden, qkv, probs, mixed, active, slope, rounded,
     bias, allowed, params, send, recv, local, loads, stores) = rest
    at = place()
    greet(at, PEERS)
    groups = gather_groups(at, 2, (att, up, down, small), fetched, send, recv, local)
    buffers = (w_att, w_up, w_down)
    served = [0] * 6
    arrived, used, waiting = set(), set(), {}
    stored = []
    points = [0]

    def store(src, dst):
        made = pltpu.make_async_copy(src, dst, stores.at[len(stored)])
        made.start()
        stored.append(made)

    def load(g):
        if g in arrived and g not in waiting and (g < 3 or g - 3 in used):
            waiting[g] = pltpu.make_async_copy(fetched[g], buffers[g % 3], loads.at[g])
            waiting[g].start()

    def serve(g):
        for chain in groups[g]:
            chain.step(served[g])
        served[g] += 1
        if served[g] == 7:
            arrived.add(g)
            load(g)
            if g == 0:
                waiting[6] = pltpu.make_async_copy(fetched[6], w_small, loads.at[6])
                waiting[6].start()

    def point():
        for g in FORWARD_SERVED[points[0]]:
            serve(g)
        points[0] += 1

    def need(g):
        point()
        waiting[g].wait()

    def done(g):
        used.add(g)
        if g < 3:
            load(g + 3)

    same = (seg_col[...] == seg_row[...]) & (iota((ROWS, ROWS), 0) >= iota((ROWS, ROWS), 1))
    allowed[...] = same.astype(F32)
    stream[0] = tokens[...].astype(F32)
    for layer in range(2):
        need(3 * layer)
        if layer == 0:
            waiting[6].wait()
        rows, shares = param_rows(w_small, layer)
        for k in range(4):
            params[layer, pl.ds(k, 1), :] = rows[k]
        by_offset = bias_rows(shares, bucket_rows[...])
        for head in range(HEADS):
            wide = jnp.broadcast_to(by_offset[head : head + 1], (16, ROWS))
            bias[head] = pltpu.roll(wide, 0, 1, stride=1, stride_axis=0)
        here, mid = stream.at[layer], middle.at[layer]
        row = lambda k: params.at[layer, pl.ds(k, 1), :]
        norm_into(hidden, here, row(0), row(1))
        wide_qkv, wide_probs, wide_mixed = qkv.at[layer], probs.at[layer], mixed.at[layer]
        wide_active, wide_slope = active.at[layer], slope.at[layer]

        def project(i, _):
            cols = pl.ds(pl.multiple_of(i * 512, 512), 512)
            weights = w_att[:, :, :, :, :, cols].reshape(WIDTH, 512)
            wide_qkv[:, cols] = dot(hidden[...], weights).astype(BF)
            return 0

        point()
        lax.fori_loop(0, 6, project, 0)
        for n in range(4):
            point()
            attention_forward(wide_qkv, wide_probs, wide_mixed, bias, allowed, 2 * n, 2 * n + 2)

        def out_project(i, _):
            cols = pl.ds(pl.multiple_of(i * 512, 512), 512)
            from_cols = pl.ds(pl.multiple_of(3072 + i * 512, 512), 512)
            weights = w_att[:, :, :, :, :, from_cols].reshape(WIDTH, 512)
            mid[:, cols] = here[:, cols] + dot(wide_mixed[...], weights)
            return 0

        point()
        lax.fori_loop(0, 2, out_project, 0)
        done(3 * layer)
        norm_into(hidden, mid, row(2), row(3))
        store(wide_qkv, o_qkv.at[layer])
        store(wide_probs, o_probs.at[layer])
        store(wide_mixed, o_mixed.at[layer])
        store(mid, (o_mid0, o_mid1)[layer])
        need(3 * layer + 1)

        def expand(i, _):
            cols = pl.ds(pl.multiple_of(i * 512, 512), 512)
            weights = w_up[:, :, :, :, :, cols].reshape(WIDTH, 512)
            u = dot(hidden[...], weights)
            square = u * u
            tangent = jnp.tanh(GELU * (u + 0.044715 * square * u))
            wide_active[:, cols] = (0.5 * u * (1.0 + tangent)).astype(BF)
            wide_slope[:, cols] = (
                0.5 * (1.0 + tangent)
                + 0.5 * u * (1.0 - tangent * tangent) * GELU * (1.0 + 3.0 * 0.044715 * square)
            ).astype(BF)
            return 0

        for n in range(4):
            if n > 0:
                point()
            lax.fori_loop(2 * n, 2 * n + 2, expand, 0)
        done(3 * layer + 1)
        store(wide_active, o_active.at[layer])
        store(wide_slope, o_slope.at[layer])
        need(3 * layer + 2)
        acts = rounded.at[layer]

        def contract(i, _):
            cols = pl.ds(pl.multiple_of(i * 256, 256), 256)
            weights = w_down[:, :, :, :, :, cols].reshape(HIDDEN, 256)
            result = mid[:, cols] + dot(wide_active[...], weights)
            if layer == 0:
                stream[1, :, cols] = result
            acts[:, cols] = result.astype(BF)
            return 0

        lax.fori_loop(0, 2, contract, 0)
        point()
        lax.fori_loop(2, 4, contract, 0)
        done(3 * layer + 2)
        store(acts, o_acts.at[layer])
    store(stream, o_stream)
    store(params, o_params)
    for made in stored:
        made.wait()


def forward(att, up, down, small, tokens, seg_ids, bucket_rows):
    lead = (4, 2, 4, 2)
    gathered = [lead + (16, 4096), lead + (16, 4096), lead + (64, 1024)] * 2 + [lead + (16, 256)]
    saved = [
        ((2, ROWS, WIDTH), BF),
        ((ROWS, WIDTH), F32),
        ((ROWS, WIDTH), F32),
        ((2, ROWS, WIDTH), F32),
        ((2, 8, WIDTH), F32),
        ((2, ROWS, 3 * WIDTH), BF),
        ((2, HEADS, ROWS, ROWS), BF),
        ((2, ROWS, WIDTH), BF),
        ((2, ROWS, HIDDEN), BF),
        ((2, ROWS, HIDDEN), BF),
    ]
    vmem = pl.BlockSpec(memory_space=pltpu.VMEM)
    hbm = pl.BlockSpec(memory_space=pl.ANY)
    return pl.pallas_call(
        forward_kernel,
        out_shape=[jax.ShapeDtypeStruct(s, BF) for s in gathered] + [jax.ShapeDtypeStruct(s, t) for s, t in saved],
        in_specs=[vmem] * 8,
        out_specs=[hbm] * 17,
        scratch_shapes=[
            pltpu.VMEM(gathered[0], BF),
            pltpu.VMEM(gathered[1], BF),
            pltpu.VMEM(gathered[2], BF),
            pltpu.VMEM(gathered[6], BF),
            pltpu.VMEM((2, ROWS, WIDTH), F32),
            pltpu.VMEM((2, ROWS, WIDTH), F32),
            pltpu.VMEM((ROWS, WIDTH), BF),
            pltpu.VMEM((2, ROWS, 3 * WIDTH), BF),
            pltpu.VMEM((2, HEADS, ROWS, ROWS), BF),
            pltpu.VMEM((2, ROWS, WIDTH), BF),
            pltpu.VMEM((2, ROWS, HIDDEN), BF),
            pltpu.VMEM((2, ROWS, HIDDEN), BF),
            pltpu.VMEM((2, ROWS, WIDTH), BF),
            pltpu.VMEM((HEADS, 16, ROWS), F32),
            pltpu.VMEM((ROWS, ROWS), F32),
            pltpu.VMEM((2, 8, WIDTH), F32),
            pltpu.SemaphoreType.DMA((19, N_GATHER)),
            pltpu.SemaphoreType.DMA((19, N_GATHER)),
            pltpu.SemaphoreType.DMA((19,)),
            pltpu.SemaphoreType.DMA((7,)),
            pltpu.SemaphoreType.DMA((16,)),
        ],
        compiler_params=pltpu.CompilerParams(
            collective_id=0, has_side_effects=True, vmem_limit_bytes=58 << 20
        ),
        name="gather_forward",
    )(att, up, down, small, tokens, seg_ids[:, None], seg_ids[None, :], bucket_rows)


SERVED = (
    (),
    (),
    (),
    (0,),
    (0, 0,),
    (0, 0,),
    (),
    (),
    (),
    (0, 1, 1,),
    (1, 1, 1,),
    (),
    (),
    (0,),
    (),
    (0, 1,),
    (),
    (0,),
    (),
    (),
    (),
    (2,),
    (0, 1, 2, 2,),
    (0, 1, 2, 2,),
    (),
    (1,),
    (),
    (2, 1,),
    (),
    (3,),
    (3,),
    (3, 3, 3,),
    (1, 2,),
    (),
    (2, 3,),
    (4,),
    (4,),
    (2, 4, 4, 4,),
    (),
    (2, 3,),
    (),
    (2, 3, 4,),
    (),
    (3,),
    (),
    (),
    (),
    (4, 3, 5, 5,),
    (5, 4, 3,),
    (5, 5,),
    (4,),
    (),
    (4, 5,),
    (),
    (4, 6, 6, 5, 6, 5, 6, 5, 6, 5, 6, 5, 6, 6,),
)


def split_cores(value, core, shape):
    both = value.reshape(shape)
    axis = len(shape) - 3
    even, odd = (lax.index_in_dim(both, i, axis, keepdims=False) for i in range(2))
    mine = core == 0
    return jnp.where(mine, even, odd), jnp.where(mine, odd, even)


def norm_back_into(grad, dst, src, gain, sums, base):
    def body(i, carry):
        by_gain, by_shift = carry
        at = pl.ds(pl.multiple_of(i * 32, 32), 32)
        normed, inverse = norm_parts(src[at, :])
        value = grad[at, :]
        scaled = value * gain[...]
        dst[at, :] = dst[at, :] + inverse * (
            scaled
            - jnp.mean(scaled, -1, keepdims=True)
            - normed * jnp.mean(scaled * normed, -1, keepdims=True)
        )
        by_gain = by_gain + jnp.sum(value * normed, 0, keepdims=True)
        return by_gain, by_shift + jnp.sum(value, 0, keepdims=True)

    zero = jnp.zeros((1, WIDTH), F32)
    by_gain, by_shift = lax.fori_loop(0, ROWS // 32, body, (zero, zero))
    sums[pl.ds(base, 1), :] = by_gain
    sums[pl.ds(base + 1, 1), :] = by_shift


def attention_backward(qkv, probs, grad_mixed, first, last):
    scale = HEAD ** (-0.5)
    low = iota((ROWS, LANES), 1) < HEAD

    def pair(i, _):
        def columns(k):
            return pl.ds(pl.multiple_of(k * WIDTH + i * LANES, LANES), LANES)

        q, k, v = (qkv[:, columns(j)] for j in range(3))
        grad = grad_mixed[:, pl.ds(pl.multiple_of(i * LANES, LANES), LANES)]
        grads = []
        for side in range(2):
            head = 2 * i + side
            rounded = probs[head]
            prob = rounded.astype(F32)
            mine = jnp.where(low == (side == 0), grad, jnp.zeros_like(grad))
            grad_probs = dot(mine, v, 1, 1)
            inner = jnp.sum(prob * grad_probs, -1, keepdims=True)
            grad_scores = (prob * (grad_probs - inner)).astype(BF)
            probs[head] = grad_scores
            grads.append(
                (dot(grad_scores, k) * scale, dot(grad_scores, q, 0, 0) * scale, dot(rounded, grad, 0, 0))
            )
        for j in range(3):
            qkv[:, columns(j)] = jnp.where(low, grads[0][j], grads[1][j]).astype(BF)
        return 0

    lax.fori_loop(first, last, pair, 0)


def table_grads(grad_scores, bucket_rows):
    total = jnp.zeros((HEADS, 16, ROWS), F32)
    for b in range(15, -1, -1):
        if b < 15:
            total = pltpu.roll(total, ROWS - 16, 2)
        total = total + grad_scores[:, pl.ds(16 * b, 16), :].astype(F32)
    line = iota((HEADS, 16, ROWS), 1)
    for bit in (1, 2, 4, 8):
        total = jnp.where((line // bit) % 2 == 1, pltpu.roll(total, ROWS - bit, 2), total)
    by_offset = jnp.sum(total, 1)
    high = by_offset.astype(BF)
    rest = (by_offset - high.astype(F32)).astype(BF)
    return dot(high, bucket_rows, 1, 1) + dot(rest, bucket_rows, 1, 1)


def share_grads(sums, table):
    owner = iota((64, 1024), 0) == iota((64, 1024), 1) // 16
    shares = jnp.zeros((64, 128), F32)
    for k in range(4):
        spread = (iota((128, 1024), 0) == 16 * k + iota((128, 1024), 1) % 16).astype(BF)
        mine = jnp.where(owner, sums[pl.ds(k, 1), :], 0.0).astype(BF)
        shares = shares + dot(mine, spread, 1, 1)
    picked = (iota((16, 128), 1) == 64 + iota((16, 128), 0) % 8).astype(BF)
    entries = jnp.where(iota((16, 64), 1) % 2 == iota((16, 64), 0) // 8, table, 0.0).astype(BF)
    return shares + dot(entries, picked, 0, 0)


def backward_kernel(*refs):
    (cotangent, params, bucket_rows, att1, up1, down1, att0, up0, down0,
     h_stream, h_mid0, h_mid1, h_qkv, h_probs, h_mixed, h_active, h_slope) = refs[:17]
    o_input, o_att, o_up, o_down, o_small = refs[17:22]
    rest = refs[22:]
    parts, lands, rest = rest[:4], rest[4:7], rest[7:]
    landings, rest = rest[:60], rest[60:]
    (stage_down, stage_wide, stage_small, tiles_down, tiles_wide, active, slope, probs, qkv, mixed, grad_mixed,
     state, stream, hidden, grad_hidden, rounded, sums, small_total,
     send, recv, across_s, across_r, free, free_land, loads, tile_sems, out_sem) = rest
    weights = ((att0, up0, down0), (att1, up1, down1))
    middles = (h_mid0, h_mid1)
    at = place()
    core = at["c"]
    partner = device(moved(at, "c", 1))
    greet(at, PEERS)

    pending = {}

    def fetch(name, i, src, dst):
        made = pltpu.make_async_copy(src, dst, loads.at[i])
        made.start()
        pending[name] = made

    def ready(name):
        pending.pop(name).wait()

    def fetch_active(layer):
        fetch("active", 0, h_active.at[layer], active)

    def fetch_slope(layer):
        fetch("slope", 1, h_slope.at[layer], slope)

    def fetch_mid(layer):
        fetch("mid", 2, middles[layer], stream)

    def fetch_stream(layer):
        fetch("stream", 3, h_stream.at[layer], stream)

    def fetch_probs(layer):
        fetch("probs", 4, h_probs.at[layer], probs)

    def fetch_qkv(layer):
        fetch("qkv", 5, h_qkv.at[layer], qkv)

    def fetch_mixed(layer):
        fetch("mixed", 6, h_mixed.at[layer], mixed)

    chains_of = {array: [c for c in CHAINS[array] if c[0] == array] for array in range(3)}
    small_chain = CHAINS[0][3]
    numbers = {}
    for array in (2, 1, 0):
        for chain in chains_of[array]:
            numbers[chain] = len(numbers)
    numbers[small_chain] = 9
    land_of = (lands[1], lands[1], lands[0], lands[2])
    outs = (o_att, o_up, o_down, o_small)

    class Group:
        def __init__(self, layer, array):
            self.layer, self.array = layer, array
            self.turn = 3 * (1 - layer) + (2 - array) if array < 3 else 6
            self.pieces = []
            self.served = 0
            todo = [small_chain] if array == 3 else chains_of[array]
            self.chains = []
            for chain in todo:
                n = numbers[chain]
                out = outs[array] if array == 3 else outs[array].at[layer]
                sems = n if array == 3 else n + 10 * (1 - layer)
                self.chains.append(
                    Scatter(at, parts[array], out, landings[6 * n : 6 * n + 6], chain, send.at[sems], recv.at[sems])
                )

        def admit(self):
            if self.array < 3 and self.layer == 0:
                pl.semaphore_wait(free.at[self.array], len(PEERS))
            if self.array in (0, 1) and (self.layer, self.array) != (1, 1):
                pl.semaphore_wait(free_land, 1)

        def piece(self, src, dst):
            n = 4 * self.turn + len(self.pieces)
            made = pltpu.make_async_remote_copy(
                src_ref=src,
                dst_ref=dst,
                send_sem=across_s.at[n],
                recv_sem=across_r.at[n],
                device_id=partner,
                device_id_type=MESH,
            )
            made.start()
            self.pieces.append(made)

        def add_piece(self, x):
            part, land = parts[self.array], land_of[self.array]
            self.pieces[x].wait_recv()
            if self.array == 3:
                add_to(part, (land,))
            else:
                add_to(part.at[x], (land.at[x],))
            if x == len(self.pieces) - 1:
                if self.array in (0, 1) and (self.layer, self.array) != (0, 0):
                    pl.semaphore_signal(free_land, inc=1, device_id=partner, device_id_type=MESH)
                for made in self.pieces[-2:]:
                    made.wait_send()

        def serve(self):
            pieces = 1 if self.array == 3 else 4
            k = self.served - pieces
            self.served += 1
            if k < 0:
                self.add_piece(k + pieces)
                return
            for chain in self.chains:
                chain.step(k)
            if k == 6 and self.layer == 1 and self.array < 3:
                for axis, by in PEERS:
                    pl.semaphore_signal(
                        free.at[self.array], inc=1, device_id=device(moved(at, axis, by)), device_id_type=MESH
                    )

    order = [(layer, array) for layer in (1, 0) for array in (2, 1, 0)] + [(0, 3)]
    groups = [Group(layer, array) for layer, array in order]
    by_name = dict(zip(order, groups))
    points = [0]

    def point():
        for g in SERVED[points[0]] if points[0] < len(SERVED) else ():
            groups[g].serve()
        points[0] += 1

    loaded = {}

    def tile_down(layer, i):
        rows = pl.ds(i * 512, 512)
        made = pltpu.make_async_copy(weights[layer][2].at[rows], tiles_down.at[i % 4], tile_sems.at[i % 4])
        made.start()
        loaded["down", i] = made

    def tile_wide(layer, array, x, slot, start, size, at_column, sem):
        made = pltpu.make_async_copy(
            weights[layer][array].at[pl.ds(x * 256, 256), pl.ds(start, size)],
            tiles_wide.at[slot, :, pl.ds(at_column, size)],
            tile_sems.at[sem],
        )
        made.start()
        return made

    def tile_up(layer, x):
        loaded["up", x] = tile_wide(layer, 1, x, x % 2, 0, HIDDEN, 0, 4 + x % 2)

    def tile_out(layer, x):
        loaded["out", x] = tile_wide(layer, 0, x, 0, 3 * WIDTH, WIDTH, x * WIDTH, 6 + x)

    def tile_qkv(layer, x):
        loaded["qkv", x] = tile_wide(layer, 0, x, 1 - x % 2, 0, 3 * WIDTH, 0, 5 - x % 2)

    def down_grads(layer):
        group = by_name[layer, 2]
        group.admit()
        for x in range(4):
            slot = x % 2
            if x >= 2:
                group.pieces[x - 2].wait_send()

            def body(j, _):
                low, pairs = j // 2, j % 2
                columns = pl.ds(pl.multiple_of((4 * x + j) * 256, 256), 256)
                value = dot(active[:, columns], rounded[...], 0, 0).astype(BF)
                mine, other = split_cores(value, core, (2, 2, 64, WIDTH))
                parts[2][x, low, pl.ds(2 * pairs, 2)] = mine
                stage_down[slot, low, pl.ds(2 * pairs, 2)] = other
                return 0

            lax.fori_loop(0, 4, body, 0)
            group.piece(stage_down.at[slot], lands[0].at[x])
            point()

    def wide_grads(layer, array, terms):
        group = by_name[layer, array]
        group.admit()
        part = parts[array]
        for x in range(4):
            slot = x % 2
            if x >= 2:
                group.pieces[x - 2].wait_send()
            for start, count, left, right, skip in terms:

                def body(j, _):
                    to = pl.ds(pl.multiple_of(start + j * 1024, 1024), 1024)
                    frm = pl.ds(pl.multiple_of(skip + j * 1024, 1024), 1024)
                    value = dot(left[:, pl.ds(256 * x, 256)], right[:, frm], 0, 0).astype(BF)
                    mine, other = split_cores(value, core, (2, 4, 2, 16, 1024))
                    part[x, :, :, :, to] = mine
                    stage_wide[slot, :, :, :, to] = other
                    return 0

                lax.fori_loop(0, count, body, 0)
            group.piece(stage_wide.at[slot], lands[1].at[x])
            point()

    for i in range(4):
        tile_down(1, i)
    fetch_active(1)
    fetch_slope(1)
    for x in range(2):
        tile_up(1, x)
    fetch_mid(1)
    fetch_probs(1)
    fetch_qkv(1)
    fetch_mixed(1)
    state[...] = cotangent[...].astype(F32)
    rounded[...] = cotangent[...]
    for layer in (1, 0):
        row = lambda k: params.at[layer, pl.ds(k, 1), :]
        ready("active")
        down_grads(layer)
        if layer == 1:
            fetch_active(0)
        ready("slope")
        for half in range(2):
            for j in range(4):
                i = 4 * half + j
                loaded.pop(("down", i)).wait()
                columns = pl.ds(i * 512, 512)
                value = dot(rounded[...], tiles_down[j], 1, 1)
                slope[:, columns] = (value * slope[:, columns].astype(F32)).astype(BF)
                if half == 0:
                    tile_down(layer, i + 4)
                elif layer == 1:
                    tile_down(0, j)
            point()
        ready("mid")
        norm_into(hidden, stream, row(2), row(3))
        wide_grads(layer, 1, ((0, 4, hidden, slope, 0),))
        for x in range(4):
            loaded.pop(("up", x)).wait()
            grad_hidden[:, pl.ds(x * 256, 256)] = dot(slope[...], tiles_wide[x % 2], 1, 1)
            if x < 2:
                tile_up(layer, x + 2)
            elif x == 2:
                for n in range(4):
                    tile_out(layer, n)
            else:
                tile_qkv(layer, 0)
            if x % 2 == 1:
                point()
        if layer == 1:
            fetch_slope(0)
        norm_back_into(grad_hidden, state, stream, row(2), sums, 2)
        fetch_stream(layer)
        rounded[...] = state[...].astype(BF)
        point()
        for x in range(4):
            loaded.pop(("out", x)).wait()
            value = dot(rounded[...], tiles_wide[0, :, pl.ds(x * WIDTH, WIDTH)], 1, 1)
            grad_mixed[:, pl.ds(x * 256, 256)] = value.astype(BF)
        tile_qkv(layer, 1)
        ready("qkv")
        ready("probs")
        point()
        for n in range(4):
            attention_backward(qkv, probs, grad_mixed, 2 * n, 2 * n + 2)
            point()
        ready("stream")
        ready("mixed")
        norm_into(hidden, stream, row(0), row(1))
        wide_grads(layer, 0, ((0, 3, hidden, qkv, 0), (3 * WIDTH, 1, mixed, rounded, 0)))
        table = table_grads(probs, bucket_rows[...])
        if layer == 1:
            fetch_probs(0)
            fetch_mixed(0)
        point()
        for x in range(4):
            loaded.pop(("qkv", x)).wait()
            grad_hidden[:, pl.ds(x * 256, 256)] = dot(qkv[...], tiles_wide[1 - x % 2, :, pl.ds(0, 3 * WIDTH)], 1, 1)
            if x < 2:
                tile_qkv(layer, x + 2)
            elif layer == 1:
                tile_up(0, 3 - x)
            if x % 2 == 1:
                point()
        norm_back_into(grad_hidden, state, stream, row(0), sums, 0)
        if layer == 1:
            fetch_qkv(0)
            fetch_mid(0)
        rounded[...] = state[...].astype(BF)
        point()
        shares = share_grads(sums, table).astype(BF)
        chosen = (iota((64, 1024), 1) == iota((64, 1024), 0) * 16 + layer).astype(BF)
        placed = dot(chosen, shares, 0, 0)
        if layer == 1:
            small_total[...] = placed
        else:
            finish = pltpu.make_async_copy(state, o_input, out_sem)
            finish.start()
            total = (small_total[...] + placed).astype(BF)
            mine, other = split_cores(total, core, (4, 2, 4, 2, 16, LANES))
            for i in range(2):
                columns = pl.ds(i * LANES, LANES)
                parts[3][:, :, :, :, columns] = mine
                stage_small[:, :, :, :, columns] = other
            by_name[0, 3].piece(stage_small, lands[2])
        point()
    while points[0] < len(SERVED):
        point()
    finish.wait()


def backward(cotangent, params, bucket_rows, fetched, saved):
    wide, tall = (1024, 4096), (4096, 1024)
    arrays = [fetched[i].reshape(s) for i, s in ((3, wide), (4, wide), (5, tall), (0, wide), (1, wide), (2, tall))]
    vmem = pl.BlockSpec(memory_space=pltpu.VMEM)
    hbm = pl.BlockSpec(memory_space=pl.ANY)
    chains = [c for array in (2, 1, 0) for c in CHAINS[array] if c[0] == array] + [CHAINS[0][3]]
    scratch = [pltpu.VMEM(s, BF) for s in PART_SHAPES]
    scratch += [pltpu.VMEM(PART_SHAPES[i], BF) for i in (2, 1, 3)]
    for chain in chains:
        scratch += [pltpu.VMEM(s, BF) for s in landing_shapes(chain)]
    scratch += [
        pltpu.VMEM((2,) + PART_SHAPES[2][1:], BF),
        pltpu.VMEM((2,) + PART_SHAPES[1][1:], BF),
        pltpu.VMEM(PART_SHAPES[3], BF),
        pltpu.VMEM((4, 512, WIDTH), BF),
        pltpu.VMEM((2, 256, HIDDEN), BF),
        pltpu.VMEM((ROWS, HIDDEN), BF),
        pltpu.VMEM((ROWS, HIDDEN), BF),
        pltpu.VMEM((HEADS, ROWS, ROWS), BF),
        pltpu.VMEM((ROWS, 3 * WIDTH), BF),
        pltpu.VMEM((ROWS, WIDTH), BF),
        pltpu.VMEM((ROWS, WIDTH), BF),
        pltpu.VMEM((ROWS, WIDTH), F32),
        pltpu.VMEM((ROWS, WIDTH), F32),
        pltpu.VMEM((ROWS, WIDTH), BF),
        pltpu.VMEM((ROWS, WIDTH), F32),
        pltpu.VMEM((ROWS, WIDTH), BF),
        pltpu.VMEM((8, WIDTH), F32),
        pltpu.VMEM((1024, LANES), F32),
        pltpu.SemaphoreType.DMA((20, N_SCATTER)),
        pltpu.SemaphoreType.DMA((20, N_SCATTER)),
        pltpu.SemaphoreType.DMA((28,)),
        pltpu.SemaphoreType.DMA((28,)),
        pltpu.SemaphoreType.REGULAR((3,)),
        pltpu.SemaphoreType.REGULAR,
        pltpu.SemaphoreType.DMA((7,)),
        pltpu.SemaphoreType.DMA((10,)),
        pltpu.SemaphoreType.DMA,
    ]
    return pl.pallas_call(
        backward_kernel,
        out_shape=[
            jax.ShapeDtypeStruct((ROWS, WIDTH), F32),
            jax.ShapeDtypeStruct((2, 16, 4096), F32),
            jax.ShapeDtypeStruct((2, 16, 4096), F32),
            jax.ShapeDtypeStruct((2, 64, 1024), F32),
            jax.ShapeDtypeStruct((16, 256), F32),
        ],
        in_specs=[vmem] * 3 + [hbm] * 14,
        out_specs=[hbm] + [vmem] * 4,
        scratch_shapes=scratch,
        compiler_params=pltpu.CompilerParams(
            collective_id=1, has_side_effects=True, vmem_limit_bytes=63 << 20
        ),
        name="backward_scatter",
    )(cotangent, params, bucket_rows, *arrays, *saved)


def on_device(
    tokens,
    seg_ids,
    buckets,
    cotangent,
    ln1_gain,
    ln1_bias,
    w_query,
    w_key,
    w_value,
    w_out,
    rel_table,
    ln2_gain,
    ln2_bias,
    w_up,
    w_down,
):
    small = jnp.concatenate([ln1_gain, ln1_bias, ln2_gain, ln2_bias, rel_table], 1)
    small = jnp.pad(small, ((0, 14), (0, 56)))
    by_offset = jnp.concatenate([buckets[:1], buckets[:0:-1]])
    bucket_rows = (by_offset[None, :] == (jnp.arange(64, dtype=jnp.int32) // 2)[:, None]).astype(BF)
    done = forward(
        jnp.concatenate([w_query, w_key, w_value, w_out], 2),
        w_up,
        w_down,
        jnp.concatenate([small, small], 1),
        tokens,
        seg_ids,
        bucket_rows,
    )
    acts, mid0, mid1, stream, params = done[7:12]
    saved = (stream, mid0, mid1) + tuple(done[12:])
    grad_input, att, up, down, small = backward(cotangent, params, bucket_rows, done[:6], saved)
    return (
        acts,
        grad_input,
        small[:2, 0:16],
        small[:2, 16:32],
        att[:, :, :1024],
        att[:, :, 1024:2048],
        att[:, :, 2048:3072],
        att[:, :, 3072:],
        small[:2, 64:72],
        small[:2, 32:48],
        small[:2, 48:64],
        up,
        down,
    )


def solution(mesh):
    placed = (
        P(("wide", "narrow"), None),
        P(("wide", "narrow")),
        P(),
        P(("wide", "narrow"), None),
        P(None, "wide"),
        P(None, "wide"),
        P(None, "wide", None),
        P(None, "wide", None),
        P(None, "wide", None),
        P(None, "wide", None),
        P(None, "wide"),
        P(None, "wide"),
        P(None, "wide"),
        P(None, "wide", None),
        P(None, "wide", None),
    )
    return jax.shard_map(
        on_device,
        mesh=mesh,
        in_specs=placed,
        out_specs=(
            P(None, ("wide", "narrow"), None),
            P(("wide", "narrow"), None),
            P(None, "wide"),
            P(None, "wide"),
            P(None, "wide", None),
            P(None, "wide", None),
            P(None, "wide", None),
            P(None, "wide", None),
            P(None, "wide"),
            P(None, "wide"),
            P(None, "wide"),
            P(None, "wide", None),
            P(None, "wide", None),
        ),
        check_vma=False,
    )
```

```python
import jax
import jax.numpy as jnp
from jax import lax
from jax.experimental import pallas as pl
from jax.experimental.pallas import tpu as pltpu
from jax.sharding import PartitionSpec as P

MESH = pl.DeviceIdType.MESH
TILE = 128
BF = jnp.bfloat16
F32 = jnp.float32
ORDERS = (("y", "x", "z"), ("z", "y", "x"), ("x", "z", "y"))
CHAINS = (
    ((0, 0, 10, 0), (0, 10, 10, 1), (0, 20, 12, 2), (3, 0, 2, 0)),
    ((1, 0, 10, 0), (1, 10, 10, 1), (1, 20, 12, 2)),
    ((2, 0, 3, 0), (2, 3, 3, 1), (2, 6, 2, 2)),
)


def place():
    wide, narrow = lax.axis_index("wide"), lax.axis_index("narrow")
    return {
        "x": wide // 16,
        "y": narrow * 2 + (wide // 8) % 2,
        "z": (wide // 2) % 4,
        "c": wide % 2,
    }


def device(at):
    return (((at["x"] * 2 + at["y"] % 2) * 4 + at["z"]) * 2 + at["c"], at["y"] // 2)


def moved(at, axis, by):
    new = dict(at)
    new[axis] = (at[axis] + by) % (2 if axis == "c" else 4)
    return new


def pick(ref, chain, sel, lead=()):
    array, tile, tiles, _ = chain
    y = sel["y"]
    columns = pl.ds(tile * TILE, tiles * TILE)
    rows = pl.ds(0, 64 if array == 2 else 16)
    if y is None:
        low = pl.ds(0, 2)
    elif isinstance(y, tuple):
        low = pl.ds(y[0], 1)
    else:
        low = y % 2
        if array == 2:
            rows = pl.ds(pl.multiple_of((y // 2) * 32, 32), 32)
        else:
            half = tiles // 2 * TILE
            columns = pl.ds(pl.multiple_of(tile * TILE + (y // 2) * half, TILE), half)

    def one(v):
        return pl.ds(0, 4) if v is None else v

    index = lead + (one(sel["x"]), low, one(sel["z"]))
    if "c" in sel:
        index = index + (sel["c"],)
    return ref.at[index + (rows, columns)]


def half_of(axis, part):
    return (part,) if axis == "y" else pl.ds(2 * part, 2)


def greet(at, peers):
    barrier = pltpu.get_barrier_semaphore()
    for axis, by in peers:
        pl.semaphore_signal(barrier, inc=1, device_id=device(moved(at, axis, by)), device_id_type=MESH)
    pl.semaphore_wait(barrier, len(peers))


PEERS = tuple((a, b) for a in "xyz" for b in (1, 3, 2)) + (("c", 1),)


class Gather:
    def __init__(self, at, ref, chain, send, recv):
        self.at, self.ref, self.chain, self.send, self.recv = at, ref, chain, send, recv
        self.axes = ORDERS[chain[3]]
        self.count = 0
        self.sent = []

    def place_own(self, mine, sem):
        array, tile, tiles, _ = self.chain
        side = self.at["y"] // 2
        if array == 2:
            where = (pl.ds(pl.multiple_of(side * 32, 32), 32), pl.ds(tile * TILE, tiles * TILE))
        else:
            wide = tiles // 2 * TILE
            where = (slice(None), pl.ds(pl.multiple_of(tile * TILE + side * wide, TILE), wide))
        self.own = pltpu.make_async_copy(mine.at[where], pick(self.ref, self.chain, self.sel(())), sem)
        self.own.start()

    def copy(self, sel, axis, by):
        slot = self.count
        self.count += 1
        block = pick(self.ref, self.chain, sel)
        made = pltpu.make_async_remote_copy(
            src_ref=block,
            dst_ref=block,
            send_sem=self.send.at[slot],
            recv_sem=self.recv.at[slot],
            device_id=device(moved(self.at, axis, by)),
            device_id_type=MESH,
        )
        made.start()
        self.sent.append(made)
        return made

    def sel(self, done, axis=None, by=0, half=None):
        at = {k: self.at[k] for k in "xyzc"}
        for d in done:
            at[d] = None
        if half is not None:
            at[done[0]] = half_of(done[0], half)
        if axis is not None:
            at[axis] = (self.at[axis] + by) % 4
        return at

    def step(self, k):
        a1, a2, a3 = self.axes
        if k == 0:
            self.own.wait()
            own = self.sel(())
            self.first = [self.copy(own, a1, by) for by in (1, 3, 2)]
        elif k in (1, 3):
            done, axis = ((a1,), a2) if k == 1 else ((a1, a2), a3)
            for c in self.first:
                c.wait_recv()
            own = self.sel(done)
            self.pair = [self.copy(own, axis, 1), self.copy(own, axis, 3)]
            if k == 3:
                self.across = [self.copy(own, "c", 1)]
        elif k in (2, 4):
            done, axis = ((a1,), a2) if k == 2 else ((a1, a2), a3)
            self.pair[0].wait_recv()
            forward = self.copy(self.sel(done, axis, 3, 0), axis, 1)
            self.pair[1].wait_recv()
            self.first = [forward, self.copy(self.sel(done, axis, 1, 1), axis, 3)]
            if k == 4:
                for by in (3, 1):
                    self.across.append(self.copy(self.sel(done, axis, by), "c", 1))
        elif k == 5:
            for c in self.first:
                c.wait_recv()
            self.across.append(self.copy(self.sel((a1, a2), a3, 2), "c", 1))
        elif k == 6:
            for c in self.across:
                c.wait_recv()
            for c in self.sent:
                c.wait_send()


N_GATHER = 15


def gather_groups(at, n_layers, mine, fetched, send, recv, local):
    groups = []
    index = 0
    for layer in range(n_layers):
        for group in CHAINS:
            chains = []
            for chain in group:
                array = chain[0]
                if array == 3 and layer > 0:
                    continue
                ref = fetched[3 * n_layers] if array == 3 else fetched[3 * layer + array]
                made = Gather(at, ref, chain, send.at[index], recv.at[index])
                made.place_own(mine[array] if array == 3 else mine[array].at[layer], local.at[index])
                chains.append(made)
                index += 1
            groups.append(chains)
    return groups


N_SCATTER = 12
PART_SHAPES = ((4, 2, 4, 16, 4096), (4, 2, 4, 16, 4096), (4, 2, 4, 64, 1024), (4, 2, 4, 16, 256))


def landing_shapes(chain):
    array, _, tiles, order = chain
    a1, a2, a3 = ORDERS[order]
    rows, cols = (64, tiles * TILE) if array == 2 else (16, tiles * TILE)
    unit = (rows // 2, cols) if array == 2 else (rows, cols // 2)

    def block(full, half=None):
        dims = []
        for axis in "xyz":
            if axis in full:
                size = 2 if axis == "y" else 4
                dims.append(size // 2 if axis == half else size)
        return tuple(dims) + ((rows, cols) if "y" in full else unit)

    return (
        (2,) + block((a1, a2), a1),
        (2,) + block((a1, a2)),
        (2,) + block((a1,), a1),
        (2,) + block((a1,)),
        (3,) + unit,
        unit,
    )


class Scatter:
    def __init__(self, at, part, out, landing, chain, send, recv):
        self.at, self.part, self.out, self.chain = at, part, out, chain
        self.landing, self.send, self.recv = landing, send, recv
        self.axes = ORDERS[chain[3]]
        self.count = 0
        self.sent = []

    def copy(self, src, dst, axis, by):
        slot = self.count
        self.count += 1
        made = pltpu.make_async_remote_copy(
            src_ref=src,
            dst_ref=dst,
            send_sem=self.send.at[slot],
            recv_sem=self.recv.at[slot],
            device_id=device(moved(self.at, axis, by)),
            device_id_type=MESH,
        )
        made.start()
        self.sent.append(made)
        return made

    def sel(self, done, axis=None, by=0, half=None):
        at = {k: self.at[k] for k in "xyz"}
        for d in done:
            at[d] = None
        if half is not None:
            at[done[0]] = half_of(done[0], half)
        if axis is not None:
            at[axis] = (self.at[axis] + by) % 4
        return pick(self.part, self.chain, at)

    def step(self, k):
        a1, a2, a3 = self.axes
        if k in (1, 3):
            done, axis = ((a1, a2), a3) if k == 1 else ((a1,), a2)
            land, blocks = self.landing[k - 1], self.landing[k]
            self.blocks = []
            for i, by in ((0, 1), (1, 3)):
                self.halves[i].wait_recv()
                add_to(self.sel(done, axis, by, i), (land.at[i],))
                self.blocks.append(self.copy(self.sel(done, axis, by), blocks.at[i], axis, by))
        if k in (2, 4):
            done = (a1, a2) if k == 2 else (a1,)
            blocks = self.landing[k - 1]
            for c in self.blocks:
                c.wait_recv()
            add_to(self.sel(done), (blocks.at[0], blocks.at[1]))
        if k in (0, 2):
            done, axis = ((a1, a2), a3) if k == 0 else ((a1,), a2)
            land = self.landing[0 if k == 0 else 2]
            self.halves = [
                self.copy(self.sel(done, axis, 2, 0), land.at[0], axis, 1),
                self.copy(self.sel(done, axis, 2, 1), land.at[1], axis, 3),
            ]
        if k == 4:
            land = self.landing[4]
            self.units = [self.copy(self.sel((), a1, by), land.at[i], a1, by) for i, by in enumerate((1, 3, 2))]
        if k == 5:
            land = self.landing[4]
            for c in self.units:
                c.wait_recv()
            add_to(self.sel(()), (land.at[0], land.at[1], land.at[2]))
            self.last = self.copy(self.sel(()), self.landing[5], "y", 2)
        if k == 6:
            self.last.wait_recv()
            array, tile, tiles, _ = self.chain
            high = self.at["y"] // 2
            for side, ref in ((high, self.sel(())), (1 - high, self.landing[5])):
                if array == 2:
                    where = (pl.ds(pl.multiple_of(side * 32, 32), 32), pl.ds(tile * TILE, tiles * TILE))
                else:
                    wide = tiles // 2 * TILE
                    where = (slice(None), pl.ds(pl.multiple_of(tile * TILE + side * wide, TILE), wide))
                self.out[where] = ref[...].astype(F32)
            for c in self.sent:
                c.wait_send()


def add_to(ref, terms):
    lead = ref.shape[:-2]
    if not lead:
        total = ref[...]
        for t in terms:
            total = total + t[...]
        ref[...] = total
        return
    n = 1
    for d in lead:
        n *= d

    def body(i, _):
        index = []
        rest = i
        for d in reversed(lead):
            index.append(rest % d)
            rest = rest // d
        index = tuple(reversed(index))
        total = ref[index]
        for t in terms:
            total = total + t[index]
        ref[index] = total
        return 0

    lax.fori_loop(0, n, body, 0, unroll=min(n, 8))


FORWARD_SERVED = (
    (0, 1, 2, 3, 0, 1, 2, 3, 0, 1, 2, 3, 0, 4, 1, 5, 2, 3, 0, 4, 1, 5, 2, 3, 0, 4, 0, 1,),
    (1, 5,),
    (2,),
    (),
    (2, 3,),
    (4, 5,),
    (3,),
    (),
    (),
    (),
    (),
    (),
    (),
    (4,),
    (),
    (),
    (),
    (5,),
    (),
    (4,),
    (5, 4, 5,),
    (),
    (),
    (),
    (),
    (),
)


LANES = 128
GELU = 0.7978845608028654
EPSILON = 1e-05
ROWS = 256
WIDTH = 1024
HIDDEN = 4096
HEADS = 16
HEAD = 64
BUCKETS = 32
MASKED = -1e30


def dot(a, b, ca=1, cb=0):
    return lax.dot_general(a, b, (((ca,), (cb,)), ((), ())), preferred_element_type=F32)


def iota(shape, dim):
    return lax.broadcasted_iota(jnp.int32, shape, dim)


def param_rows(small, layer):
    flat = small[...].reshape(1024, 256)[:, :128]
    chosen = (iota((64, 1024), 1) == iota((64, 1024), 0) * 16 + layer).astype(BF)
    shares = dot(chosen, flat).astype(BF)
    owner = iota((64, 1024), 0) == iota((64, 1024), 1) // 16
    rows = []
    for k in range(4):
        spread = (iota((128, 1024), 0) == 16 * k + iota((128, 1024), 1) % 16).astype(BF)
        rows.append(jnp.sum(jnp.where(owner, dot(shares, spread), 0.0), 0, keepdims=True))
    return rows, shares


def bias_rows(shares, bucket_rows):
    picked = (iota((16, 128), 1) == 64 + iota((16, 128), 0) % 8).astype(BF)
    entries = dot(picked, shares, 1, 1)
    entries = jnp.where(iota((16, 64), 1) % 2 == iota((16, 64), 0) // 8, entries, 0.0).astype(BF)
    return dot(entries, bucket_rows)


def norm_parts(rows):
    center = jnp.mean(rows, -1, keepdims=True)
    centered = rows - center
    inverse = lax.rsqrt(jnp.mean(centered * centered, -1, keepdims=True) + EPSILON)
    return centered * inverse, inverse


def norm_into(dst, src, gain, shift):
    def body(i, _):
        at = pl.ds(pl.multiple_of(i * 128, 128), 128)
        normed, _unused = norm_parts(src[at, :])
        dst[at, :] = (normed * gain[...] + shift[...]).astype(BF)
        return 0

    lax.fori_loop(0, ROWS // 128, body, 0, unroll=True)


def transpose_into(dst, src):
    for i in range(WIDTH // 256):
        dst[pl.ds(i * 256, 256), :] = src[:, pl.ds(i * 256, 256)].T


def attention_forward(qkv, probs, mixed, mixed_t, bias, allowed, start, stop):
    scale = HEAD ** (-0.5)
    low = iota((ROWS, LANES), 1) < HEAD

    def pair(i, _):
        def columns(k):
            return pl.ds(pl.multiple_of(k * WIDTH + i * LANES, LANES), LANES)

        q, k, v = (qkv[:, columns(j)] for j in range(3))
        halves = []
        for side in range(2):
            head = 2 * i + side
            mine = jnp.where(low == (side == 0), q, jnp.zeros_like(q))
            scores = dot(mine, k, 1, 1) * scale
            first = bias[head]
            shifted = jnp.concatenate([first] + [pltpu.roll(first, 16 * b, 1) for b in range(1, 16)], 0)
            scores = jnp.where(allowed[...] > 0, scores + shifted, MASKED)
            peak = jnp.max(scores, -1, keepdims=True)
            terms = jnp.exp(scores - peak)
            rounded = (terms / jnp.sum(terms, -1, keepdims=True)).astype(BF)
            probs[head] = rounded
            halves.append(dot(rounded, v))
        at = pl.ds(pl.multiple_of(i * LANES, LANES), LANES)
        both = jnp.where(low, halves[0], halves[1]).astype(BF)
        mixed[:, at] = both
        mixed_t[at, :] = both.T
        return 0

    lax.fori_loop(start, stop, pair, 0, unroll=True)


def forward_kernel(att, up, down, small, tokens, seg_col, seg_row, bucket_rows, *rest):
    outs, rest = rest[:18], rest[18:]
    fetched = outs[:7]
    o_acts, o_mid0, o_mid1, o_stream, o_params, o_qkv, o_probs, o_mixed, o_active, o_slope, o_hidden = outs[7:]
    (w_att, w_up, w_down, w_small, stream, middle, hidden, hidden_t, qkv, probs, mixed, mixed_t, active, active_t, slope, rounded,
     bias, allowed, params, send, recv, local, loads, stores) = rest
    at = place()
    greet(at, PEERS)
    groups = gather_groups(at, 2, (att, up, down, small), fetched, send, recv, local)
    buffers = (w_att, w_up, w_down)
    served = [0] * 6
    arrived, used, waiting = set(), set(), {}
    stored = []
    points = [0]

    def store(src, dst):
        made = pltpu.make_async_copy(src, dst, stores.at[len(stored)])
        made.start()
        stored.append(made)

    def load(g):
        if g in arrived and g not in waiting and (g < 3 or g - 3 in used):
            waiting[g] = pltpu.make_async_copy(fetched[g], buffers[g % 3], loads.at[g])
            waiting[g].start()

    def serve(g):
        for chain in groups[g]:
            chain.step(served[g])
        served[g] += 1
        if served[g] == 7:
            arrived.add(g)
            load(g)
            if g == 0:
                waiting[6] = pltpu.make_async_copy(fetched[6], w_small, loads.at[6])
                waiting[6].start()

    def point():
        for g in FORWARD_SERVED[points[0]]:
            serve(g)
        points[0] += 1

    def need(g):
        point()
        waiting[g].wait()

    def done(g):
        used.add(g)
        if g < 3:
            load(g + 3)

    same = (seg_col[...] == seg_row[...]) & (iota((ROWS, ROWS), 0) >= iota((ROWS, ROWS), 1))
    allowed[...] = same.astype(F32)
    stream[0] = tokens[...].astype(F32)
    for layer in range(2):
        need(3 * layer)
        if layer == 0:
            waiting[6].wait()
        rows, shares = param_rows(w_small, layer)
        for k in range(4):
            params[layer, pl.ds(k, 1), :] = rows[k]
        by_offset = bias_rows(shares, bucket_rows[...])
        for head in range(HEADS):
            wide = jnp.broadcast_to(by_offset[head : head + 1], (16, ROWS))
            bias[head] = pltpu.roll(wide, 0, 1, stride=1, stride_axis=0)
        here, mid = stream.at[layer], middle.at[layer]
        row = lambda k: params.at[layer, pl.ds(k, 1), :]
        norm_into(hidden, here, row(0), row(1))
        transpose_into(hidden_t.at[layer, 0], hidden)
        store(hidden_t.at[layer, 0], o_hidden.at[layer, 0])
        wide_qkv, wide_probs, wide_mixed = qkv.at[layer], probs.at[layer], mixed_t.at[layer]
        wide_active, wide_slope = active_t.at[layer], slope.at[layer]

        def project(i, _):
            cols = pl.ds(pl.multiple_of(i * 512, 512), 512)
            weights = w_att[:, :, :, :, :, cols].reshape(WIDTH, 512)
            wide_qkv[:, cols] = dot(hidden[...], weights).astype(BF)
            return 0

        point()
        lax.fori_loop(0, 6, project, 0, unroll=True)
        for n in range(4):
            point()
            attention_forward(wide_qkv, wide_probs, mixed, wide_mixed, bias, allowed, 2 * n, 2 * n + 2)

        def out_project(i, _):
            cols = pl.ds(pl.multiple_of(i * 512, 512), 512)
            from_cols = pl.ds(pl.multiple_of(3072 + i * 512, 512), 512)
            weights = w_att[:, :, :, :, :, from_cols].reshape(WIDTH, 512)
            mid[:, cols] = here[:, cols] + dot(mixed[...], weights)
            return 0

        point()
        lax.fori_loop(0, 2, out_project, 0, unroll=True)
        done(3 * layer)
        norm_into(hidden, mid, row(2), row(3))
        transpose_into(hidden_t.at[layer, 1], hidden)
        store(hidden_t.at[layer, 1], o_hidden.at[layer, 1])
        store(wide_qkv, o_qkv.at[layer])
        store(wide_probs, o_probs.at[layer])
        store(wide_mixed, o_mixed.at[layer])
        store(mid, (o_mid0, o_mid1)[layer])
        need(3 * layer + 1)

        def expand(i, _):
            cols = pl.ds(pl.multiple_of(i * 512, 512), 512)
            weights = w_up[:, :, :, :, :, cols].reshape(WIDTH, 512)
            u = dot(hidden[...], weights)
            square = u * u
            tangent = jnp.tanh(GELU * (u + 0.044715 * square * u))
            value = (0.5 * u * (1.0 + tangent)).astype(BF)
            active[:, cols] = value
            wide_active[cols, :] = value.T
            wide_slope[:, cols] = (
                0.5 * (1.0 + tangent)
                + 0.5 * u * (1.0 - tangent * tangent) * GELU * (1.0 + 3.0 * 0.044715 * square)
            ).astype(BF)
            return 0

        for n in range(4):
            if n > 0:
                point()
            lax.fori_loop(2 * n, 2 * n + 2, expand, 0, unroll=True)
        done(3 * layer + 1)
        store(wide_active, o_active.at[layer])
        store(wide_slope, o_slope.at[layer])
        need(3 * layer + 2)
        acts = rounded.at[layer]

        def contract(i, _):
            cols = pl.ds(pl.multiple_of(i * 256, 256), 256)
            weights = w_down[:, :, :, :, :, cols].reshape(HIDDEN, 256)
            result = mid[:, cols] + dot(active[...], weights)
            if layer == 0:
                stream[1, :, cols] = result
            acts[:, cols] = result.astype(BF)
            return 0

        lax.fori_loop(0, 2, contract, 0, unroll=True)
        point()
        lax.fori_loop(2, 4, contract, 0, unroll=True)
        done(3 * layer + 2)
        store(acts, o_acts.at[layer])
    store(stream, o_stream)
    store(params, o_params)
    for made in stored:
        made.wait()


def forward(att, up, down, small, tokens, seg_ids, bucket_rows):
    lead = (4, 2, 4, 2)
    gathered = [lead + (16, 4096), lead + (16, 4096), lead + (64, 1024)] * 2 + [lead + (16, 256)]
    saved = [
        ((2, ROWS, WIDTH), BF),
        ((ROWS, WIDTH), F32),
        ((ROWS, WIDTH), F32),
        ((2, ROWS, WIDTH), F32),
        ((2, 8, WIDTH), F32),
        ((2, ROWS, 3 * WIDTH), BF),
        ((2, HEADS, ROWS, ROWS), BF),
        ((2, WIDTH, ROWS), BF),
        ((2, HIDDEN, ROWS), BF),
        ((2, ROWS, HIDDEN), BF),
        ((2, 2, WIDTH, ROWS), BF),
    ]
    vmem = pl.BlockSpec(memory_space=pltpu.VMEM)
    hbm = pl.BlockSpec(memory_space=pl.ANY)
    return pl.pallas_call(
        forward_kernel,
        out_shape=[jax.ShapeDtypeStruct(s, BF) for s in gathered] + [jax.ShapeDtypeStruct(s, t) for s, t in saved],
        in_specs=[vmem] * 8,
        out_specs=[hbm] * 18,
        scratch_shapes=[
            pltpu.VMEM(gathered[0], BF),
            pltpu.VMEM(gathered[1], BF),
            pltpu.VMEM(gathered[2], BF),
            pltpu.VMEM(gathered[6], BF),
            pltpu.VMEM((2, ROWS, WIDTH), F32),
            pltpu.VMEM((2, ROWS, WIDTH), F32),
            pltpu.VMEM((ROWS, WIDTH), BF),
            pltpu.VMEM((2, 2, WIDTH, ROWS), BF),
            pltpu.VMEM((2, ROWS, 3 * WIDTH), BF),
            pltpu.VMEM((2, HEADS, ROWS, ROWS), BF),
            pltpu.VMEM((ROWS, WIDTH), BF),
            pltpu.VMEM((2, WIDTH, ROWS), BF),
            pltpu.VMEM((ROWS, HIDDEN), BF),
            pltpu.VMEM((2, HIDDEN, ROWS), BF),
            pltpu.VMEM((2, ROWS, HIDDEN), BF),
            pltpu.VMEM((2, ROWS, WIDTH), BF),
            pltpu.VMEM((HEADS, 16, ROWS), F32),
            pltpu.VMEM((ROWS, ROWS), F32),
            pltpu.VMEM((2, 8, WIDTH), F32),
            pltpu.SemaphoreType.DMA((19, N_GATHER)),
            pltpu.SemaphoreType.DMA((19, N_GATHER)),
            pltpu.SemaphoreType.DMA((19,)),
            pltpu.SemaphoreType.DMA((7,)),
            pltpu.SemaphoreType.DMA((20,)),
        ],
        compiler_params=pltpu.CompilerParams(
            collective_id=0, has_side_effects=True, vmem_limit_bytes=58 << 20
        ),
        name="gather_forward",
    )(att, up, down, small, tokens, seg_ids[:, None], seg_ids[None, :], bucket_rows)


SERVED = (
    (),
    (),
    (),
    (),
    (0,),
    (0, 0,),
    (0, 0,),
    (),
    (),
    (1,),
    (1,),
    (0, 1, 1, 1,),
    (),
    (),
    (),
    (),
    (),
    (0,),
    (),
    (),
    (1,),
    (0, 2,),
    (2,),
    (2,),
    (2, 2,),
    (),
    (1, 0, 2, 1, 0, 2, 1, 0,),
    (),
    (2,),
    (1,),
    (3,),
    (2, 1, 3, 3,),
    (2, 3, 3,),
    (),
    (),
    (2,),
    (4,),
    (3, 4, 4,),
    (4, 4,),
    (),
    (),
    (),
    (),
    (3,),
    (4,),
    (3,),
    (),
    (),
    (5,),
    (5,),
    (5,),
    (5, 5, 4,),
    (3,),
    (),
    (5, 6, 6, 4, 3, 5, 6, 4, 3, 5, 6, 4, 5, 6, 4, 5, 6, 5, 6, 6,),
)


def split_cores(value, core, shape):
    both = value.reshape(shape)
    axis = len(shape) - 3
    even, odd = (lax.index_in_dim(both, i, axis, keepdims=False) for i in range(2))
    mine = core == 0
    return jnp.where(mine, even, odd), jnp.where(mine, odd, even)


def norm_back_into(grad, dst, src, gain, sums, base):
    def body(i, carry):
        by_gain, by_shift = carry
        at = pl.ds(pl.multiple_of(i * 128, 128), 128)
        normed, inverse = norm_parts(src[at, :])
        value = grad[at, :]
        scaled = value * gain[...]
        dst[at, :] = dst[at, :] + inverse * (
            scaled
            - jnp.mean(scaled, -1, keepdims=True)
            - normed * jnp.mean(scaled * normed, -1, keepdims=True)
        )
        by_gain = by_gain + jnp.sum(value * normed, 0, keepdims=True)
        return by_gain, by_shift + jnp.sum(value, 0, keepdims=True)

    zero = jnp.zeros((1, WIDTH), F32)
    by_gain, by_shift = lax.fori_loop(0, ROWS // 128, body, (zero, zero), unroll=True)
    sums[pl.ds(base, 1), :] = by_gain
    sums[pl.ds(base + 1, 1), :] = by_shift


def attention_backward(qkv, probs, grad_mixed, first, last):
    scale = HEAD ** (-0.5)
    low = iota((ROWS, LANES), 1) < HEAD

    def pair(i, _):
        def columns(k):
            return pl.ds(pl.multiple_of(k * WIDTH + i * LANES, LANES), LANES)

        q, k, v = (qkv[:, columns(j)] for j in range(3))
        grad = grad_mixed[:, pl.ds(pl.multiple_of(i * LANES, LANES), LANES)]
        grads = []
        for side in range(2):
            head = 2 * i + side
            rounded = probs[head]
            prob = rounded.astype(F32)
            mine = jnp.where(low == (side == 0), grad, jnp.zeros_like(grad))
            grad_probs = dot(mine, v, 1, 1)
            inner = jnp.sum(prob * grad_probs, -1, keepdims=True)
            grad_scores = (prob * (grad_probs - inner)).astype(BF)
            probs[head] = grad_scores
            grads.append(
                (dot(grad_scores, k) * scale, dot(grad_scores, q, 0, 0) * scale, dot(rounded, grad, 0, 0))
            )
        for j in range(3):
            qkv[:, columns(j)] = jnp.where(low, grads[0][j], grads[1][j]).astype(BF)
        return 0

    lax.fori_loop(first, last, pair, 0, unroll=True)


def table_grads(grad_scores, bucket_rows):
    total = jnp.zeros((HEADS, 16, ROWS), F32)
    for b in range(15, -1, -1):
        if b < 15:
            total = pltpu.roll(total, ROWS - 16, 2)
        total = total + grad_scores[:, pl.ds(16 * b, 16), :].astype(F32)
    line = iota((HEADS, 16, ROWS), 1)
    for bit in (1, 2, 4, 8):
        total = jnp.where((line // bit) % 2 == 1, pltpu.roll(total, ROWS - bit, 2), total)
    by_offset = jnp.sum(total, 1)
    high = by_offset.astype(BF)
    rest = (by_offset - high.astype(F32)).astype(BF)
    return dot(high, bucket_rows, 1, 1) + dot(rest, bucket_rows, 1, 1)


def share_grads(sums, table):
    owner = iota((64, 1024), 0) == iota((64, 1024), 1) // 16
    shares = jnp.zeros((64, 128), F32)
    for k in range(4):
        spread = (iota((128, 1024), 0) == 16 * k + iota((128, 1024), 1) % 16).astype(BF)
        mine = jnp.where(owner, sums[pl.ds(k, 1), :], 0.0).astype(BF)
        shares = shares + dot(mine, spread, 1, 1)
    picked = (iota((16, 128), 1) == 64 + iota((16, 128), 0) % 8).astype(BF)
    entries = jnp.where(iota((16, 64), 1) % 2 == iota((16, 64), 0) // 8, table, 0.0).astype(BF)
    return shares + dot(entries, picked, 0, 0)


def backward_kernel(*refs):
    (cotangent, params, bucket_rows, att1, up1, down1, att0, up0, down0,
     h_stream, h_mid0, h_mid1, h_qkv, h_probs, h_mixed, h_active, h_slope, h_hidden) = refs[:18]
    o_input, o_att, o_up, o_down, o_small = refs[18:23]
    rest = refs[23:]
    parts, lands, rest = rest[:4], rest[4:7], rest[7:]
    landings, rest = rest[:60], rest[60:]
    (stage_down, stage_wide, stage_small, tiles_down, tiles_wide, active, slope, probs, qkv, mixed, grad_mixed,
     state, stream, hidden, grad_hidden, rounded, sums, small_total,
     send, recv, across_s, across_r, free, free_land, loads, tile_sems, out_sem) = rest
    weights = ((att0, up0, down0), (att1, up1, down1))
    middles = (h_mid0, h_mid1)
    at = place()
    core = at["c"]
    partner = device(moved(at, "c", 1))
    greet(at, PEERS)

    pending = {}

    def fetch(name, i, src, dst):
        made = pltpu.make_async_copy(src, dst, loads.at[i])
        made.start()
        pending[name] = made

    def ready(name):
        pending.pop(name).wait()

    def fetch_active(layer):
        fetch("active", 0, h_active.at[layer], active)

    def fetch_slope(layer):
        fetch("slope", 1, h_slope.at[layer], slope)

    def fetch_mid(layer):
        fetch("mid", 2, middles[layer], stream)

    def fetch_stream(layer):
        fetch("stream", 3, h_stream.at[layer], stream)

    def fetch_probs(layer):
        fetch("probs", 4, h_probs.at[layer], probs)

    def fetch_qkv(layer):
        fetch("qkv", 5, h_qkv.at[layer], qkv)

    def fetch_mixed(layer):
        fetch("mixed", 6, h_mixed.at[layer], mixed)

    def fetch_hidden(layer, which):
        fetch("hidden", 7, h_hidden.at[layer, which], hidden)

    chains_of = {array: [c for c in CHAINS[array] if c[0] == array] for array in range(3)}
    small_chain = CHAINS[0][3]
    numbers = {}
    for array in (2, 1, 0):
        for chain in chains_of[array]:
            numbers[chain] = len(numbers)
    numbers[small_chain] = 9
    land_of = (lands[1], lands[1], lands[0], lands[2])
    outs = (o_att, o_up, o_down, o_small)

    class Group:
        def __init__(self, layer, array):
            self.layer, self.array = layer, array
            self.turn = 3 * (1 - layer) + (2 - array) if array < 3 else 6
            self.pieces = []
            self.served = 0
            todo = [small_chain] if array == 3 else chains_of[array]
            self.chains = []
            for chain in todo:
                n = numbers[chain]
                out = outs[array] if array == 3 else outs[array].at[layer]
                sems = n if array == 3 else n + 10 * (1 - layer)
                self.chains.append(
                    Scatter(at, parts[array], out, landings[6 * n : 6 * n + 6], chain, send.at[sems], recv.at[sems])
                )

        def admit(self):
            if self.array < 3 and self.layer == 0:
                pl.semaphore_wait(free.at[self.array], len(PEERS))
            if self.array in (0, 1) and (self.layer, self.array) != (1, 1):
                pl.semaphore_wait(free_land, 1)

        def piece(self, src, dst):
            n = 4 * self.turn + len(self.pieces)
            made = pltpu.make_async_remote_copy(
                src_ref=src,
                dst_ref=dst,
                send_sem=across_s.at[n],
                recv_sem=across_r.at[n],
                device_id=partner,
                device_id_type=MESH,
            )
            made.start()
            self.pieces.append(made)

        def add_piece(self, x):
            part, land = parts[self.array], land_of[self.array]
            self.pieces[x].wait_recv()
            if self.array == 3:
                add_to(part, (land,))
            else:
                add_to(part.at[x], (land.at[x],))
            if x == len(self.pieces) - 1:
                if self.array in (0, 1) and (self.layer, self.array) != (0, 0):
                    pl.semaphore_signal(free_land, inc=1, device_id=partner, device_id_type=MESH)
                for made in self.pieces[-2:]:
                    made.wait_send()

        def serve(self):
            pieces = 1 if self.array == 3 else 4
            k = self.served - pieces
            self.served += 1
            if k < 0:
                self.add_piece(k + pieces)
                return
            for chain in self.chains:
                chain.step(k)
            if k == 6 and self.layer == 1 and self.array < 3:
                for axis, by in PEERS:
                    pl.semaphore_signal(
                        free.at[self.array], inc=1, device_id=device(moved(at, axis, by)), device_id_type=MESH
                    )

    order = [(layer, array) for layer in (1, 0) for array in (2, 1, 0)] + [(0, 3)]
    groups = [Group(layer, array) for layer, array in order]
    by_name = dict(zip(order, groups))
    points = [0]

    def point():
        for g in SERVED[points[0]] if points[0] < len(SERVED) else ():
            groups[g].serve()
        points[0] += 1

    loaded = {}

    def tile_down(layer, i):
        rows = pl.ds(i * 512, 512)
        made = pltpu.make_async_copy(weights[layer][2].at[rows], tiles_down.at[i % 3], tile_sems.at[i % 3])
        made.start()
        loaded["down", i] = made

    def tile_wide(layer, array, x, slot, start, size, at_column, sem):
        made = pltpu.make_async_copy(
            weights[layer][array].at[pl.ds(x * 256, 256), pl.ds(start, size)],
            tiles_wide.at[slot, :, pl.ds(at_column, size)],
            tile_sems.at[sem],
        )
        made.start()
        return made

    def tile_up(layer, x):
        loaded["up", x] = tile_wide(layer, 1, x, x % 2, 0, HIDDEN, 0, 4 + x % 2)

    def tile_out(layer, x):
        loaded["out", x] = tile_wide(layer, 0, x, 0, 3 * WIDTH, WIDTH, x * WIDTH, 6 + x)

    def tile_qkv(layer, x):
        loaded["qkv", x] = tile_wide(layer, 0, x, 1 - x % 2, 0, 3 * WIDTH, 0, 5 - x % 2)

    def down_grads(layer):
        group = by_name[layer, 2]
        group.admit()
        for x in range(4):
            slot = x % 2
            if x >= 2:
                group.pieces[x - 2].wait_send()

            def body(j, _):
                low, pairs = j // 2, j % 2
                at_rows = pl.ds(pl.multiple_of((4 * x + j) * 256, 256), 256)
                value = dot(active[at_rows, :], rounded[...]).astype(BF)
                mine, other = split_cores(value, core, (2, 2, 64, WIDTH))
                parts[2][x, low, pl.ds(2 * pairs, 2)] = mine
                stage_down[slot, low, pl.ds(2 * pairs, 2)] = other
                return 0

            lax.fori_loop(0, 4, body, 0, unroll=True)
            group.piece(stage_down.at[slot], lands[0].at[x])
            point()

    def wide_grads(layer, array, terms):
        group = by_name[layer, array]
        group.admit()
        part = parts[array]
        for x in range(4):
            slot = x % 2
            if x >= 2:
                group.pieces[x - 2].wait_send()
            for start, count, left, right, skip in terms:

                def body(j, _):
                    to = pl.ds(pl.multiple_of(start + j * 1024, 1024), 1024)
                    frm = pl.ds(pl.multiple_of(skip + j * 1024, 1024), 1024)
                    value = dot(left[pl.ds(256 * x, 256), :], right[:, frm]).astype(BF)
                    mine, other = split_cores(value, core, (2, 4, 2, 16, 1024))
                    part[x, :, :, :, to] = mine
                    stage_wide[slot, :, :, :, to] = other
                    return 0

                lax.fori_loop(0, count, body, 0, unroll=True)
            group.piece(stage_wide.at[slot], lands[1].at[x])
            point()

    for i in range(3):
        tile_down(1, i)
    fetch_active(1)
    fetch_slope(1)
    for x in range(2):
        tile_up(1, x)
    fetch_hidden(1, 1)
    fetch_mid(1)
    fetch_probs(1)
    fetch_qkv(1)
    fetch_mixed(1)
    state[...] = cotangent[...].astype(F32)
    rounded[...] = cotangent[...]
    for layer in (1, 0):
        row = lambda k: params.at[layer, pl.ds(k, 1), :]
        ready("active")
        down_grads(layer)
        if layer == 1:
            fetch_active(0)
        ready("slope")
        for half in range(2):
            for j in range(4):
                i = 4 * half + j
                loaded.pop(("down", i)).wait()
                columns = pl.ds(i * 512, 512)
                value = dot(rounded[...], tiles_down[i % 3], 1, 1)
                slope[:, columns] = (value * slope[:, columns].astype(F32)).astype(BF)
                if i + 3 < 8:
                    tile_down(layer, i + 3)
                elif layer == 1:
                    tile_down(0, i % 3)
            point()
        ready("mid")
        ready("hidden")
        wide_grads(layer, 1, ((0, 4, hidden, slope, 0),))
        fetch_hidden(layer, 0)
        for x in range(4):
            loaded.pop(("up", x)).wait()
            grad_hidden[:, pl.ds(x * 256, 256)] = dot(slope[...], tiles_wide[x % 2], 1, 1)
            if x < 2:
                tile_up(layer, x + 2)
            elif x == 2:
                for n in range(4):
                    tile_out(layer, n)
            else:
                tile_qkv(layer, 0)
            if x % 2 == 1:
                point()
        if layer == 1:
            fetch_slope(0)
        norm_back_into(grad_hidden, state, stream, row(2), sums, 2)
        fetch_stream(layer)
        rounded[...] = state[...].astype(BF)
        point()
        for x in range(4):
            loaded.pop(("out", x)).wait()
            value = dot(rounded[...], tiles_wide[0, :, pl.ds(x * WIDTH, WIDTH)], 1, 1)
            grad_mixed[:, pl.ds(x * 256, 256)] = value.astype(BF)
        tile_qkv(layer, 1)
        ready("qkv")
        ready("probs")
        point()
        for n in range(4):
            attention_backward(qkv, probs, grad_mixed, 2 * n, 2 * n + 2)
            point()
        ready("stream")
        ready("mixed")
        ready("hidden")
        wide_grads(layer, 0, ((0, 3, hidden, qkv, 0), (3 * WIDTH, 1, mixed, rounded, 0)))
        table = table_grads(probs, bucket_rows[...])
        if layer == 1:
            fetch_hidden(0, 1)
            fetch_probs(0)
            fetch_mixed(0)
        point()
        for x in range(4):
            loaded.pop(("qkv", x)).wait()
            grad_hidden[:, pl.ds(x * 256, 256)] = dot(qkv[...], tiles_wide[1 - x % 2, :, pl.ds(0, 3 * WIDTH)], 1, 1)
            if x < 2:
                tile_qkv(layer, x + 2)
            elif layer == 1:
                tile_up(0, 3 - x)
            if x % 2 == 1:
                point()
        norm_back_into(grad_hidden, state, stream, row(0), sums, 0)
        if layer == 1:
            fetch_qkv(0)
            fetch_mid(0)
        rounded[...] = state[...].astype(BF)
        point()
        shares = share_grads(sums, table).astype(BF)
        chosen = (iota((64, 1024), 1) == iota((64, 1024), 0) * 16 + layer).astype(BF)
        placed = dot(chosen, shares, 0, 0)
        if layer == 1:
            small_total[...] = placed
        else:
            finish = pltpu.make_async_copy(state, o_input, out_sem)
            finish.start()
            total = (small_total[...] + placed).astype(BF)
            mine, other = split_cores(total, core, (4, 2, 4, 2, 16, LANES))
            for i in range(2):
                columns = pl.ds(i * LANES, LANES)
                parts[3][:, :, :, :, columns] = mine
                stage_small[:, :, :, :, columns] = other
            by_name[0, 3].piece(stage_small, lands[2])
        point()
    while points[0] < len(SERVED):
        point()
    finish.wait()


def backward(cotangent, params, bucket_rows, fetched, saved):
    wide, tall = (1024, 4096), (4096, 1024)
    arrays = [fetched[i].reshape(s) for i, s in ((3, wide), (4, wide), (5, tall), (0, wide), (1, wide), (2, tall))]
    vmem = pl.BlockSpec(memory_space=pltpu.VMEM)
    hbm = pl.BlockSpec(memory_space=pl.ANY)
    chains = [c for array in (2, 1, 0) for c in CHAINS[array] if c[0] == array] + [CHAINS[0][3]]
    scratch = [pltpu.VMEM(s, BF) for s in PART_SHAPES]
    scratch += [pltpu.VMEM(PART_SHAPES[i], BF) for i in (2, 1, 3)]
    for chain in chains:
        scratch += [pltpu.VMEM(s, BF) for s in landing_shapes(chain)]
    scratch += [
        pltpu.VMEM((2,) + PART_SHAPES[2][1:], BF),
        pltpu.VMEM((2,) + PART_SHAPES[1][1:], BF),
        pltpu.VMEM(PART_SHAPES[3], BF),
        pltpu.VMEM((3, 512, WIDTH), BF),
        pltpu.VMEM((2, 256, HIDDEN), BF),
        pltpu.VMEM((HIDDEN, ROWS), BF),
        pltpu.VMEM((ROWS, HIDDEN), BF),
        pltpu.VMEM((HEADS, ROWS, ROWS), BF),
        pltpu.VMEM((ROWS, 3 * WIDTH), BF),
        pltpu.VMEM((WIDTH, ROWS), BF),
        pltpu.VMEM((ROWS, WIDTH), BF),
        pltpu.VMEM((ROWS, WIDTH), F32),
        pltpu.VMEM((ROWS, WIDTH), F32),
        pltpu.VMEM((WIDTH, ROWS), BF),
        pltpu.VMEM((ROWS, WIDTH), F32),
        pltpu.VMEM((ROWS, WIDTH), BF),
        pltpu.VMEM((8, WIDTH), F32),
        pltpu.VMEM((1024, LANES), F32),
        pltpu.SemaphoreType.DMA((20, N_SCATTER)),
        pltpu.SemaphoreType.DMA((20, N_SCATTER)),
        pltpu.SemaphoreType.DMA((28,)),
        pltpu.SemaphoreType.DMA((28,)),
        pltpu.SemaphoreType.REGULAR((3,)),
        pltpu.SemaphoreType.REGULAR,
        pltpu.SemaphoreType.DMA((8,)),
        pltpu.SemaphoreType.DMA((10,)),
        pltpu.SemaphoreType.DMA,
    ]
    return pl.pallas_call(
        backward_kernel,
        out_shape=[
            jax.ShapeDtypeStruct((ROWS, WIDTH), F32),
            jax.ShapeDtypeStruct((2, 16, 4096), F32),
            jax.ShapeDtypeStruct((2, 16, 4096), F32),
            jax.ShapeDtypeStruct((2, 64, 1024), F32),
            jax.ShapeDtypeStruct((16, 256), F32),
        ],
        in_specs=[vmem] * 3 + [hbm] * 15,
        out_specs=[hbm] + [vmem] * 4,
        scratch_shapes=scratch,
        compiler_params=pltpu.CompilerParams(
            collective_id=1, has_side_effects=True, vmem_limit_bytes=63 << 20
        ),
        name="backward_scatter",
    )(cotangent, params, bucket_rows, *arrays, *saved)


def on_device(
    tokens,
    seg_ids,
    buckets,
    cotangent,
    ln1_gain,
    ln1_bias,
    w_query,
    w_key,
    w_value,
    w_out,
    rel_table,
    ln2_gain,
    ln2_bias,
    w_up,
    w_down,
):
    small = jnp.concatenate([ln1_gain, ln1_bias, ln2_gain, ln2_bias, rel_table], 1)
    small = jnp.pad(small, ((0, 14), (0, 56)))
    by_offset = jnp.concatenate([buckets[:1], buckets[:0:-1]])
    bucket_rows = (by_offset[None, :] == (jnp.arange(64, dtype=jnp.int32) // 2)[:, None]).astype(BF)
    done = forward(
        jnp.concatenate([w_query, w_key, w_value, w_out], 2),
        w_up,
        w_down,
        jnp.concatenate([small, small], 1),
        tokens,
        seg_ids,
        bucket_rows,
    )
    acts, mid0, mid1, stream, params = done[7:12]
    saved = (stream, mid0, mid1) + tuple(done[12:])
    grad_input, att, up, down, small = backward(cotangent, params, bucket_rows, done[:6], saved)
    return (
        acts,
        grad_input,
        small[:2, 0:16],
        small[:2, 16:32],
        att[:, :, :1024],
        att[:, :, 1024:2048],
        att[:, :, 2048:3072],
        att[:, :, 3072:],
        small[:2, 64:72],
        small[:2, 32:48],
        small[:2, 48:64],
        up,
        down,
    )


def solution(mesh):
    placed = (
        P(("wide", "narrow"), None),
        P(("wide", "narrow")),
        P(),
        P(("wide", "narrow"), None),
        P(None, "wide"),
        P(None, "wide"),
        P(None, "wide", None),
        P(None, "wide", None),
        P(None, "wide", None),
        P(None, "wide", None),
        P(None, "wide"),
        P(None, "wide"),
        P(None, "wide"),
        P(None, "wide", None),
        P(None, "wide", None),
    )
    return jax.shard_map(
        on_device,
        mesh=mesh,
        in_specs=placed,
        out_specs=(
            P(None, ("wide", "narrow"), None),
            P(("wide", "narrow"), None),
            P(None, "wide"),
            P(None, "wide"),
            P(None, "wide", None),
            P(None, "wide", None),
            P(None, "wide", None),
            P(None, "wide", None),
            P(None, "wide"),
            P(None, "wide"),
            P(None, "wide"),
            P(None, "wide", None),
            P(None, "wide", None),
        ),
        check_vma=False,
    )
```

```python
import jax
import jax.numpy as jnp
from jax import lax
from jax.experimental import pallas as pl
from jax.experimental.pallas import tpu as pltpu
from jax.sharding import PartitionSpec as P

MESH = pl.DeviceIdType.MESH
TILE = 128
BF = jnp.bfloat16
F32 = jnp.float32
ORDERS = (("y", "x", "z"), ("z", "y", "x"), ("x", "z", "y"))
CHAINS = (
    ((0, 0, 10, 0), (0, 10, 10, 1), (0, 20, 12, 2), (3, 0, 2, 0)),
    ((1, 0, 10, 0), (1, 10, 10, 1), (1, 20, 12, 2)),
    ((2, 0, 3, 0), (2, 3, 3, 1), (2, 6, 2, 2)),
)


def place():
    wide, narrow = lax.axis_index("wide"), lax.axis_index("narrow")
    return {
        "x": wide // 16,
        "y": narrow * 2 + (wide // 8) % 2,
        "z": (wide // 2) % 4,
        "c": wide % 2,
    }


def device(at):
    return (((at["x"] * 2 + at["y"] % 2) * 4 + at["z"]) * 2 + at["c"], at["y"] // 2)


def moved(at, axis, by):
    new = dict(at)
    new[axis] = (at[axis] + by) % (2 if axis == "c" else 4)
    return new


def pick(ref, chain, sel, lead=()):
    array, tile, tiles, _ = chain
    y = sel["y"]
    columns = pl.ds(tile * TILE, tiles * TILE)
    rows = pl.ds(0, 64 if array == 2 else 16)
    if y is None:
        low = pl.ds(0, 2)
    elif isinstance(y, tuple):
        low = pl.ds(y[0], 1)
    else:
        low = y % 2
        if array == 2:
            rows = pl.ds(pl.multiple_of((y // 2) * 32, 32), 32)
        else:
            half = tiles // 2 * TILE
            columns = pl.ds(pl.multiple_of(tile * TILE + (y // 2) * half, TILE), half)

    def one(v):
        return pl.ds(0, 4) if v is None else v

    index = lead + (one(sel["x"]), low, one(sel["z"]))
    if "c" in sel:
        index = index + (sel["c"],)
    return ref.at[index + (rows, columns)]


def half_of(axis, part):
    return (part,) if axis == "y" else pl.ds(2 * part, 2)


def greet(at, peers):
    barrier = pltpu.get_barrier_semaphore()
    for axis, by in peers:
        pl.semaphore_signal(barrier, inc=1, device_id=device(moved(at, axis, by)), device_id_type=MESH)
    pl.semaphore_wait(barrier, len(peers))


PEERS = tuple((a, b) for a in "xyz" for b in (1, 3, 2)) + (("c", 1),)


class Gather:
    def __init__(self, at, ref, chain, send, recv):
        self.at, self.ref, self.chain, self.send, self.recv = at, ref, chain, send, recv
        self.axes = ORDERS[chain[3]]
        self.count = 0
        self.sent = []

    def place_own(self, mine, sem):
        array, tile, tiles, _ = self.chain
        side = self.at["y"] // 2
        if array == 2:
            where = (pl.ds(pl.multiple_of(side * 32, 32), 32), pl.ds(tile * TILE, tiles * TILE))
        else:
            wide = tiles // 2 * TILE
            where = (slice(None), pl.ds(pl.multiple_of(tile * TILE + side * wide, TILE), wide))
        self.own = pltpu.make_async_copy(mine.at[where], pick(self.ref, self.chain, self.sel(())), sem)
        self.own.start()

    def copy(self, sel, axis, by):
        slot = self.count
        self.count += 1
        block = pick(self.ref, self.chain, sel)
        made = pltpu.make_async_remote_copy(
            src_ref=block,
            dst_ref=block,
            send_sem=self.send.at[slot],
            recv_sem=self.recv.at[slot],
            device_id=device(moved(self.at, axis, by)),
            device_id_type=MESH,
        )
        made.start()
        self.sent.append(made)
        return made

    def sel(self, done, axis=None, by=0, half=None):
        at = {k: self.at[k] for k in "xyzc"}
        for d in done:
            at[d] = None
        if half is not None:
            at[done[0]] = half_of(done[0], half)
        if axis is not None:
            at[axis] = (self.at[axis] + by) % 4
        return at

    def step(self, k):
        a1, a2, a3 = self.axes
        if k == 0:
            self.own.wait()
            own = self.sel(())
            self.first = [self.copy(own, a1, by) for by in (1, 3, 2)]
        elif k in (1, 3):
            done, axis = ((a1,), a2) if k == 1 else ((a1, a2), a3)
            for c in self.first:
                c.wait_recv()
            own = self.sel(done)
            self.pair = [self.copy(own, axis, 1), self.copy(own, axis, 3)]
            if k == 3:
                self.across = [self.copy(own, "c", 1)]
        elif k in (2, 4):
            done, axis = ((a1,), a2) if k == 2 else ((a1, a2), a3)
            self.pair[0].wait_recv()
            forward = self.copy(self.sel(done, axis, 3, 0), axis, 1)
            self.pair[1].wait_recv()
            self.first = [forward, self.copy(self.sel(done, axis, 1, 1), axis, 3)]
            if k == 4:
                for by in (3, 1):
                    self.across.append(self.copy(self.sel(done, axis, by), "c", 1))
        elif k == 5:
            for c in self.first:
                c.wait_recv()
            self.across.append(self.copy(self.sel((a1, a2), a3, 2), "c", 1))
        elif k == 6:
            for c in self.across:
                c.wait_recv()
            for c in self.sent:
                c.wait_send()


N_GATHER = 15


def gather_groups(at, n_layers, mine, fetched, send, recv, local):
    groups = []
    index = 0
    for layer in range(n_layers):
        for group in CHAINS:
            chains = []
            for chain in group:
                array = chain[0]
                if array == 3 and layer > 0:
                    continue
                ref = fetched[3 * n_layers] if array == 3 else fetched[3 * layer + array]
                made = Gather(at, ref, chain, send.at[index], recv.at[index])
                made.place_own(mine[array] if array == 3 else mine[array].at[layer], local.at[index])
                chains.append(made)
                index += 1
            groups.append(chains)
    return groups


N_SCATTER = 12
PART_SHAPES = ((4, 2, 4, 16, 4096), (4, 2, 4, 16, 4096), (4, 2, 4, 64, 1024), (4, 2, 4, 16, 256))


def landing_shapes(chain):
    array, _, tiles, order = chain
    a1, a2, a3 = ORDERS[order]
    rows, cols = (64, tiles * TILE) if array == 2 else (16, tiles * TILE)
    unit = (rows // 2, cols) if array == 2 else (rows, cols // 2)

    def block(full, half=None):
        dims = []
        for axis in "xyz":
            if axis in full:
                size = 2 if axis == "y" else 4
                dims.append(size // 2 if axis == half else size)
        return tuple(dims) + ((rows, cols) if "y" in full else unit)

    return (
        (2,) + block((a1, a2), a1),
        (2,) + block((a1, a2)),
        (2,) + block((a1,), a1),
        (2,) + block((a1,)),
        (3,) + unit,
        unit,
    )


class Scatter:
    def __init__(self, at, part, out, landing, chain, send, recv):
        self.at, self.part, self.out, self.chain = at, part, out, chain
        self.landing, self.send, self.recv = landing, send, recv
        self.axes = ORDERS[chain[3]]
        self.count = 0
        self.sent = []

    def copy(self, src, dst, axis, by):
        slot = self.count
        self.count += 1
        made = pltpu.make_async_remote_copy(
            src_ref=src,
            dst_ref=dst,
            send_sem=self.send.at[slot],
            recv_sem=self.recv.at[slot],
            device_id=device(moved(self.at, axis, by)),
            device_id_type=MESH,
        )
        made.start()
        self.sent.append(made)
        return made

    def sel(self, done, axis=None, by=0, half=None):
        at = {k: self.at[k] for k in "xyz"}
        for d in done:
            at[d] = None
        if half is not None:
            at[done[0]] = half_of(done[0], half)
        if axis is not None:
            at[axis] = (self.at[axis] + by) % 4
        return pick(self.part, self.chain, at)

    def step(self, k):
        a1, a2, a3 = self.axes
        if k in (1, 3):
            done, axis = ((a1, a2), a3) if k == 1 else ((a1,), a2)
            land, blocks = self.landing[k - 1], self.landing[k]
            self.blocks = []
            for i, by in ((0, 1), (1, 3)):
                self.halves[i].wait_recv()
                add_to(self.sel(done, axis, by, i), (land.at[i],))
                self.blocks.append(self.copy(self.sel(done, axis, by), blocks.at[i], axis, by))
        if k in (2, 4):
            done = (a1, a2) if k == 2 else (a1,)
            blocks = self.landing[k - 1]
            for c in self.blocks:
                c.wait_recv()
            add_to(self.sel(done), (blocks.at[0], blocks.at[1]))
        if k in (0, 2):
            done, axis = ((a1, a2), a3) if k == 0 else ((a1,), a2)
            land = self.landing[0 if k == 0 else 2]
            self.halves = [
                self.copy(self.sel(done, axis, 2, 0), land.at[0], axis, 1),
                self.copy(self.sel(done, axis, 2, 1), land.at[1], axis, 3),
            ]
        if k == 4:
            land = self.landing[4]
            self.units = [self.copy(self.sel((), a1, by), land.at[i], a1, by) for i, by in enumerate((1, 3, 2))]
        if k == 5:
            land = self.landing[4]
            for c in self.units:
                c.wait_recv()
            add_to(self.sel(()), (land.at[0], land.at[1], land.at[2]))
            self.last = self.copy(self.sel(()), self.landing[5], "y", 2)
        if k == 6:
            self.last.wait_recv()
            array, tile, tiles, _ = self.chain
            high = self.at["y"] // 2
            for side, ref in ((high, self.sel(())), (1 - high, self.landing[5])):
                if array == 2:
                    where = (pl.ds(pl.multiple_of(side * 32, 32), 32), pl.ds(tile * TILE, tiles * TILE))
                else:
                    wide = tiles // 2 * TILE
                    where = (slice(None), pl.ds(pl.multiple_of(tile * TILE + side * wide, TILE), wide))
                self.out[where] = ref[...].astype(F32)
            for c in self.sent:
                c.wait_send()


def add_to(ref, terms):
    lead = ref.shape[:-2]
    if not lead:
        total = ref[...]
        for t in terms:
            total = total + t[...]
        ref[...] = total
        return
    n = 1
    for d in lead:
        n *= d

    def body(i, _):
        index = []
        rest = i
        for d in reversed(lead):
            index.append(rest % d)
            rest = rest // d
        index = tuple(reversed(index))
        total = ref[index]
        for t in terms:
            total = total + t[index]
        ref[index] = total
        return 0

    lax.fori_loop(0, n, body, 0, unroll=min(n, 8))


FORWARD_SERVED = (
    (0, 1, 2, 3, 0, 1, 2, 3, 0, 1, 2, 3, 0, 4, 1, 5, 2, 3, 0, 4, 1, 5, 2, 3, 0, 4, 0, 1,),
    (1, 5,),
    (2,),
    (),
    (2, 3,),
    (4, 5,),
    (3,),
    (),
    (),
    (),
    (),
    (),
    (),
    (4,),
    (),
    (),
    (),
    (5,),
    (),
    (4,),
    (5, 4, 5,),
    (),
    (),
    (),
    (),
    (),
)


LANES = 128
GELU = 0.7978845608028654
EPSILON = 1e-05
ROWS = 256
WIDTH = 1024
HIDDEN = 4096
HEADS = 16
HEAD = 64
BUCKETS = 32
MASKED = -1e30


def dot(a, b, ca=1, cb=0):
    return lax.dot_general(a, b, (((ca,), (cb,)), ((), ())), preferred_element_type=F32)


def iota(shape, dim):
    return lax.broadcasted_iota(jnp.int32, shape, dim)


def param_rows(small, layer):
    flat = small[...].reshape(1024, 256)[:, :128]
    chosen = (iota((64, 1024), 1) == iota((64, 1024), 0) * 16 + layer).astype(BF)
    shares = dot(chosen, flat).astype(BF)
    owner = iota((64, 1024), 0) == iota((64, 1024), 1) // 16
    rows = []
    for k in range(4):
        spread = (iota((128, 1024), 0) == 16 * k + iota((128, 1024), 1) % 16).astype(BF)
        rows.append(jnp.sum(jnp.where(owner, dot(shares, spread), 0.0), 0, keepdims=True))
    return rows, shares


def by_offset_of(bucket_rows):
    turn = ((iota((ROWS, ROWS), 0) + iota((ROWS, ROWS), 1)) % ROWS == 0).astype(BF)
    return dot(bucket_rows, turn).astype(BF)


def bias_rows(shares, bucket_rows):
    picked = (iota((16, 128), 1) == 64 + iota((16, 128), 0) % 8).astype(BF)
    entries = dot(picked, shares, 1, 1)
    entries = jnp.where(iota((16, 64), 1) % 2 == iota((16, 64), 0) // 8, entries, 0.0).astype(BF)
    return dot(entries, bucket_rows)


def norm_parts(rows):
    center = jnp.mean(rows, -1, keepdims=True)
    centered = rows - center
    inverse = lax.rsqrt(jnp.mean(centered * centered, -1, keepdims=True) + EPSILON)
    return centered * inverse, inverse


def norm_into(dst, src, gain, shift):
    def body(i, _):
        at = pl.ds(pl.multiple_of(i * 128, 128), 128)
        normed, _unused = norm_parts(src[at, :])
        dst[at, :] = (normed * gain[...] + shift[...]).astype(BF)
        return 0

    lax.fori_loop(0, ROWS // 128, body, 0, unroll=True)


def transpose_into(dst, src):
    for i in range(WIDTH // 256):
        dst[pl.ds(i * 256, 256), :] = src[:, pl.ds(i * 256, 256)].T


def attention_forward(qkv, probs, mixed, mixed_t, bias, allowed, start, stop):
    scale = HEAD ** (-0.5)
    low = iota((ROWS, LANES), 1) < HEAD

    def pair(i, _):
        def columns(k):
            return pl.ds(pl.multiple_of(k * WIDTH + i * LANES, LANES), LANES)

        q, k, v = (qkv[:, columns(j)] for j in range(3))
        halves = []
        for side in range(2):
            head = 2 * i + side
            mine = jnp.where(low == (side == 0), q, jnp.zeros_like(q))
            scores = dot(mine, k, 1, 1) * scale
            first = bias[head]
            shifted = jnp.concatenate([first] + [pltpu.roll(first, 16 * b, 1) for b in range(1, 16)], 0)
            scores = jnp.where(allowed[...] > 0, scores + shifted, MASKED)
            peak = jnp.max(scores, -1, keepdims=True)
            terms = jnp.exp(scores - peak)
            rounded = (terms / jnp.sum(terms, -1, keepdims=True)).astype(BF)
            probs[head] = rounded
            halves.append(dot(rounded, v))
        at = pl.ds(pl.multiple_of(i * LANES, LANES), LANES)
        both = jnp.where(low, halves[0], halves[1]).astype(BF)
        mixed[:, at] = both
        mixed_t[at, :] = both.T
        return 0

    lax.fori_loop(start, stop, pair, 0, unroll=True)


def forward_kernel(att, up, down, small, tokens, seg_row, bucket_rows, *rest):
    outs, rest = rest[:18], rest[18:]
    fetched = outs[:7]
    o_acts, o_mid0, o_mid1, o_stream, o_params, o_qkv, o_probs, o_mixed, o_active, o_slope, o_hidden = outs[7:]
    (w_att, w_up, w_down, w_small, stream, middle, hidden, hidden_t, qkv, probs, mixed, mixed_t, active, active_t, slope, rounded,
     bias, allowed, params, send, recv, local, loads, stores) = rest
    at = place()
    greet(at, PEERS)
    groups = gather_groups(at, 2, (att, up, down, small), fetched, send, recv, local)
    buffers = (w_att, w_up, w_down)
    served = [0] * 6
    arrived, used, waiting = set(), set(), {}
    stored = []
    points = [0]

    def store(src, dst):
        made = pltpu.make_async_copy(src, dst, stores.at[len(stored)])
        made.start()
        stored.append(made)

    def load(g):
        if g in arrived and g not in waiting and (g < 3 or g - 3 in used):
            waiting[g] = pltpu.make_async_copy(fetched[g], buffers[g % 3], loads.at[g])
            waiting[g].start()

    def serve(g):
        for chain in groups[g]:
            chain.step(served[g])
        served[g] += 1
        if served[g] == 7:
            arrived.add(g)
            load(g)
            if g == 0:
                waiting[6] = pltpu.make_async_copy(fetched[6], w_small, loads.at[6])
                waiting[6].start()

    def point():
        for g in FORWARD_SERVED[points[0]]:
            serve(g)
        points[0] += 1

    def need(g):
        point()
        waiting[g].wait()

    def done(g):
        used.add(g)
        if g < 3:
            load(g + 3)

    ids = jnp.broadcast_to(seg_row[...].astype(F32), (ROWS, ROWS))
    same = (ids.T == ids) & (iota((ROWS, ROWS), 0) >= iota((ROWS, ROWS), 1))
    allowed[...] = same.astype(F32)
    stream[0] = tokens[...].astype(F32)
    for layer in range(2):
        need(3 * layer)
        if layer == 0:
            waiting[6].wait()
        rows, shares = param_rows(w_small, layer)
        for k in range(4):
            params[layer, pl.ds(k, 1), :] = rows[k]
        by_offset = bias_rows(shares, by_offset_of(bucket_rows[...]))
        for head in range(HEADS):
            wide = jnp.broadcast_to(by_offset[head : head + 1], (16, ROWS))
            bias[head] = pltpu.roll(wide, 0, 1, stride=1, stride_axis=0)
        here, mid = stream.at[layer], middle.at[layer]
        row = lambda k: params.at[layer, pl.ds(k, 1), :]
        norm_into(hidden, here, row(0), row(1))
        transpose_into(hidden_t.at[layer, 0], hidden)
        store(hidden_t.at[layer, 0], o_hidden.at[layer, 0])
        wide_qkv, wide_probs, wide_mixed = qkv.at[layer], probs.at[layer], mixed_t.at[layer]
        wide_active, wide_slope = active_t.at[layer], slope.at[layer]

        def project(i, _):
            cols = pl.ds(pl.multiple_of(i * 512, 512), 512)
            weights = w_att[:, :, :, :, :, cols].reshape(WIDTH, 512)
            wide_qkv[:, cols] = dot(hidden[...], weights).astype(BF)
            return 0

        point()
        lax.fori_loop(0, 6, project, 0, unroll=True)
        for n in range(4):
            point()
            attention_forward(wide_qkv, wide_probs, mixed, wide_mixed, bias, allowed, 2 * n, 2 * n + 2)

        def out_project(i, _):
            cols = pl.ds(pl.multiple_of(i * 512, 512), 512)
            from_cols = pl.ds(pl.multiple_of(3072 + i * 512, 512), 512)
            weights = w_att[:, :, :, :, :, from_cols].reshape(WIDTH, 512)
            mid[:, cols] = here[:, cols] + dot(mixed[...], weights)
            return 0

        point()
        lax.fori_loop(0, 2, out_project, 0, unroll=True)
        done(3 * layer)
        norm_into(hidden, mid, row(2), row(3))
        transpose_into(hidden_t.at[layer, 1], hidden)
        store(hidden_t.at[layer, 1], o_hidden.at[layer, 1])
        store(wide_qkv, o_qkv.at[layer])
        store(wide_probs, o_probs.at[layer])
        store(wide_mixed, o_mixed.at[layer])
        store(mid, (o_mid0, o_mid1)[layer])
        need(3 * layer + 1)

        def expand(i, _):
            cols = pl.ds(pl.multiple_of(i * 512, 512), 512)
            weights = w_up[:, :, :, :, :, cols].reshape(WIDTH, 512)
            u = dot(hidden[...], weights)
            square = u * u
            tangent = jnp.tanh(GELU * (u + 0.044715 * square * u))
            value = (0.5 * u * (1.0 + tangent)).astype(BF)
            active[:, cols] = value
            wide_active[cols, :] = value.T
            wide_slope[:, cols] = (
                0.5 * (1.0 + tangent)
                + 0.5 * u * (1.0 - tangent * tangent) * GELU * (1.0 + 3.0 * 0.044715 * square)
            ).astype(BF)
            return 0

        for n in range(4):
            if n > 0:
                point()
            lax.fori_loop(2 * n, 2 * n + 2, expand, 0, unroll=True)
        done(3 * layer + 1)
        store(wide_active, o_active.at[layer])
        store(wide_slope, o_slope.at[layer])
        need(3 * layer + 2)
        acts = rounded.at[layer]

        def contract(i, _):
            cols = pl.ds(pl.multiple_of(i * 256, 256), 256)
            weights = w_down[:, :, :, :, :, cols].reshape(HIDDEN, 256)
            result = mid[:, cols] + dot(active[...], weights)
            if layer == 0:
                stream[1, :, cols] = result
            acts[:, cols] = result.astype(BF)
            return 0

        lax.fori_loop(0, 2, contract, 0, unroll=True)
        point()
        lax.fori_loop(2, 4, contract, 0, unroll=True)
        done(3 * layer + 2)
        store(acts, o_acts.at[layer])
    store(stream, o_stream)
    store(params, o_params)
    for made in stored:
        made.wait()


def forward(att, up, down, small, tokens, seg_ids, bucket_rows):
    lead = (4, 2, 4, 2)
    gathered = [lead + (16, 4096), lead + (16, 4096), lead + (64, 1024)] * 2 + [lead + (16, 256)]
    saved = [
        ((2, ROWS, WIDTH), BF),
        ((ROWS, WIDTH), F32),
        ((ROWS, WIDTH), F32),
        ((2, ROWS, WIDTH), F32),
        ((2, 8, WIDTH), F32),
        ((2, ROWS, 3 * WIDTH), BF),
        ((2, HEADS, ROWS, ROWS), BF),
        ((2, WIDTH, ROWS), BF),
        ((2, HIDDEN, ROWS), BF),
        ((2, ROWS, HIDDEN), BF),
        ((2, 2, WIDTH, ROWS), BF),
    ]
    vmem = pl.BlockSpec(memory_space=pltpu.VMEM)
    hbm = pl.BlockSpec(memory_space=pl.ANY)
    return pl.pallas_call(
        forward_kernel,
        out_shape=[jax.ShapeDtypeStruct(s, BF) for s in gathered] + [jax.ShapeDtypeStruct(s, t) for s, t in saved],
        in_specs=[vmem] * 7,
        out_specs=[hbm] * 18,
        scratch_shapes=[
            pltpu.VMEM(gathered[0], BF),
            pltpu.VMEM(gathered[1], BF),
            pltpu.VMEM(gathered[2], BF),
            pltpu.VMEM(gathered[6], BF),
            pltpu.VMEM((2, ROWS, WIDTH), F32),
            pltpu.VMEM((2, ROWS, WIDTH), F32),
            pltpu.VMEM((ROWS, WIDTH), BF),
            pltpu.VMEM((2, 2, WIDTH, ROWS), BF),
            pltpu.VMEM((2, ROWS, 3 * WIDTH), BF),
            pltpu.VMEM((2, HEADS, ROWS, ROWS), BF),
            pltpu.VMEM((ROWS, WIDTH), BF),
            pltpu.VMEM((2, WIDTH, ROWS), BF),
            pltpu.VMEM((ROWS, HIDDEN), BF),
            pltpu.VMEM((2, HIDDEN, ROWS), BF),
            pltpu.VMEM((2, ROWS, HIDDEN), BF),
            pltpu.VMEM((2, ROWS, WIDTH), BF),
            pltpu.VMEM((HEADS, 16, ROWS), F32),
            pltpu.VMEM((ROWS, ROWS), F32),
            pltpu.VMEM((2, 8, WIDTH), F32),
            pltpu.SemaphoreType.DMA((19, N_GATHER)),
            pltpu.SemaphoreType.DMA((19, N_GATHER)),
            pltpu.SemaphoreType.DMA((19,)),
            pltpu.SemaphoreType.DMA((7,)),
            pltpu.SemaphoreType.DMA((20,)),
        ],
        compiler_params=pltpu.CompilerParams(
            collective_id=0, has_side_effects=True, vmem_limit_bytes=58 << 20
        ),
        name="gather_forward",
    )(att, up, down, small, tokens, seg_ids[None, :], bucket_rows)


SERVED = (
    (),
    (),
    (),
    (),
    (0,),
    (0, 0,),
    (0, 0,),
    (),
    (),
    (1,),
    (1,),
    (0, 1, 1, 1,),
    (),
    (),
    (),
    (),
    (),
    (0,),
    (),
    (),
    (1,),
    (0, 2,),
    (2,),
    (2,),
    (2, 2,),
    (),
    (1, 0, 2, 1, 0, 2, 1, 0,),
    (),
    (2,),
    (1,),
    (3,),
    (2, 1, 3, 3,),
    (2, 3, 3,),
    (),
    (),
    (2,),
    (4,),
    (3, 4, 4,),
    (4, 4,),
    (),
    (),
    (),
    (),
    (3,),
    (4,),
    (3,),
    (),
    (),
    (5,),
    (5,),
    (5,),
    (5, 5, 4,),
    (3,),
    (),
    (5, 6, 6, 4, 3, 5, 6, 4, 3, 5, 6, 4, 5, 6, 4, 5, 6, 5, 6, 6,),
)


def split_cores(value, core, shape):
    both = value.reshape(shape)
    axis = len(shape) - 3
    even, odd = (lax.index_in_dim(both, i, axis, keepdims=False) for i in range(2))
    mine = core == 0
    return jnp.where(mine, even, odd), jnp.where(mine, odd, even)


def norm_back_into(grad, dst, src, gain, sums, base):
    def body(i, carry):
        by_gain, by_shift = carry
        at = pl.ds(pl.multiple_of(i * 128, 128), 128)
        normed, inverse = norm_parts(src[at, :])
        value = grad[at, :]
        scaled = value * gain[...]
        dst[at, :] = dst[at, :] + inverse * (
            scaled
            - jnp.mean(scaled, -1, keepdims=True)
            - normed * jnp.mean(scaled * normed, -1, keepdims=True)
        )
        by_gain = by_gain + jnp.sum(value * normed, 0, keepdims=True)
        return by_gain, by_shift + jnp.sum(value, 0, keepdims=True)

    zero = jnp.zeros((1, WIDTH), F32)
    by_gain, by_shift = lax.fori_loop(0, ROWS // 128, body, (zero, zero), unroll=True)
    sums[pl.ds(base, 1), :] = by_gain
    sums[pl.ds(base + 1, 1), :] = by_shift


def attention_backward(qkv, probs, grad_mixed, first, last):
    scale = HEAD ** (-0.5)
    low = iota((ROWS, LANES), 1) < HEAD

    def pair(i, _):
        def columns(k):
            return pl.ds(pl.multiple_of(k * WIDTH + i * LANES, LANES), LANES)

        q, k, v = (qkv[:, columns(j)] for j in range(3))
        grad = grad_mixed[:, pl.ds(pl.multiple_of(i * LANES, LANES), LANES)]
        grads = []
        for side in range(2):
            head = 2 * i + side
            rounded = probs[head]
            prob = rounded.astype(F32)
            mine = jnp.where(low == (side == 0), grad, jnp.zeros_like(grad))
            grad_probs = dot(mine, v, 1, 1)
            inner = jnp.sum(prob * grad_probs, -1, keepdims=True)
            grad_scores = (prob * (grad_probs - inner)).astype(BF)
            probs[head] = grad_scores
            grads.append(
                (dot(grad_scores, k) * scale, dot(grad_scores, q, 0, 0) * scale, dot(rounded, grad, 0, 0))
            )
        for j in range(3):
            qkv[:, columns(j)] = jnp.where(low, grads[0][j], grads[1][j]).astype(BF)
        return 0

    lax.fori_loop(first, last, pair, 0, unroll=True)


def table_grads(grad_scores, bucket_rows):
    total = jnp.zeros((HEADS, 16, ROWS), F32)
    for b in range(15, -1, -1):
        if b < 15:
            total = pltpu.roll(total, ROWS - 16, 2)
        total = total + grad_scores[:, pl.ds(16 * b, 16), :].astype(F32)
    line = iota((HEADS, 16, ROWS), 1)
    for bit in (1, 2, 4, 8):
        total = jnp.where((line // bit) % 2 == 1, pltpu.roll(total, ROWS - bit, 2), total)
    by_offset = jnp.sum(total, 1)
    high = by_offset.astype(BF)
    rest = (by_offset - high.astype(F32)).astype(BF)
    return dot(high, bucket_rows, 1, 1) + dot(rest, bucket_rows, 1, 1)


def share_grads(sums, table):
    owner = iota((64, 1024), 0) == iota((64, 1024), 1) // 16
    shares = jnp.zeros((64, 128), F32)
    for k in range(4):
        spread = (iota((128, 1024), 0) == 16 * k + iota((128, 1024), 1) % 16).astype(BF)
        mine = jnp.where(owner, sums[pl.ds(k, 1), :], 0.0).astype(BF)
        shares = shares + dot(mine, spread, 1, 1)
    picked = (iota((16, 128), 1) == 64 + iota((16, 128), 0) % 8).astype(BF)
    entries = jnp.where(iota((16, 64), 1) % 2 == iota((16, 64), 0) // 8, table, 0.0).astype(BF)
    return shares + dot(entries, picked, 0, 0)


def backward_kernel(*refs):
    (cotangent, params, bucket_rows, att1, up1, down1, att0, up0, down0,
     h_stream, h_mid0, h_mid1, h_qkv, h_probs, h_mixed, h_active, h_slope, h_hidden) = refs[:18]
    o_input, o_att, o_up, o_down, o_small = refs[18:23]
    rest = refs[23:]
    parts, lands, rest = rest[:4], rest[4:7], rest[7:]
    landings, rest = rest[:60], rest[60:]
    (stage_down, stage_wide, stage_small, tiles_down, tiles_wide, active, slope, probs, qkv, mixed, grad_mixed,
     state, stream, hidden, grad_hidden, rounded, sums, small_total,
     send, recv, across_s, across_r, free, free_land, loads, tile_sems, out_sem) = rest
    weights = ((att0, up0, down0), (att1, up1, down1))
    middles = (h_mid0, h_mid1)
    at = place()
    core = at["c"]
    partner = device(moved(at, "c", 1))
    greet(at, PEERS)

    pending = {}

    def fetch(name, i, src, dst):
        made = pltpu.make_async_copy(src, dst, loads.at[i])
        made.start()
        pending[name] = made

    def ready(name):
        pending.pop(name).wait()

    def fetch_active(layer):
        fetch("active", 0, h_active.at[layer], active)

    def fetch_slope(layer):
        fetch("slope", 1, h_slope.at[layer], slope)

    def fetch_mid(layer):
        fetch("mid", 2, middles[layer], stream)

    def fetch_stream(layer):
        fetch("stream", 3, h_stream.at[layer], stream)

    def fetch_probs(layer):
        fetch("probs", 4, h_probs.at[layer], probs)

    def fetch_qkv(layer):
        fetch("qkv", 5, h_qkv.at[layer], qkv)

    def fetch_mixed(layer):
        fetch("mixed", 6, h_mixed.at[layer], mixed)

    def fetch_hidden(layer, which):
        fetch("hidden", 7, h_hidden.at[layer, which], hidden)

    chains_of = {array: [c for c in CHAINS[array] if c[0] == array] for array in range(3)}
    small_chain = CHAINS[0][3]
    numbers = {}
    for array in (2, 1, 0):
        for chain in chains_of[array]:
            numbers[chain] = len(numbers)
    numbers[small_chain] = 9
    land_of = (lands[1], lands[1], lands[0], lands[2])
    outs = (o_att, o_up, o_down, o_small)

    class Group:
        def __init__(self, layer, array):
            self.layer, self.array = layer, array
            self.turn = 3 * (1 - layer) + (2 - array) if array < 3 else 6
            self.pieces = []
            self.served = 0
            todo = [small_chain] if array == 3 else chains_of[array]
            self.chains = []
            for chain in todo:
                n = numbers[chain]
                out = outs[array] if array == 3 else outs[array].at[layer]
                sems = n if array == 3 else n + 10 * (1 - layer)
                self.chains.append(
                    Scatter(at, parts[array], out, landings[6 * n : 6 * n + 6], chain, send.at[sems], recv.at[sems])
                )

        def admit(self):
            if self.array < 3 and self.layer == 0:
                pl.semaphore_wait(free.at[self.array], len(PEERS))
            if self.array in (0, 1) and (self.layer, self.array) != (1, 1):
                pl.semaphore_wait(free_land, 1)

        def piece(self, src, dst):
            n = 4 * self.turn + len(self.pieces)
            made = pltpu.make_async_remote_copy(
                src_ref=src,
                dst_ref=dst,
                send_sem=across_s.at[n],
                recv_sem=across_r.at[n],
                device_id=partner,
                device_id_type=MESH,
            )
            made.start()
            self.pieces.append(made)

        def add_piece(self, x):
            part, land = parts[self.array], land_of[self.array]
            self.pieces[x].wait_recv()
            if self.array == 3:
                add_to(part, (land,))
            else:
                add_to(part.at[x], (land.at[x],))
            if x == len(self.pieces) - 1:
                if self.array in (0, 1) and (self.layer, self.array) != (0, 0):
                    pl.semaphore_signal(free_land, inc=1, device_id=partner, device_id_type=MESH)
                for made in self.pieces[-2:]:
                    made.wait_send()

        def serve(self):
            pieces = 1 if self.array == 3 else 4
            k = self.served - pieces
            self.served += 1
            if k < 0:
                self.add_piece(k + pieces)
                return
            for chain in self.chains:
                chain.step(k)
            if k == 6 and self.layer == 1 and self.array < 3:
                for axis, by in PEERS:
                    pl.semaphore_signal(
                        free.at[self.array], inc=1, device_id=device(moved(at, axis, by)), device_id_type=MESH
                    )

    order = [(layer, array) for layer in (1, 0) for array in (2, 1, 0)] + [(0, 3)]
    groups = [Group(layer, array) for layer, array in order]
    by_name = dict(zip(order, groups))
    points = [0]

    def point():
        for g in SERVED[points[0]] if points[0] < len(SERVED) else ():
            groups[g].serve()
        points[0] += 1

    loaded = {}

    def tile_down(layer, i):
        rows = pl.ds(i * 512, 512)
        made = pltpu.make_async_copy(weights[layer][2].at[rows], tiles_down.at[i % 3], tile_sems.at[i % 3])
        made.start()
        loaded["down", i] = made

    def tile_wide(layer, array, x, slot, start, size, at_column, sem):
        made = pltpu.make_async_copy(
            weights[layer][array].at[pl.ds(x * 256, 256), pl.ds(start, size)],
            tiles_wide.at[slot, :, pl.ds(at_column, size)],
            tile_sems.at[sem],
        )
        made.start()
        return made

    def tile_up(layer, x):
        loaded["up", x] = tile_wide(layer, 1, x, x % 2, 0, HIDDEN, 0, 4 + x % 2)

    def tile_out(layer, x):
        loaded["out", x] = tile_wide(layer, 0, x, 0, 3 * WIDTH, WIDTH, x * WIDTH, 6 + x)

    def tile_qkv(layer, x):
        loaded["qkv", x] = tile_wide(layer, 0, x, 1 - x % 2, 0, 3 * WIDTH, 0, 5 - x % 2)

    def down_grads(layer):
        group = by_name[layer, 2]
        group.admit()
        for x in range(4):
            slot = x % 2
            if x >= 2:
                group.pieces[x - 2].wait_send()

            def body(j, _):
                low, pairs = j // 2, j % 2
                at_rows = pl.ds(pl.multiple_of((4 * x + j) * 256, 256), 256)
                value = dot(active[at_rows, :], rounded[...]).astype(BF)
                mine, other = split_cores(value, core, (2, 2, 64, WIDTH))
                parts[2][x, low, pl.ds(2 * pairs, 2)] = mine
                stage_down[slot, low, pl.ds(2 * pairs, 2)] = other
                return 0

            lax.fori_loop(0, 4, body, 0, unroll=True)
            group.piece(stage_down.at[slot], lands[0].at[x])
            point()

    def wide_grads(layer, array, terms):
        group = by_name[layer, array]
        group.admit()
        part = parts[array]
        for x in range(4):
            slot = x % 2
            if x >= 2:
                group.pieces[x - 2].wait_send()
            for start, count, left, right, skip in terms:

                def body(j, _):
                    to = pl.ds(pl.multiple_of(start + j * 1024, 1024), 1024)
                    frm = pl.ds(pl.multiple_of(skip + j * 1024, 1024), 1024)
                    value = dot(left[pl.ds(256 * x, 256), :], right[:, frm]).astype(BF)
                    mine, other = split_cores(value, core, (2, 4, 2, 16, 1024))
                    part[x, :, :, :, to] = mine
                    stage_wide[slot, :, :, :, to] = other
                    return 0

                lax.fori_loop(0, count, body, 0, unroll=True)
            group.piece(stage_wide.at[slot], lands[1].at[x])
            point()

    fetch_active(1)
    for i in range(3):
        tile_down(1, i)
    fetch_slope(1)
    for x in range(2):
        tile_up(1, x)
    fetch_hidden(1, 1)
    fetch_mid(1)
    fetch_probs(1)
    fetch_qkv(1)
    fetch_mixed(1)
    state[...] = cotangent[...].astype(F32)
    rounded[...] = cotangent[...]
    for layer in (1, 0):
        row = lambda k: params.at[layer, pl.ds(k, 1), :]
        ready("active")
        down_grads(layer)
        if layer == 1:
            fetch_active(0)
        ready("slope")
        for half in range(2):
            for j in range(4):
                i = 4 * half + j
                loaded.pop(("down", i)).wait()
                columns = pl.ds(i * 512, 512)
                value = dot(rounded[...], tiles_down[i % 3], 1, 1)
                slope[:, columns] = (value * slope[:, columns].astype(F32)).astype(BF)
                if i + 3 < 8:
                    tile_down(layer, i + 3)
                elif layer == 1:
                    tile_down(0, i % 3)
            point()
        ready("mid")
        ready("hidden")
        wide_grads(layer, 1, ((0, 4, hidden, slope, 0),))
        fetch_hidden(layer, 0)
        for x in range(4):
            loaded.pop(("up", x)).wait()
            grad_hidden[:, pl.ds(x * 256, 256)] = dot(slope[...], tiles_wide[x % 2], 1, 1)
            if x < 2:
                tile_up(layer, x + 2)
            elif x == 2:
                for n in range(4):
                    tile_out(layer, n)
            else:
                tile_qkv(layer, 0)
            if x % 2 == 1:
                point()
        if layer == 1:
            fetch_slope(0)
        norm_back_into(grad_hidden, state, stream, row(2), sums, 2)
        fetch_stream(layer)
        rounded[...] = state[...].astype(BF)
        point()
        for x in range(4):
            loaded.pop(("out", x)).wait()
            value = dot(rounded[...], tiles_wide[0, :, pl.ds(x * WIDTH, WIDTH)], 1, 1)
            grad_mixed[:, pl.ds(x * 256, 256)] = value.astype(BF)
        tile_qkv(layer, 1)
        ready("qkv")
        ready("probs")
        point()
        for n in range(4):
            attention_backward(qkv, probs, grad_mixed, 2 * n, 2 * n + 2)
            point()
        ready("stream")
        ready("mixed")
        ready("hidden")
        wide_grads(layer, 0, ((0, 3, hidden, qkv, 0), (3 * WIDTH, 1, mixed, rounded, 0)))
        table = table_grads(probs, by_offset_of(bucket_rows[...]))
        if layer == 1:
            fetch_hidden(0, 1)
            fetch_probs(0)
            fetch_mixed(0)
        point()
        for x in range(4):
            loaded.pop(("qkv", x)).wait()
            grad_hidden[:, pl.ds(x * 256, 256)] = dot(qkv[...], tiles_wide[1 - x % 2, :, pl.ds(0, 3 * WIDTH)], 1, 1)
            if x < 2:
                tile_qkv(layer, x + 2)
            elif layer == 1:
                tile_up(0, 3 - x)
            if x % 2 == 1:
                point()
        norm_back_into(grad_hidden, state, stream, row(0), sums, 0)
        if layer == 1:
            fetch_qkv(0)
            fetch_mid(0)
        rounded[...] = state[...].astype(BF)
        point()
        shares = share_grads(sums, table).astype(BF)
        chosen = (iota((64, 1024), 1) == iota((64, 1024), 0) * 16 + layer).astype(BF)
        placed = dot(chosen, shares, 0, 0)
        if layer == 1:
            small_total[...] = placed
        else:
            finish = pltpu.make_async_copy(state, o_input, out_sem)
            finish.start()
            total = (small_total[...] + placed).astype(BF)
            mine, other = split_cores(total, core, (4, 2, 4, 2, 16, LANES))
            for i in range(2):
                columns = pl.ds(i * LANES, LANES)
                parts[3][:, :, :, :, columns] = mine
                stage_small[:, :, :, :, columns] = other
            by_name[0, 3].piece(stage_small, lands[2])
        point()
    while points[0] < len(SERVED):
        point()
    finish.wait()


def backward(cotangent, params, bucket_rows, fetched, saved):
    wide, tall = (1024, 4096), (4096, 1024)
    arrays = [fetched[i].reshape(s) for i, s in ((3, wide), (4, wide), (5, tall), (0, wide), (1, wide), (2, tall))]
    vmem = pl.BlockSpec(memory_space=pltpu.VMEM)
    hbm = pl.BlockSpec(memory_space=pl.ANY)
    chains = [c for array in (2, 1, 0) for c in CHAINS[array] if c[0] == array] + [CHAINS[0][3]]
    scratch = [pltpu.VMEM(s, BF) for s in PART_SHAPES]
    scratch += [pltpu.VMEM(PART_SHAPES[i], BF) for i in (2, 1, 3)]
    for chain in chains:
        scratch += [pltpu.VMEM(s, BF) for s in landing_shapes(chain)]
    scratch += [
        pltpu.VMEM((2,) + PART_SHAPES[2][1:], BF),
        pltpu.VMEM((2,) + PART_SHAPES[1][1:], BF),
        pltpu.VMEM(PART_SHAPES[3], BF),
        pltpu.VMEM((3, 512, WIDTH), BF),
        pltpu.VMEM((2, 256, HIDDEN), BF),
        pltpu.VMEM((HIDDEN, ROWS), BF),
        pltpu.VMEM((ROWS, HIDDEN), BF),
        pltpu.VMEM((HEADS, ROWS, ROWS), BF),
        pltpu.VMEM((ROWS, 3 * WIDTH), BF),
        pltpu.VMEM((WIDTH, ROWS), BF),
        pltpu.VMEM((ROWS, WIDTH), BF),
        pltpu.VMEM((ROWS, WIDTH), F32),
        pltpu.VMEM((ROWS, WIDTH), F32),
        pltpu.VMEM((WIDTH, ROWS), BF),
        pltpu.VMEM((ROWS, WIDTH), F32),
        pltpu.VMEM((ROWS, WIDTH), BF),
        pltpu.VMEM((8, WIDTH), F32),
        pltpu.VMEM((1024, LANES), F32),
        pltpu.SemaphoreType.DMA((20, N_SCATTER)),
        pltpu.SemaphoreType.DMA((20, N_SCATTER)),
        pltpu.SemaphoreType.DMA((28,)),
        pltpu.SemaphoreType.DMA((28,)),
        pltpu.SemaphoreType.REGULAR((3,)),
        pltpu.SemaphoreType.REGULAR,
        pltpu.SemaphoreType.DMA((8,)),
        pltpu.SemaphoreType.DMA((10,)),
        pltpu.SemaphoreType.DMA,
    ]
    return pl.pallas_call(
        backward_kernel,
        out_shape=[
            jax.ShapeDtypeStruct((ROWS, WIDTH), F32),
            jax.ShapeDtypeStruct((2, 16, 4096), F32),
            jax.ShapeDtypeStruct((2, 16, 4096), F32),
            jax.ShapeDtypeStruct((2, 64, 1024), F32),
            jax.ShapeDtypeStruct((16, 256), F32),
        ],
        in_specs=[vmem] * 3 + [hbm] * 15,
        out_specs=[hbm] + [vmem] * 4,
        scratch_shapes=scratch,
        compiler_params=pltpu.CompilerParams(
            collective_id=1, has_side_effects=True, vmem_limit_bytes=63 << 20
        ),
        name="backward_scatter",
    )(cotangent, params, bucket_rows, *arrays, *saved)


def on_device(
    tokens,
    seg_ids,
    buckets,
    cotangent,
    ln1_gain,
    ln1_bias,
    w_query,
    w_key,
    w_value,
    w_out,
    rel_table,
    ln2_gain,
    ln2_bias,
    w_up,
    w_down,
):
    small = jnp.concatenate([ln1_gain, ln1_bias, ln2_gain, ln2_bias, rel_table], 1)
    small = jnp.pad(small, ((0, 14), (0, 56)))
    bucket_rows = (buckets[None, :] == (jnp.arange(64, dtype=jnp.int32) // 2)[:, None]).astype(BF)
    done = forward(
        jnp.concatenate([w_query, w_key, w_value, w_out], 2),
        w_up,
        w_down,
        jnp.concatenate([small, small], 1),
        tokens,
        seg_ids,
        bucket_rows,
    )
    acts, mid0, mid1, stream, params = done[7:12]
    saved = (stream, mid0, mid1) + tuple(done[12:])
    grad_input, att, up, down, small = backward(cotangent, params, bucket_rows, done[:6], saved)
    return (
        acts,
        grad_input,
        small[:2, 0:16],
        small[:2, 16:32],
        att[:, :, :1024],
        att[:, :, 1024:2048],
        att[:, :, 2048:3072],
        att[:, :, 3072:],
        small[:2, 64:72],
        small[:2, 32:48],
        small[:2, 48:64],
        up,
        down,
    )


def solution(mesh):
    placed = (
        P(("wide", "narrow"), None),
        P(("wide", "narrow")),
        P(),
        P(("wide", "narrow"), None),
        P(None, "wide"),
        P(None, "wide"),
        P(None, "wide", None),
        P(None, "wide", None),
        P(None, "wide", None),
        P(None, "wide", None),
        P(None, "wide"),
        P(None, "wide"),
        P(None, "wide"),
        P(None, "wide", None),
        P(None, "wide", None),
    )
    return jax.shard_map(
        on_device,
        mesh=mesh,
        in_specs=placed,
        out_specs=(
            P(None, ("wide", "narrow"), None),
            P(("wide", "narrow"), None),
            P(None, "wide"),
            P(None, "wide"),
            P(None, "wide", None),
            P(None, "wide", None),
            P(None, "wide", None),
            P(None, "wide", None),
            P(None, "wide"),
            P(None, "wide"),
            P(None, "wide"),
            P(None, "wide", None),
            P(None, "wide", None),
        ),
        check_vma=False,
    )
```
